32 devices in a mesh: fsdp: 32 (over z, y, x, core).
Axes of the slice: x: 2, y: 2, z: 4, core: 2. Of those that a mesh axis runs over, the one named last changes fastest.
Arguments:
- tokens: bfloat16 [32768, 512], P('fsdp')
- out_grad: bfloat16 [32768, 512], P('fsdp'), may hold values from -6 to 6
- key_valid: int32 [32768], replicated, may hold values from 0 to 1, as said below
- expert_ids: int32 [32768, 2], P('fsdp'), may hold values from 0 to 3, all different within a row; in each aligned block of 1024 rows (0 to 1023, 1024 to 2047, ...) at most 640 rows name the same one
- gate_logits: float32 [32768, 2], P('fsdp'), may hold values from -4 to 4
- attn_norm_gain: bfloat16 [512], P('fsdp'), may hold values from 0.5 to 1.5
- attn_norm_bias: bfloat16 [512], P('fsdp'), may hold values from -1.5 to 1.5
- qkv_weight: bfloat16 [512, 1536], P('fsdp'), may hold values from -0.25 to 0.25
- query_bias: bfloat16 [512], P('fsdp'), may hold values from -1.5 to 1.5
- value_bias: bfloat16 [512], P('fsdp'), may hold values from -1.5 to 1.5
- attn_out_weight: bfloat16 [512, 512], P('fsdp'), may hold values from -2 to 2
- attn_out_bias: bfloat16 [512], P('fsdp'), may hold values from -1.5 to 1.5
- moe_norm_gain: bfloat16 [512], P('fsdp'), may hold values from 0.5 to 1.5
- moe_norm_bias: bfloat16 [512], P('fsdp'), may hold values from -1.5 to 1.5
- expert_in: bfloat16 [2048, 2048], P('fsdp'), may hold values from -0.25 to 0.25
- expert_in_bias: bfloat16 [8192], P('fsdp'), may hold values from -1.5 to 1.5
- expert_out: bfloat16 [8192, 512], P('fsdp'), may hold values from -0.25 to 0.25
- expert_out_bias: bfloat16 [2048], P('fsdp'), may hold values from -1.5 to 1.5
Outputs:
- block_out: bfloat16 [32768, 512], P('fsdp')
- tokens_grad: float32 [32768, 512], P('fsdp')
- logits_grad: float32 [32768, 2], P('fsdp')
- attn_norm_gain_grad: float32 [512], P('fsdp')
- attn_norm_bias_grad: float32 [512], P('fsdp')
- qkv_weight_grad: float32 [512, 1536], P('fsdp')
- query_bias_grad: float32 [512], P('fsdp')
- value_bias_grad: float32 [512], P('fsdp')
- attn_out_weight_grad: float32 [512, 512], P('fsdp')
- attn_out_bias_grad: float32 [512], P('fsdp')
- moe_norm_gain_grad: float32 [512], P('fsdp')
- moe_norm_bias_grad: float32 [512], P('fsdp')
- expert_in_grad: float32 [2048, 2048], P('fsdp')
- expert_in_bias_grad: float32 [8192], P('fsdp')
- expert_out_grad: float32 [8192, 512], P('fsdp')
- expert_out_bias_grad: float32 [2048], P('fsdp')
- block_stats: float32 [3], replicated
The draws below stay inside these ranges and needn't reach their ends.
Inputs may be any that keep to these rules, and one draw needn't show every extreme that they name: `expert_ids`: each row names 2 different experts. Within the rows of one device (aligned blocks of 1024 rows) no expert is named more than 640 times, and in some block one expert is named exactly 640 times. key_valid[r] is 1 exactly where r < 32600, r % 200 < 197, and image floor(r / 200) is not one of 10 fully masked images; it is 0 elsewhere.
All inputs are finite; a program needn't handle non-finite values.
Results may differ from the reference program's by a relative error of at most 0.013.
Values may be sent and summed in bfloat16 or wider, within the bound.
No kernel may reach another device: no remote copies, remote signals or barrier semaphores. Data moves between devices by JAX's collectives and lax.ppermute only.
A program may use at most 192 MiB of HBM per device.

```python
import math
import jax
import jax.numpy as jnp
import numpy as np
from jax import lax

D = 512
FF = 2048
HEADS = 8
HEAD_DIM = 64
EXPERTS = 4
TOP = 2
IMG_TOK = 200
PAD = 3
ROWS_DEV = 1024
ROWS = 32768
IMAGES = 163
MASKED = 10
CAP = 640


def draw_tokens(key, part):
    key = jax.random.fold_in(key, 5)
    position = jnp.arange(ROWS, dtype=jnp.float32) / (ROWS - 1)
    rising = 0.6 + 1.2 * position
    base = jnp.clip(jax.random.normal(key, (ROWS, D), jnp.float32), -6.0, 6.0)
    return (base * rising[:, None]).astype(jnp.bfloat16)


def draw_key_valid(key, part):
    key = jax.random.fold_in(key, 7)
    order = jax.random.permutation(key, IMAGES)
    kept_image = order >= MASKED
    row_index = jnp.arange(ROWS, dtype=jnp.int32)
    image_index = row_index // IMG_TOK
    inside = row_index % IMG_TOK < IMG_TOK - PAD
    complete = image_index < IMAGES
    kept_row = kept_image[jnp.minimum(image_index, IMAGES - 1)]
    return (inside & complete & kept_row).astype(jnp.int32)


def level_of(rng, shape, cuts, least, largest):
    gain = 1.0
    for axis_at, shards_of in cuts:
        steps = jax.random.uniform(jax.random.fold_in(jax.random.fold_in(rng, 6), axis_at), (shards_of,), jnp.float32, least / len(cuts), largest / len(cuts))
        gain = gain * jnp.repeat(jnp.exp(steps), shape[axis_at] // shards_of).reshape((-1,) + (1,) * (len(shape) - 1 - axis_at))
    return gain


def shared_out(rng, own, number, rows, count, top, limit, skew):
    ranking = jax.random.permutation(rng, count)
    crowded, ordinary = portions_of(count, rows * top, limit, skew, True), portions_of(count, rows * top, limit, skew, False)
    places = jnp.arange(count)

    def named(lengths, offset_by):
        used = int((lengths > 0).sum())
        fixed = max(1, used // 4)
        passed = fixed + (places - fixed + offset_by * (used - fixed)) % max(1, count - fixed)
        return jnp.zeros((count,), jnp.int32).at[ranking[jnp.where(places < fixed, places, passed)]].set(jnp.asarray(lengths, jnp.int32))

    lengths = jnp.where(number % 4 == 0, named(crowded, number // 4), named(ordinary, number - number // 4 - 1))
    mixed = jax.random.permutation(jax.random.fold_in(own, 3), count)
    giver, sink = mixed[0:count // 2 * 2:2], mixed[1:count // 2 * 2:2]
    room = jnp.minimum(lengths[giver] - 1, limit - lengths[sink]) // 2
    room = jnp.where((giver == ranking[0]) | (sink == ranking[0]) | (lengths[sink] == 0), 0, jnp.maximum(room, 0))
    passed = jax.random.randint(jax.random.fold_in(own, 4), (count // 2,), 0, 1 << 20) % (room + 1)
    lengths = lengths.at[giver].add(-passed).at[sink].add(passed)
    labels = jnp.searchsorted(jnp.cumsum(lengths), jnp.arange(rows * top), side="right").astype(jnp.int32)
    grid = labels.reshape(top, rows).T
    grid = grid[jax.random.permutation(jax.random.fold_in(own, 1), rows)]
    offset_by = jax.random.randint(jax.random.fold_in(own, 2), (rows, 1), 0, top)
    return jnp.take_along_axis(grid, (jnp.arange(top)[None, :] + offset_by) % top, axis=1)


def portions_of(number_of, total, reach, skew, full):
    portions = [(1 << 20) // math.isqrt(grade ** skew) + 1 for grade in range(1, number_of + 1)]
    largest = reach if full else min(reach, max(-(-total // number_of), total * portions[0] // sum(portions)))
    least = 1 if total - largest >= number_of - 1 else 0
    holding, surplus = [largest] + [least] * (number_of - 1), total - largest - least * (number_of - 1)
    while surplus > 0:
        movable = [i for i in range(1, number_of) if holding[i] < largest] or [i for i in range(1, number_of) if holding[i] < reach]
        pool, left = sum([portions[i] for i in movable]), surplus
        for i in movable:
            addition = min(reach - holding[i], max(1, left * portions[i] // pool), surplus)
            holding[i] = holding[i] + addition
            surplus = surplus - addition
    return np.array(holding)


def scatter_about(stream_key, shape, deviation, reach, cuts=(), kind=jnp.bfloat16):
    loudness = level_of(stream_key, shape, cuts, -0.22, 0.18) if cuts else 1.0
    drawn = jax.random.normal(stream_key, shape, jnp.float32) * deviation * loudness
    return jnp.minimum(jnp.maximum(drawn, -reach), reach).astype(kind)


def setup_inputs(seed: int = 0) -> dict:
    streams_of = jax.random.split(jax.random.key(seed), 19)
    tokens = draw_tokens(jax.random.fold_in(streams_of[18], 71), 0)
    out_grad = scatter_about(streams_of[1], (ROWS, D), 1.0, 6.0, ((0, 32),))
    key_valid = draw_key_valid(jax.random.fold_in(streams_of[18], 71), 0)
    expert_ids_keys = jax.random.split(jax.random.fold_in(streams_of[3], 1), ROWS // ROWS_DEV)
    expert_ids_turns = jax.random.permutation(jax.random.fold_in(streams_of[3], 3), ROWS // ROWS_DEV)
    expert_ids = jax.vmap(lambda own, number: shared_out(jax.random.fold_in(streams_of[3], 2), own, number, ROWS_DEV, EXPERTS, TOP, CAP, 0))(expert_ids_keys, expert_ids_turns).reshape((ROWS, TOP))
    gate_logits = scatter_about(streams_of[4], (ROWS, TOP), 0.75, 4.0, ((0, 32),), jnp.float32)
    attn_norm_gain = jnp.clip(1.0 + 0.1 * jax.random.normal(streams_of[5], (D,), jnp.float32), 0.5, 1.5).astype(jnp.bfloat16)
    attn_norm_bias = scatter_about(streams_of[6], (D,), 0.1, 1.5, ((0, 32),))
    qkv_weight = scatter_about(streams_of[7], (D, 3 * D), D ** -0.5, 0.25, ((0, 32),))
    query_bias = scatter_about(streams_of[8], (D,), 0.1, 1.5, ((0, 32),))
    value_bias = scatter_about(streams_of[9], (D,), 0.1, 1.5, ((0, 32),))
    attn_out_weight = scatter_about(streams_of[10], (D, D), (D // 64) ** -0.5, 2.0, ((0, 32),))
    attn_out_bias = scatter_about(streams_of[11], (D,), 0.1, 1.5, ((0, 32),))
    moe_norm_gain = jnp.clip(1.0 + 0.1 * jax.random.normal(streams_of[12], (D,), jnp.float32), 0.5, 1.5).astype(jnp.bfloat16)
    moe_norm_bias = scatter_about(streams_of[13], (D,), 0.1, 1.5, ((0, 32),))
    expert_in = scatter_about(streams_of[14], (EXPERTS * D, FF), D ** -0.5, 0.25, ((0, 32),))
    expert_in_bias = scatter_about(streams_of[15], (EXPERTS * FF,), 0.1, 1.5, ((0, 32),))
    expert_out = scatter_about(streams_of[16], (EXPERTS * FF, D), (FF // 4) ** -0.5, 0.25, ((0, 32),))
    expert_out_bias = scatter_about(streams_of[17], (EXPERTS * D,), 0.1, 1.5, ((0, 32),))
    return dict(tokens=tokens, out_grad=out_grad, key_valid=key_valid, expert_ids=expert_ids, gate_logits=gate_logits, attn_norm_gain=attn_norm_gain, attn_norm_bias=attn_norm_bias, qkv_weight=qkv_weight, query_bias=query_bias, value_bias=value_bias, attn_out_weight=attn_out_weight, attn_out_bias=attn_out_bias, moe_norm_gain=moe_norm_gain, moe_norm_bias=moe_norm_bias, expert_in=expert_in, expert_in_bias=expert_in_bias, expert_out=expert_out, expert_out_bias=expert_out_bias)


@jax.custom_vjp
def low(v):
    return lax.optimization_barrier(v.astype(jnp.bfloat16)).astype(jnp.float32)

@jax.custom_vjp
def low_back(v):
    return v

def low_keep(v):
    return (low(v), None)

def low_pass(kept, grad):
    return (grad,)

def back_keep(v):
    return (v, None)

def back_low(kept, grad):
    return (low(grad),)
low.defvjp(low_keep, low_pass)
low_back.defvjp(back_keep, back_low)
EPS = 1e-06
MASKED_SCORE = -1000000000.0
FAR_SCORE = -1e+30
HIGHEST = lax.Precision.HIGHEST

def gelu(values):
    return 0.5 * values * (1.0 + jnp.tanh(0.7978845608028654 * (values + 0.044715 * values * values * values)))

def layer_norm(values, gain_vec, shift_vec):
    average = lax.optimization_barrier(jnp.mean(values, axis=-1, keepdims=True))
    centered = values - average
    inverse = lax.rsqrt(lax.optimization_barrier(jnp.mean(centered * centered, axis=-1, keepdims=True)) + EPS)
    return centered * inverse * gain_vec + shift_vec

def softmax_last(scores):
    highest = lax.optimization_barrier(jnp.max(scores, axis=-1, keepdims=True))
    raised = jnp.exp(scores - highest)
    return raised / lax.optimization_barrier(jnp.sum(raised, axis=-1, keepdims=True))

def image_group(pieces):
    queries, keyed, valued, usable, present = pieces
    scores = jnp.einsum('gqhd,gkhd->ghqk', queries, keyed, precision=HIGHEST) * HEAD_DIM ** (-0.5)
    scores = low_back(scores)
    scores = jnp.where(usable[:, None, None, :], scores, MASKED_SCORE)
    scores = jnp.where(present[:, None, None, :], scores, FAR_SCORE)
    softmaxed = low(softmax_last(scores))
    return jnp.einsum('ghqk,gkhd->gqhd', softmaxed, valued, precision=HIGHEST)

def attention(projected, key_valid):
    per_group = 16
    image_count = -(-ROWS // IMG_TOK)
    group_count = -(-image_count // per_group)
    padded_rows = group_count * per_group * IMG_TOK
    padded = jnp.pad(projected, ((0, padded_rows - ROWS), (0, 0)))
    shaped = padded.reshape(group_count, per_group, IMG_TOK, 3, HEADS, HEAD_DIM)
    usable = jnp.pad(key_valid == 1, (0, padded_rows - ROWS)).reshape(group_count, per_group, IMG_TOK)
    present = (jnp.arange(padded_rows) < ROWS).reshape(group_count, per_group, IMG_TOK)
    mixed = lax.map(jax.checkpoint(image_group), (shaped[:, :, :, 0], shaped[:, :, :, 1], shaped[:, :, :, 2], usable, present))
    return mixed.reshape(padded_rows, HEADS * HEAD_DIM)[:ROWS]

def expert_mix(normed, gate_share, routes, expert_in, expert_in_bias, expert_out, expert_out_bias):
    block_rows = math.gcd(ROWS, 4096)

    def one_block(pieces):
        rows_in, gate_rows, route_rows = pieces
        totals = jnp.zeros((block_rows, D), jnp.float32)
        for expert_index in range(EXPERTS):
            pre_act = jnp.dot(rows_in, expert_in[expert_index * D:(expert_index + 1) * D], precision=HIGHEST) + expert_in_bias[expert_index * FF:(expert_index + 1) * FF]
            hidden = low(gelu(low_back(pre_act)))
            result = low_back(jnp.dot(hidden, expert_out[expert_index * FF:(expert_index + 1) * FF], precision=HIGHEST) + expert_out_bias[expert_index * D:(expert_index + 1) * D])
            share = lax.optimization_barrier(jnp.sum(jnp.where(route_rows == expert_index, gate_rows, 0.0), axis=1))
            totals = totals + share[:, None] * result
        return totals
    block_count = ROWS // block_rows
    mixed = lax.map(jax.checkpoint(one_block), (normed.reshape(block_count, block_rows, D), gate_share.reshape(block_count, block_rows, TOP), routes.reshape(block_count, block_rows, TOP)))
    return mixed.reshape(ROWS, D)

def forward(layer_in, logits, params, key_valid, routes):
    attn_norm_gain, attn_norm_bias, qkv_weight, query_bias, value_bias, attn_out_weight, attn_out_bias, moe_norm_gain, moe_norm_bias, expert_in, expert_in_bias, expert_out, expert_out_bias = params
    first_low = low(layer_norm(layer_in, attn_norm_gain, attn_norm_bias))
    bias_all = jnp.concatenate([query_bias, jnp.zeros_like(query_bias), value_bias])
    projected = low_back(low(jnp.dot(first_low, qkv_weight, precision=HIGHEST) + bias_all))
    mixed = low_back(low(attention(projected, key_valid)))
    attn_branch = low_back(jnp.dot(mixed, attn_out_weight, precision=HIGHEST) + attn_out_bias)
    middle = layer_in + attn_branch
    second_low = low(layer_norm(middle, moe_norm_gain, moe_norm_bias))
    gate_share = softmax_last(logits)
    moe_branch = expert_mix(second_low, gate_share, routes, expert_in, expert_in_bias, expert_out, expert_out_bias)
    return (middle + moe_branch, (attn_branch, moe_branch))

def reference(tokens, out_grad, key_valid, expert_ids, gate_logits, attn_norm_gain, attn_norm_bias, qkv_weight, query_bias, value_bias, attn_out_weight, attn_out_bias, moe_norm_gain, moe_norm_bias, expert_in, expert_in_bias, expert_out, expert_out_bias):
    params = tuple((item.astype(jnp.float32) for item in (attn_norm_gain, attn_norm_bias, qkv_weight, query_bias, value_bias, attn_out_weight, attn_out_bias, moe_norm_gain, moe_norm_bias, expert_in, expert_in_bias, expert_out, expert_out_bias)))

    def run(layer_in, logits, *weights):
        return forward(layer_in, logits, weights, key_valid, expert_ids)
    block_value, pull, branches = jax.vjp(run, tokens.astype(jnp.float32), gate_logits.astype(jnp.float32), *params, has_aux=True)
    grads = pull(out_grad.astype(jnp.float32))
    attn_branch, moe_branch = branches
    valid_rows = (key_valid == 1).astype(jnp.float32)
    count = jnp.sum(valid_rows)
    stats = jnp.stack([jnp.sqrt(jnp.sum(valid_rows[:, None] * block_value * block_value) / (count * D)), jnp.sqrt(jnp.sum(valid_rows[:, None] * attn_branch * attn_branch) / (count * D)), jnp.sqrt(jnp.sum(valid_rows[:, None] * moe_branch * moe_branch) / (count * D))])
    return (block_value.astype(jnp.bfloat16), grads[0], grads[1], grads[2], grads[3], grads[4], grads[5], grads[6], grads[7], grads[8], grads[9], grads[10], grads[11], grads[12], grads[13], grads[14], stats)
```

```python
import functools

import jax
import jax.numpy as jnp
from jax import lax
from jax.experimental import pallas as pl
from jax.experimental.pallas import tpu as pltpu
from jax.sharding import PartitionSpec as P

D = 512
FF = 2048
HEAD_DIM = 64
EXPERTS = 4
TOP = 2
IMG = 200
CAP = 640
HALO = 200
SLOT = 208
NIMG = 7
CHUNK = 512
SMALL = 128
HALF = 1024 + SMALL

EPS = 1e-06
MASKED_SCORE = -1000000000.0
FAR_SCORE = -1e30
F32 = jnp.float32
BF16 = jnp.bfloat16
VMEM_LIMIT = 60 * 1024 * 1024


def dot_nn(a, b):
    return lax.dot_general(a, b, (((1,), (0,)), ((), ())), preferred_element_type=F32)


def dot_nt(a, b):
    return lax.dot_general(a, b, (((1,), (1,)), ((), ())), preferred_element_type=F32)


def dot_tn(a, b):
    return lax.dot_general(a, b, (((0,), (0,)), ((), ())), preferred_element_type=F32)


def norm_parts(values):
    average = jnp.mean(values, axis=-1, keepdims=True)
    centered = values - average
    inverse = lax.rsqrt(jnp.mean(centered * centered, axis=-1, keepdims=True) + EPS)
    return centered * inverse, inverse


def norm_back(upstream, normed, inverse, gain):
    scaled = upstream * gain
    inner = (
        scaled
        - jnp.mean(scaled, axis=-1, keepdims=True)
        - normed * jnp.mean(scaled * normed, axis=-1, keepdims=True)
    )
    return inverse * inner


def route_kernel(ids_ref, idst_ref, logits_ref, poscol_ref, posrow_ref, gate_ref):
    rows = ids_ref.shape[0]
    lane = lax.broadcasted_iota(jnp.int32, (rows, 128), 1)
    chosen = (ids_ref[:, 0:1] == lane) | (ids_ref[:, 1:2] == lane)
    r0 = lax.broadcasted_iota(jnp.int32, (rows, rows), 0)
    r1 = lax.broadcasted_iota(jnp.int32, (rows, rows), 1)
    lower = jnp.where(r1 < r0, 1.0, 0.0).astype(BF16)
    upper = jnp.where(r0 < r1, 1.0, 0.0).astype(BF16)
    count = dot_nn(lower, jnp.where(chosen, 1.0, 0.0).astype(BF16))
    pos = jnp.where(chosen, count, -1.0)
    poscol_ref[...] = pos[:, :8].astype(jnp.int32)
    sub = lax.broadcasted_iota(jnp.int32, (16, rows), 0)
    chosen_t = (idst_ref[0:1, :] == sub) | (idst_ref[1:2, :] == sub)
    count_t = dot_nn(jnp.where(chosen_t, 1.0, 0.0).astype(BF16), upper)
    posrow_ref[...] = jnp.where(chosen_t, count_t, -1.0)[:8].astype(jnp.int32)
    a = logits_ref[:, 0:1]
    b = logits_ref[:, 1:2]
    top = jnp.maximum(a, b)
    ea = jnp.exp(a - top)
    eb = jnp.exp(b - top)
    total = ea + eb
    which = lax.broadcasted_iota(jnp.int32, (rows, 2), 1)
    gate_ref[...] = jnp.where(which == 0, ea / total, eb / total)


def image_fill(fill_ref, st):
    fill = fill_ref[pl.ds(st, SLOT), :]
    row = lax.broadcasted_iota(jnp.int32, (SLOT, 1), 0)
    return jnp.where(row < IMG, fill, FAR_SCORE)


def lane_halves():
    lane = lax.broadcasted_iota(jnp.int32, (1, 128), 1)
    low = jnp.where(lane < HEAD_DIM, 1.0, 0.0).astype(BF16)
    return low, (1.0 - low.astype(F32)).astype(BF16)


def softmax_t(keys, queries, fill):
    scores = jnp.where(fill > 0, dot_nt(keys, queries), fill)
    raised = jnp.exp(scores - jnp.max(scores, axis=0, keepdims=True))
    return raised * (1.0 / jnp.sum(raised, axis=0, keepdims=True))


def attn_fwd_kernel(
    sc, x_ref, fill_ref, wqk, wvo, vecs, qkv_ref, o_ref, y1_ref, a2_ref, stat_ref, xs, os_
):
    rows = o_ref.shape[0]
    xs[...] = x_ref[...].astype(F32)
    masks = lane_halves()

    def image(j, carry):
        st = pl.multiple_of(sc[0] + IMG * j, 8)
        normed, _ = norm_parts(xs[pl.ds(st, SLOT), :])
        a1 = (normed * vecs[0:1, :] + vecs[1:2, :]).astype(BF16)
        qk = dot_nn(a1, wqk[:, : 2 * D])
        q = (qk[:, :D] + vecs[2:3, :]).astype(BF16)
        k = qk[:, D:].astype(BF16)
        v = (dot_nn(a1, wvo[:, :D]) + vecs[3:4, :]).astype(BF16)
        qkv_ref[j, :, 0:D] = q
        qkv_ref[j, :, D : 2 * D] = k
        qkv_ref[j, :, 2 * D : 3 * D] = v
        fill = image_fill(fill_ref, st)
        q8 = q * jnp.asarray(HEAD_DIM**-0.5, BF16)
        for hp in range(4):
            cols = slice(hp * 128, hp * 128 + 128)
            mixed = None
            for mask in masks:
                probs = softmax_t(k[:, cols] * mask, q8[:, cols], fill).astype(BF16)
                part = dot_tn(probs, v[:, cols] * mask)
                mixed = part if mixed is None else mixed + part
            os_[pl.ds(st, SLOT), cols] = mixed
        return carry

    lax.fori_loop(0, sc[1], image, 0)
    total = jnp.zeros((1, D), F32)
    for i in range(rows // 256):
        own = slice(HALO + 256 * i, HALO + 256 * (i + 1))
        here = slice(256 * i, 256 * (i + 1))
        o_low = os_[own, :].astype(BF16)
        o_ref[here, :] = o_low
        attn = dot_nn(o_low, wvo[:, D : 2 * D]) + vecs[4:5, :]
        valid = jnp.where(fill_ref[own, :] > 0, 1.0, 0.0)
        total = total + jnp.sum(valid * attn * attn, axis=0, keepdims=True)
        y1 = xs[own, :] + attn
        y1_ref[here, :] = y1
        normed, _ = norm_parts(y1)
        a2_ref[here, :] = (normed * vecs[5:6, :] + vecs[6:7, :]).astype(BF16)
    stat_ref[...] = jnp.broadcast_to(total, (8, D))


def gelu_both(x):
    square = x * x
    t = jnp.tanh(0.7978845608028654 * (x + 0.044715 * (x * square)))
    half = 0.5 * (1.0 + t)
    slope = half + 0.5 * x * (1.0 - t * t) * (
        0.7978845608028654 * (1.0 + (3.0 * 0.044715) * square)
    )
    return x * half, slope


def moe_kernel(
    blocks,
    tab,
    a2_ref,
    g_ref,
    poscol,
    posrow,
    ids_ref,
    gate_ref,
    bin_ref,
    bout_ref,
    win_ref,
    wout_ref,
    moe_ref,
    da2_ref,
    dgate_ref,
    dbin_ref,
    dbout_ref,
    in_send,
    in_keep,
    out_send,
    out_keep,
    xg,
    xt_keep,
    xt_send,
    gg,
    gt,
    yacc,
    dacc,
):
    e = pl.program_id(0)
    cc = pl.program_id(1)
    core = tab[0]
    rows = a2_ref.shape[0]
    size = D // blocks

    @pl.when((e == 0) & (cc == 0))
    def _():
        moe_ref[...] = jnp.zeros_like(moe_ref)
        da2_ref[...] = jnp.zeros_like(da2_ref)
        dgate_ref[...] = jnp.zeros_like(dgate_ref)

    def gate_of_expert():
        return jnp.sum(jnp.where(ids_ref[...] == e, gate_ref[...], 0.0), axis=1, keepdims=True)

    @pl.when(cc == 0)
    def _():
        slot = lax.broadcasted_iota(jnp.int32, (CAP, rows), 0)
        pick = jnp.where(posrow[pl.ds(e, 1), :] == slot, 1.0, 0.0).astype(BF16)
        x = dot_nn(pick, a2_ref[...]).astype(BF16)
        xg[...] = x
        xt = x.T
        for j in range(blocks):
            here = slice(j * size, (j + 1) * size)
            for b in range(blocks):
                there = slice(b * size, (b + 1) * size)

                @pl.when(tab[1 + j] == b)
                def _():
                    xt_keep[here, :] = xt[there, :]

                @pl.when(tab[1 + blocks + j] == b)
                def _():
                    xt_send[here, :] = xt[there, :]

        gy = (gate_of_expert() * g_ref[...].astype(F32)).astype(BF16)
        g = dot_nn(pick, gy)
        dbout_ref[pl.ds(e, 1), :] = jnp.sum(g, axis=0, keepdims=True)
        g = g.astype(BF16)
        gg[...] = g
        gt[...] = g.T

    chunk = jnp.where(cc < 2, 2 * (1 - core) + cc, 2 * core + cc - 2)
    row = e * 4 + chunk
    x = xg[...]
    win = win_ref[...]
    wout = wout_ref[...]
    pre = dot_nn(x, win) + bin_ref[pl.ds(row, 1), :]
    hidden, slope = gelu_both(pre)
    hidden = hidden.astype(BF16)
    dpre = dot_nt(gg[...], wout) * slope
    dpre = dpre.astype(BF16)
    dbin_ref[pl.ds(row, 1), :] = jnp.sum(dpre.astype(F32), axis=0, keepdims=True)
    y = dot_nn(hidden, wout)
    da = dot_nt(dpre, win)

    @pl.when(cc == 0)
    def _():
        yacc[...] = y + bout_ref[pl.ds(e, 1), :]
        dacc[...] = da

    @pl.when(cc > 0)
    def _():
        yacc[...] += y
        dacc[...] += da

    @pl.when(cc < 2)
    def _():
        in_send[0] = dot_nn(xt_send[...], dpre).astype(BF16)

    @pl.when(cc >= 2)
    def _():
        in_keep[0] = dot_nn(xt_keep[...], dpre).astype(BF16)

    mine = pl.multiple_of(core * 256, 256)
    theirs = pl.multiple_of((1 - core) * 256, 256)
    out_send[0, 0] = dot_nn(gt[pl.ds(theirs, 256), :], hidden).astype(BF16)
    out_keep[0, 0] = dot_nn(gt[pl.ds(mine, 256), :], hidden).astype(BF16)

    @pl.when(cc == 3)
    def _():
        lane = lax.broadcasted_iota(jnp.int32, (rows, 8), 1)
        pos = jnp.sum(jnp.where(lane == e, poscol[...], 0), axis=1, keepdims=True)
        slot = lax.broadcasted_iota(jnp.int32, (rows, CAP), 1)
        place = jnp.where(pos == slot, 1.0, 0.0).astype(BF16)
        yrow = dot_nn(place, yacc[...].astype(BF16))
        da2_ref[...] += dot_nn(place, dacc[...].astype(BF16))
        moe_ref[...] += gate_of_expert() * yrow
        pull = jnp.sum(g_ref[...].astype(F32) * yrow, axis=1, keepdims=True)
        dgate_ref[...] += jnp.where(ids_ref[...] == e, pull, 0.0)


def middle_kernel(
    y1_ref,
    moe_ref,
    da2_ref,
    g_ref,
    dgate_ref,
    gate_ref,
    o_ref,
    fill_ref,
    vecs,
    out_ref,
    dy1_ref,
    gattn_ref,
    dwo_ref,
    lgrad_ref,
    sums_ref,
):
    rows = y1_ref.shape[0]
    sums = [jnp.zeros((1, D), F32) for _ in range(5)]
    for i in range(rows // 256):
        here = slice(256 * i, 256 * (i + 1))
        y1 = y1_ref[here, :]
        moe = moe_ref[here, :]
        value = y1 + moe
        out_ref[here, :] = value.astype(BF16)
        valid = jnp.where(fill_ref[here, :] > 0, 1.0, 0.0)
        normed, inverse = norm_parts(y1)
        upstream = da2_ref[here, :]
        dy1 = g_ref[here, :].astype(F32) + norm_back(upstream, normed, inverse, vecs[5:6, :])
        dy1_ref[here, :] = dy1
        low = dy1.astype(BF16)
        gattn_ref[here, :] = low
        parts = (
            upstream * normed,
            upstream,
            low.astype(F32),
            valid * value * value,
            valid * moe * moe,
        )
        sums = [s + jnp.sum(p, axis=0, keepdims=True) for s, p in zip(sums, parts)]
    for i, s in enumerate(sums):
        sums_ref[i : i + 1, :] = s
    dwo_ref[...] = dot_tn(o_ref[...], gattn_ref[...]).astype(BF16)
    gate = gate_ref[...]
    dgate = dgate_ref[...]
    lgrad_ref[...] = gate * (dgate - jnp.sum(gate * dgate, axis=1, keepdims=True))


def attn_bwd_kernel(
    sc,
    x_ref,
    fill_ref,
    qkv_ref,
    gattn_ref,
    dy1_ref,
    wqk,
    wvo,
    vecs,
    dtok_ref,
    dqk_ref,
    dv_ref,
    sums_ref,
    gs,
    acc,
    a1s,
    gq_s,
):
    rows = dy1_ref.shape[0]
    gs[...] = gattn_ref[...].astype(F32)
    masks = lane_halves()
    scale = jnp.asarray(HEAD_DIM**-0.5, BF16)
    wo = wvo[:, D : 2 * D]

    def image(j, carry):
        st = pl.multiple_of(sc[0] + IMG * j, 8)
        row = lax.broadcasted_iota(jnp.int32, (SLOT, 1), 0)
        upstream = jnp.where(row < IMG, gs[pl.ds(st, SLOT), :], 0.0).astype(BF16)
        go = dot_nt(upstream, wo).astype(BF16)
        q8 = qkv_ref[j, :, 0:D] * scale
        k = qkv_ref[j, :, D : 2 * D]
        v = qkv_ref[j, :, 2 * D : 3 * D]
        fill = image_fill(fill_ref, st)
        for hp in range(4):
            cols = slice(hp * 128, hp * 128 + 128)
            gq = gk = gv = None
            for mask in masks:
                km = k[:, cols] * mask
                probs = softmax_t(km, q8[:, cols], fill)
                pull = dot_nt(v[:, cols] * mask, go[:, cols])
                centre = jnp.sum(probs * pull, axis=0, keepdims=True)
                ds = jnp.where(fill > 0, probs * (pull - centre), 0.0).astype(BF16)
                dq = dot_tn(ds, km)
                dk = dot_nn(ds, q8[:, cols] * mask)
                dv = dot_nn(probs.astype(BF16), go[:, cols] * mask)
                gq = dq if gq is None else gq + dq
                gk = dk if gk is None else gk + dk
                gv = dv if gv is None else gv + dv
            acc[pl.ds(st, SLOT), hp * 128 : hp * 128 + 128] = gq * HEAD_DIM**-0.5
            acc[pl.ds(st, SLOT), D + hp * 128 : D + hp * 128 + 128] = gk
            acc[pl.ds(st, SLOT), 2 * D + hp * 128 : 2 * D + hp * 128 + 128] = gv
        return carry

    lax.fori_loop(0, sc[1], image, 0)
    sums = [jnp.zeros((1, D), F32) for _ in range(4)]
    for i in range(rows // 256):
        own = slice(HALO + 256 * i, HALO + 256 * (i + 1))
        here = slice(256 * i, 256 * (i + 1))
        low = acc[own, :].astype(BF16)
        gq_s[here, :] = low
        normed, inverse = norm_parts(x_ref[here, :].astype(F32))
        a1s[here, :] = (normed * vecs[0:1, :] + vecs[1:2, :]).astype(BF16)
        upstream = dot_nt(low[:, : 2 * D], wqk[:, : 2 * D]) + dot_nt(low[:, 2 * D :], wvo[:, :D])
        dtok_ref[here, :] = dy1_ref[here, :] + norm_back(upstream, normed, inverse, vecs[0:1, :])
        parts = (
            upstream * normed,
            upstream,
            low[:, :D].astype(F32),
            low[:, 2 * D :].astype(F32),
        )
        sums = [s + jnp.sum(p, axis=0, keepdims=True) for s, p in zip(sums, parts)]
    for i, s in enumerate(sums):
        sums_ref[i : i + 1, :] = s
    a1 = a1s[...]
    dqk_ref[...] = dot_tn(a1, gq_s[:, : 2 * D]).astype(BF16)
    dv_ref[...] = dot_tn(a1, gq_s[:, 2 * D :]).astype(BF16)


class Places:
    def __init__(self, n):
        self.n = n
        self.planes = EXPERTS
        self.group = n // EXPERTS
        self.chips = self.group // 2
        self.bits = self.chips.bit_length() - 1
        self.me = lax.axis_index("fsdp")
        self.core = self.me % 2
        self.chip = (self.me // 2) % self.chips
        self.plane = self.me // self.group

    def swap(self):
        return [(i, i ^ 1) for i in range(self.n)]

    def cross(self, step):
        moves = []
        for i in range(self.n):
            bit = step if i % 2 == 0 else self.bits - 1 - step
            moves.append((i, i ^ (2 << bit)))
        return moves

    def turn(self, k):
        return [(i, (i + k * self.group) % self.n) for i in range(self.n)]

    def order(self, core):
        plain = list(range(self.chips))
        back = [int(format(j, "0%db" % self.bits)[::-1], 2) for j in plain]
        rel = jnp.where(core == 0, jnp.array(plain, jnp.int32), jnp.array(back, jnp.int32))
        return jnp.bitwise_xor(self.chip, rel)

    def place(self, core):
        back = [int(format(j, "0%db" % self.bits)[::-1], 2) for j in range(self.chips)]
        rel = jnp.bitwise_xor(self.chip, jnp.arange(self.chips, dtype=jnp.int32))
        return jnp.where(core == 0, rel, jnp.array(back, jnp.int32)[rel])


def send(x, moves):
    return lax.ppermute(x, "fsdp", moves)


def gather_small(shard, pos):
    width = shard.shape[1]
    mine = lax.dynamic_index_in_dim(shard, pos.core, 0, keepdims=False)
    other = lax.dynamic_index_in_dim(shard, 1 - pos.core, 0, keepdims=False)
    got = send(other, pos.swap())
    block = jnp.where(pos.core == 0, jnp.stack([mine, got]), jnp.stack([got, mine]))
    pieces = [block] + [send(block, pos.turn(k)) for k in range(1, 4)]
    have = jnp.stack(pieces)[None]
    for step in range(pos.bits):
        have = jnp.concatenate([have, send(have, pos.cross(step))], axis=0)
    other = send(have, pos.swap())
    planes = (pos.plane - jnp.arange(4, dtype=jnp.int32)) % 4
    halves = []
    for data, core in ((have, pos.core), (other, 1 - pos.core)):
        where = (pos.place(core)[None, :] * 4 + planes[:, None]).reshape(-1)
        flat = data.reshape(4 * pos.chips, 2 * width, HALF)
        halves.append(jnp.take(flat, where, axis=0).reshape(-1, HALF))
    first = jnp.where(pos.core == 0, halves[0], halves[1])
    second = jnp.where(pos.core == 0, halves[1], halves[0])
    return first, second


def add_low(a, b):
    return (a.astype(F32) + b.astype(F32)).astype(BF16)


def reduce_blocks(keep, give, pos):
    have = add_low(keep, send(give, pos.swap()))
    tail = have.shape[2:]
    for step in reversed(range(pos.bits)):
        have = have.reshape((4, 2, -1) + tail)
        got = send(have[:, 1], pos.cross(step))
        have = add_low(have[:, 0], got)
    have = have.reshape((4,) + tail)

    def block(k):
        return lax.dynamic_index_in_dim(have, (pos.plane + k) % 4, 0, keepdims=False)

    total = block(0).astype(F32)
    for k in range(1, 4):
        total = total + send(block(k), pos.turn(k)).astype(F32)
    return total


def local(
    tokens,
    out_grad,
    key_valid,
    expert_ids,
    gate_logits,
    attn_norm_gain,
    attn_norm_bias,
    qkv_weight,
    query_bias,
    value_bias,
    attn_out_weight,
    attn_out_bias,
    moe_norm_gain,
    moe_norm_bias,
    expert_in,
    expert_in_bias,
    expert_out,
    expert_out_bias,
):
    n = lax.axis_size("fsdp")
    pos = Places(n)
    rows = tokens.shape[0]
    ext = rows + 2 * HALO
    width = qkv_weight.shape[0]
    total_rows = rows * n
    vmem = pl.BlockSpec(memory_space=pltpu.VMEM)
    smem = pl.BlockSpec(memory_space=pltpu.SMEM)
    params = pltpu.CompilerParams(vmem_limit_bytes=VMEM_LIMIT)

    def sds(shape, kind):
        return jax.ShapeDtypeStruct(shape, kind)

    def cost(flops, moved, trans=0):
        return pl.CostEstimate(flops=int(flops), bytes_accessed=int(moved), transcendentals=trans)

    up = [(i, i + 1) for i in range(n - 1)]
    down = [(i + 1, i) for i in range(n - 1)]

    def with_halo(x):
        before = send(x[rows - HALO :], up)
        after = send(x[:HALO], down)
        return jnp.concatenate([before, x, after], axis=0)

    vectors = (
        attn_norm_gain,
        attn_norm_bias,
        query_bias,
        value_bias,
        attn_out_bias,
        moe_norm_gain,
        moe_norm_bias,
    )
    small = jnp.concatenate(
        [v.reshape(width, 1) for v in vectors]
        + [
            expert_in_bias.reshape(width, 16),
            expert_out_bias.reshape(width, 4),
            jnp.zeros((width, SMALL - 27), BF16),
        ],
        axis=1,
    )
    shard = jnp.stack(
        [
            jnp.concatenate([qkv_weight[:, : 2 * D], small], axis=1),
            jnp.concatenate(
                [qkv_weight[:, 2 * D :], attn_out_weight, jnp.zeros((width, SMALL), BF16)], axis=1
            ),
        ]
    )
    wqk, wvo = gather_small(shard, pos)
    win_all = lax.all_gather(expert_in, "fsdp", axis=0, tiled=True)
    wout_all = lax.all_gather(expert_out, "fsdp", axis=0, tiled=True)

    small_all = wqk[:, 2 * D :].astype(F32)
    vecs = jnp.concatenate([small_all[:, :7].T, jnp.zeros((1, D), F32)], axis=0)
    bin_all = small_all[:, 7:23].reshape(16, CHUNK)
    bout_all = small_all[:, 23:27].reshape(EXPERTS, D)

    x_ext = with_halo(tokens)
    first_row = pos.me * rows
    offset = first_row % IMG
    scalars = jnp.stack([HALO - offset, (rows + offset + IMG - 1) // IMG]).astype(jnp.int32)
    key_rows = first_row - HALO + jnp.arange(ext, dtype=jnp.int32)
    usable = lax.dynamic_slice_in_dim(jnp.pad(key_valid, (HALO, HALO)), first_row, ext)
    present = (key_rows >= 0) & (key_rows < total_rows)
    fill = jnp.where(usable == 1, 1.0, jnp.where(present, MASKED_SCORE, FAR_SCORE))
    fill = fill.astype(F32).reshape(ext, 1)

    poscol, posrow, gate = pl.pallas_call(
        route_kernel,
        name="route",
        out_shape=(
            sds((rows, 8), jnp.int32),
            sds((8, rows), jnp.int32),
            sds((rows, TOP), F32),
        ),
        in_specs=[vmem] * 3,
        out_specs=(vmem,) * 3,
        compiler_params=params,
        cost_estimate=cost(4 * rows * rows * 128, 1 << 20),
    )(expert_ids, expert_ids.T, gate_logits)

    qkv, o_low, y1, a2, attn_sum = pl.pallas_call(
        attn_fwd_kernel,
        name="attn_fwd",
        out_shape=(
            sds((NIMG, SLOT, 3 * D), BF16),
            sds((rows, D), BF16),
            sds((rows, D), F32),
            sds((rows, D), BF16),
            sds((8, D), F32),
        ),
        in_specs=[smem] + [vmem] * 5,
        out_specs=(vmem,) * 5,
        scratch_shapes=[pltpu.VMEM((ext, D), F32), pltpu.VMEM((ext, D), F32)],
        compiler_params=params,
        cost_estimate=cost(30e9, 12e6),
    )(scalars, x_ext, fill, wqk, wvo, vecs)

    blocks = pos.chips
    keep_order = pos.order(pos.core)
    send_order = pos.order(1 - pos.core)
    if blocks == 4:
        keep_place = pos.place(pos.core)
        send_place = pos.place(1 - pos.core)
    else:
        keep_place = send_place = jnp.arange(4, dtype=jnp.int32)
    tab = jnp.concatenate(
        [pos.core.reshape(1), keep_order, send_order, keep_place, send_place]
    ).astype(jnp.int32)
    p0 = 1 + 2 * blocks

    def chunk_of(cc, t):
        return jnp.where(cc < 2, 2 * (1 - t[0]) + cc, 2 * t[0] + cc - 2)

    whole = lambda e, cc, t: (0, 0)
    grid_spec = pltpu.PrefetchScalarGridSpec(
        num_scalar_prefetch=1,
        grid=(EXPERTS, 4),
        in_specs=[
            pl.BlockSpec((rows, D), whole),
            pl.BlockSpec((rows, D), whole),
            pl.BlockSpec((rows, 8), whole),
            pl.BlockSpec((8, rows), whole),
            pl.BlockSpec((rows, TOP), whole),
            pl.BlockSpec((rows, TOP), whole),
            pl.BlockSpec((16, CHUNK), whole),
            pl.BlockSpec((EXPERTS, D), whole),
            pl.BlockSpec((D, CHUNK), lambda e, cc, t: (e, chunk_of(cc, t))),
            pl.BlockSpec((CHUNK, D), lambda e, cc, t: (e * 4 + chunk_of(cc, t), 0)),
        ],
        out_specs=(
            pl.BlockSpec((rows, D), whole),
            pl.BlockSpec((rows, D), whole),
            pl.BlockSpec((rows, TOP), whole),
            pl.BlockSpec((16, CHUNK), whole),
            pl.BlockSpec((EXPERTS, D), whole),
            pl.BlockSpec((1, D, CHUNK), lambda e, cc, t: (e, 0, jnp.minimum(cc, 1))),
            pl.BlockSpec((1, D, CHUNK), lambda e, cc, t: (e, 0, jnp.maximum(cc - 2, 0))),
            pl.BlockSpec(
                (1, 1, 256, CHUNK), lambda e, cc, t: (e, t[p0 + 4 + chunk_of(cc, t)], 0, 0)
            ),
            pl.BlockSpec((1, 1, 256, CHUNK), lambda e, cc, t: (e, t[p0 + chunk_of(cc, t)], 0, 0)),
        ),
        scratch_shapes=[
            pltpu.VMEM((CAP, D), BF16),
            pltpu.VMEM((D, CAP), BF16),
            pltpu.VMEM((D, CAP), BF16),
            pltpu.VMEM((CAP, D), BF16),
            pltpu.VMEM((D, CAP), BF16),
            pltpu.VMEM((CAP, D), F32),
            pltpu.VMEM((CAP, D), F32),
        ],
    )
    moe, da2, dgate, dbin, dbout, in_send, in_keep, out_send, out_keep = pl.pallas_call(
        functools.partial(moe_kernel, blocks),
        name="experts",
        grid_spec=grid_spec,
        out_shape=(
            sds((rows, D), F32),
            sds((rows, D), F32),
            sds((rows, TOP), F32),
            sds((16, CHUNK), F32),
            sds((EXPERTS, D), F32),
            sds((EXPERTS, D, 2 * CHUNK), BF16),
            sds((EXPERTS, D, 2 * CHUNK), BF16),
            sds((EXPERTS, 4, 256, CHUNK), BF16),
            sds((EXPERTS, 4, 256, CHUNK), BF16),
        ),
        compiler_params=params,
        cost_estimate=cost(45e9, 40e6),
    )(tab, a2, out_grad, poscol, posrow, expert_ids, gate, bin_all, bout_all, win_all, wout_all)

    block_out, dy1, gattn, dwo, logits_grad, sums2 = pl.pallas_call(
        middle_kernel,
        name="middle",
        out_shape=(
            sds((rows, D), BF16),
            sds((rows, D), F32),
            sds((rows, D), BF16),
            sds((D, D), BF16),
            sds((rows, TOP), F32),
            sds((8, D), F32),
        ),
        in_specs=[vmem] * 9,
        out_specs=(vmem,) * 6,
        compiler_params=params,
        cost_estimate=cost(2 * rows * D * D, 14e6),
    )(y1, moe, da2, out_grad, dgate, gate, o_low, fill[HALO : HALO + rows], vecs)

    gattn_ext = with_halo(gattn)
    tokens_grad, dqk, dv, sums1 = pl.pallas_call(
        attn_bwd_kernel,
        name="attn_bwd",
        out_shape=(
            sds((rows, D), F32),
            sds((D, 2 * D), BF16),
            sds((D, D), BF16),
            sds((8, D), F32),
        ),
        in_specs=[smem] + [vmem] * 8,
        out_specs=(vmem,) * 4,
        scratch_shapes=[
            pltpu.VMEM((ext, D), F32),
            pltpu.VMEM((ext, 3 * D), F32),
            pltpu.VMEM((rows, D), BF16),
            pltpu.VMEM((rows, 3 * D), BF16),
        ],
        compiler_params=params,
        cost_estimate=cost(60e9, 16e6),
    )(scalars, tokens, fill, qkv, gattn_ext, dy1, wqk, wvo, vecs)

    chips = pos.chips
    rin = D // chips
    if chips != 4:

        def split(x, core):
            x = x.reshape(EXPERTS, 4, 256, chips // 4, CHUNK * 4 // chips)
            x = x.transpose(0, 1, 3, 2, 4).reshape(EXPERTS, chips, 256, CHUNK * 4 // chips)
            return jnp.take(x, pos.order(core), axis=1)

        out_keep = split(out_keep, pos.core)
        out_send = split(out_send, 1 - pos.core)
    in_sum = reduce_blocks(
        in_keep.reshape(EXPERTS, chips, rin, 2 * CHUNK),
        in_send.reshape(EXPERTS, chips, rin, 2 * CHUNK),
        pos,
    )
    out_sum = reduce_blocks(out_keep, out_send, pos)

    def own_halves(pair, axis):
        mine = lax.dynamic_index_in_dim(pair, pos.core, 0, keepdims=False)
        got = send(lax.dynamic_index_in_dim(pair, 1 - pos.core, 0, keepdims=False), pos.swap())
        return jnp.where(
            pos.core == 0,
            jnp.concatenate([mine, got], axis=axis),
            jnp.concatenate([got, mine], axis=axis),
        )

    expert_in_grad = own_halves(in_sum.reshape(2, rin // 2, 2 * CHUNK), 1)
    cols = out_sum.shape[-1] // 2
    expert_out_grad = own_halves(out_sum.reshape(256, 2, cols).transpose(1, 0, 2), 0).T

    stats = jnp.stack([jnp.sum(sums2[3]), jnp.sum(attn_sum[0]), jnp.sum(sums2[4])])
    small_grad = jnp.concatenate(
        [
            jnp.stack([sums1[0], sums1[1], sums1[2], sums1[3], sums2[2], sums2[0], sums2[1]]).T,
            dbin.reshape(D, 16),
            dbout.reshape(D, 4),
            jnp.broadcast_to(stats, (D, 3)),
            jnp.zeros((D, SMALL - 30), F32),
        ],
        axis=1,
    ).astype(BF16)
    halves = jnp.stack(
        [
            jnp.concatenate([dqk, small_grad], axis=1),
            jnp.concatenate([dv, dwo, jnp.zeros((D, SMALL), BF16)], axis=1),
        ]
    ).reshape(2, EXPERTS, chips, 2 * width, HALF)

    def relative(half, core):
        picked = lax.dynamic_index_in_dim(halves, half, 0, keepdims=False)
        return jnp.take(picked, pos.order(core), axis=1)

    rest = reduce_blocks(relative(pos.core, pos.core), relative(1 - pos.core, 1 - pos.core), pos)
    rest = own_halves(rest.reshape(2, width, HALF), 1)
    tail = rest[:, 2 * D : HALF]
    count = jnp.sum((key_valid == 1).astype(F32))
    block_stats = jnp.sqrt(tail[0, 27:30] / (count * D))
    return (
        block_out,
        tokens_grad,
        logits_grad,
        tail[:, 0].reshape(-1),
        tail[:, 1].reshape(-1),
        jnp.concatenate([rest[:, : 2 * D], rest[:, HALF : HALF + D]], axis=1),
        tail[:, 2].reshape(-1),
        tail[:, 3].reshape(-1),
        rest[:, HALF + D : HALF + 2 * D],
        tail[:, 4].reshape(-1),
        tail[:, 5].reshape(-1),
        tail[:, 6].reshape(-1),
        expert_in_grad,
        tail[:, 7:23].reshape(-1),
        expert_out_grad,
        tail[:, 23:27].reshape(-1),
        block_stats,
    )


def solution(mesh):
    row = P("fsdp", None)
    vec = P("fsdp")
    return jax.shard_map(
        local,
        mesh=mesh,
        in_specs=(
            row,
            row,
            P(),
            row,
            row,
            vec,
            vec,
            row,
            vec,
            vec,
            row,
            vec,
            vec,
            vec,
            row,
            vec,
            row,
            vec,
        ),
        out_specs=(
            row,
            row,
            row,
            vec,
            vec,
            row,
            vec,
            vec,
            row,
            vec,
            vec,
            vec,
            row,
            vec,
            row,
            vec,
            P(),
        ),
        check_vma=False,
    )
```

```python
import functools

import jax
import jax.numpy as jnp
from jax import lax
from jax.experimental import pallas as pl
from jax.experimental.pallas import tpu as pltpu
from jax.sharding import PartitionSpec as P

D = 512
FF = 2048
HEAD_DIM = 64
EXPERTS = 4
TOP = 2
IMG = 200
CAP = 640
HALO = 200
SLOT = 208
NIMG = 7
CHUNK = 512
SMALL = 128
HALF = 1024 + SMALL

SEQ = (0, 1, 3, 2)

EPS = 1e-06
MASKED_SCORE = -1000000000.0
FAR_SCORE = -1e30
F32 = jnp.float32
BF16 = jnp.bfloat16
VMEM_LIMIT = 28 * 1024 * 1024


def dot_nn(a, b):
    return lax.dot_general(a, b, (((1,), (0,)), ((), ())), preferred_element_type=F32)


def dot_nt(a, b):
    return lax.dot_general(a, b, (((1,), (1,)), ((), ())), preferred_element_type=F32)


def dot_tn(a, b):
    return lax.dot_general(a, b, (((0,), (0,)), ((), ())), preferred_element_type=F32)


def norm_parts(values):
    average = jnp.mean(values, axis=-1, keepdims=True)
    centered = values - average
    inverse = lax.rsqrt(jnp.mean(centered * centered, axis=-1, keepdims=True) + EPS)
    return centered * inverse, inverse


def norm_back(upstream, normed, inverse, gain):
    scaled = upstream * gain
    inner = (
        scaled
        - jnp.mean(scaled, axis=-1, keepdims=True)
        - normed * jnp.mean(scaled * normed, axis=-1, keepdims=True)
    )
    return inverse * inner


def route_kernel(ids_ref, idst_ref, logits_ref, poscol_ref, posrow_ref, gate_ref):
    rows = ids_ref.shape[0]
    lane = lax.broadcasted_iota(jnp.int32, (rows, 128), 1)
    chosen = (ids_ref[:, 0:1] == lane) | (ids_ref[:, 1:2] == lane)
    r0 = lax.broadcasted_iota(jnp.int32, (rows, rows), 0)
    r1 = lax.broadcasted_iota(jnp.int32, (rows, rows), 1)
    lower = jnp.where(r1 < r0, 1.0, 0.0).astype(BF16)
    upper = jnp.where(r0 < r1, 1.0, 0.0).astype(BF16)
    count = dot_nn(lower, jnp.where(chosen, 1.0, 0.0).astype(BF16))
    pos = jnp.where(chosen, count, -1.0)
    poscol_ref[...] = pos[:, :8].astype(jnp.int32)
    sub = lax.broadcasted_iota(jnp.int32, (16, rows), 0)
    chosen_t = (idst_ref[0:1, :] == sub) | (idst_ref[1:2, :] == sub)
    count_t = dot_nn(jnp.where(chosen_t, 1.0, 0.0).astype(BF16), upper)
    posrow_ref[...] = jnp.where(chosen_t, count_t, -1.0)[:8].astype(jnp.int32)
    a = logits_ref[:, 0:1]
    b = logits_ref[:, 1:2]
    top = jnp.maximum(a, b)
    ea = jnp.exp(a - top)
    eb = jnp.exp(b - top)
    total = ea + eb
    which = lax.broadcasted_iota(jnp.int32, (rows, 2), 1)
    gate_ref[...] = jnp.where(which == 0, ea / total, eb / total)


def image_fill(fill_ref, st):
    fill = fill_ref[pl.ds(st, SLOT), :]
    row = lax.broadcasted_iota(jnp.int32, (SLOT, 1), 0)
    return jnp.where(row < IMG, fill, FAR_SCORE)


def lane_halves():
    lane = lax.broadcasted_iota(jnp.int32, (1, 128), 1)
    low = jnp.where(lane < HEAD_DIM, 1.0, 0.0).astype(BF16)
    return low, (1.0 - low.astype(F32)).astype(BF16)


def softmax_t(keys, queries, fill):
    scores = jnp.where(fill > 0, dot_nt(keys, queries), fill)
    raised = jnp.exp(scores - jnp.max(scores, axis=0, keepdims=True))
    return raised * (1.0 / jnp.sum(raised, axis=0, keepdims=True))


def halo_rows(out, before_ref, x_ref, after_ref):
    rows = x_ref.shape[0]
    out[0:HALO, :] = before_ref[...].astype(F32)
    out[HALO : HALO + rows, :] = x_ref[...].astype(F32)
    out[HALO + rows :, :] = after_ref[...].astype(F32)


def attn_fwd_kernel(
    sc,
    before_ref,
    x_ref,
    after_ref,
    fill_ref,
    mine_ref,
    other_ref,
    qkv_ref,
    o_ref,
    y1_ref,
    a2_ref,
    stat_ref,
    wqk,
    wvo,
    vecs,
    xs,
    os_,
):
    rows = o_ref.shape[0]
    size = D // 16
    for core, refs in ((0, (mine_ref, other_ref)), (1, (other_ref, mine_ref))):

        @pl.when(sc[2] == core)
        def _():
            for at in range(16):
                for ref, out, base in ((refs[0], wqk, 3), (refs[1], wvo, 19)):
                    row = pl.multiple_of(sc[base + at] * size, size)
                    out[pl.ds(row, size), :] = ref[at]

    vecs[...] = wqk[:, 2 * D :].astype(F32).T[:32]
    halo_rows(xs, before_ref, x_ref, after_ref)
    masks = lane_halves()

    def image(j, carry):
        st = pl.multiple_of(sc[0] + IMG * j, 8)
        normed, _ = norm_parts(xs[pl.ds(st, SLOT), :])
        a1 = (normed * vecs[0:1, :] + vecs[1:2, :]).astype(BF16)
        qk = dot_nn(a1, wqk[:, : 2 * D])
        q = (qk[:, :D] + vecs[2:3, :]).astype(BF16)
        k = qk[:, D:].astype(BF16)
        v = (dot_nn(a1, wvo[:, :D]) + vecs[3:4, :]).astype(BF16)
        qkv_ref[j, :, 0:D] = q
        qkv_ref[j, :, D : 2 * D] = k
        qkv_ref[j, :, 2 * D : 3 * D] = v
        fill = image_fill(fill_ref, st)
        q8 = q * jnp.asarray(HEAD_DIM**-0.5, BF16)
        for hp in range(4):
            cols = slice(hp * 128, hp * 128 + 128)
            mixed = None
            for mask in masks:
                probs = softmax_t(k[:, cols] * mask, q8[:, cols], fill).astype(BF16)
                part = dot_tn(probs, v[:, cols] * mask)
                mixed = part if mixed is None else mixed + part
            os_[pl.ds(st, SLOT), cols] = mixed
        return carry

    lax.fori_loop(0, sc[1], image, 0)
    total = jnp.zeros((1, D), F32)
    for i in range(rows // 256):
        own = slice(HALO + 256 * i, HALO + 256 * (i + 1))
        here = slice(256 * i, 256 * (i + 1))
        o_low = os_[own, :].astype(BF16)
        o_ref[here, :] = o_low
        attn = dot_nn(o_low, wvo[:, D : 2 * D]) + vecs[4:5, :]
        valid = jnp.where(fill_ref[own, :] > 0, 1.0, 0.0)
        total = total + jnp.sum(valid * attn * attn, axis=0, keepdims=True)
        y1 = xs[own, :] + attn
        y1_ref[here, :] = y1
        normed, _ = norm_parts(y1)
        a2_ref[here, :] = (normed * vecs[5:6, :] + vecs[6:7, :]).astype(BF16)
    stat_ref[...] = jnp.broadcast_to(total, (8, D))


def gelu_both(x):
    square = x * x
    t = jnp.tanh(0.7978845608028654 * (x + 0.044715 * (x * square)))
    half = 0.5 * (1.0 + t)
    slope = half + 0.5 * x * (1.0 - t * t) * (
        0.7978845608028654 * (1.0 + (3.0 * 0.044715) * square)
    )
    return x * half, slope


def gate_of(e, ids_ref, gate_ref):
    return jnp.sum(jnp.where(ids_ref[...] == e, gate_ref[...], 0.0), axis=1, keepdims=True)


def expert_kernel(
    item,
    chips,
    tab,
    a2_ref,
    g_ref,
    posrow,
    ids_ref,
    gate_ref,
    bin_ref,
    bout_ref,
    mine0,
    mine1,
    other0,
    other1,
    y_ref,
    da_ref,
    dbin_ref,
    dbout_ref,
    keep,
    give,
    win,
    wout,
    xg,
    xt,
    gg,
    gt,
    hall,
    dall,
    load_sems,
):
    core = tab[0]
    e = tab[1 + item]
    half_chips = chips // 2
    rows = a2_ref.shape[0]
    span = D // chips
    part = CHUNK * 4 // chips // 4
    orders = 5
    places = orders + 2 * chips

    for half_at, pieces in ((0, (mine0, mine1)), (1, (other0, other1))):
        half = core if half_at == 0 else 1 - core
        for number, piece in enumerate(pieces):

            def fetch(j, carry):
                chip = tab[orders + half_at * chips + number * half_chips + j]
                src = piece.at[j]
                for c in range(2):
                    at = pl.multiple_of(chip * 4 * part + (2 * c + half) * part, part)
                    pltpu.make_async_copy(
                        src.at[pl.ds(c * part, part)], wout.at[pl.ds(at, part)], load_sems.at[0]
                    ).start()
                    pltpu.make_async_copy(
                        src.at[pl.ds(2 * part + c * span, span)],
                        win.at[2 * half + c, pl.ds(pl.multiple_of(chip * span, span), span)],
                        load_sems.at[1],
                    ).start()
                return carry

            lax.fori_loop(0, half_chips, fetch, 0)

    slot = lax.broadcasted_iota(jnp.int32, (CAP, rows), 0)
    pick = jnp.where(posrow[pl.ds(e, 1), :] == slot, 1.0, 0.0).astype(BF16)
    x = dot_nn(pick, a2_ref[...]).astype(BF16)
    xg[...] = x
    xt[...] = x.T
    gy = (gate_of(e, ids_ref, gate_ref) * g_ref[...].astype(F32)).astype(BF16)
    g = dot_nn(pick, gy)
    dbout_ref[...] = jnp.zeros_like(dbout_ref)
    dbout_ref[pl.ds(e, 1), :] = jnp.sum(g, axis=0, keepdims=True)
    g = g.astype(BF16)
    gg[...] = g
    gt[...] = g.T
    dbin_ref[...] = jnp.zeros_like(dbin_ref)
    pltpu.make_async_copy(wout, wout, load_sems.at[0]).wait()
    pltpu.make_async_copy(win, win, load_sems.at[1]).wait()

    for c in range(4):
        row = e * 4 + c
        w1 = win[c]
        w2 = wout[CHUNK * c : CHUNK * (c + 1), :]
        total = jnp.zeros((1, CHUNK), F32)
        for r in range(2):
            here = slice(r * (CAP // 2), (r + 1) * (CAP // 2))
            pre = dot_nn(xg[here, :], w1) + bin_ref[pl.ds(row, 1), :]
            hidden, slope = gelu_both(pre)
            hall[c, here, :] = hidden.astype(BF16)
            dpre = (dot_nt(gg[here, :], w2) * slope).astype(BF16)
            dall[c, here, :] = dpre
            total = total + jnp.sum(dpre.astype(F32), axis=0, keepdims=True)
        dbin_ref[pl.ds(row, 1), :] = total

    mine = pl.multiple_of(core * 256, 256)
    theirs = pl.multiple_of((1 - core) * 256, 256)
    for i in range(2):
        for first, where, at in ((1 - core, give, places + 4), (core, keep, places)):
            dwin = dot_nn(xt[...], dall[2 * first + i]).astype(BF16)
            for b in range(4):
                where[tab[at + b], 256 + 128 * i : 384 + 128 * i, :] = dwin[128 * b : 128 * (b + 1)]
    for c in range(4):
        give[tab[places + 4 + c], 0:256, :] = dot_nn(gt[pl.ds(theirs, 256), :], hall[c]).astype(BF16)
        keep[tab[places + c], 0:256, :] = dot_nn(gt[pl.ds(mine, 256), :], hall[c]).astype(BF16)

    hidden = jnp.concatenate([hall[c] for c in range(4)], axis=1)
    y = dot_nn(hidden, wout[...]) + bout_ref[pl.ds(e, 1), :]
    y_ref[...] = y.astype(BF16)
    da = None
    for c in range(4):
        more = dot_nt(dall[c], win[c])
        da = more if da is None else da + more
    da_ref[...] = da.astype(BF16)


def combine(e, poscol, ids_ref, gate_ref, g_ref, y, da):
    rows = poscol.shape[0]
    lane = lax.broadcasted_iota(jnp.int32, (rows, 8), 1)
    pos = jnp.sum(jnp.where(lane == e, poscol[...], 0), axis=1, keepdims=True)
    slot = lax.broadcasted_iota(jnp.int32, (rows, CAP), 1)
    place = jnp.where(pos == slot, 1.0, 0.0).astype(BF16)
    yrow = dot_nn(place, y)
    pull = jnp.sum(g_ref[...].astype(F32) * yrow, axis=1, keepdims=True)
    dgate = jnp.where(ids_ref[...] == e, pull, 0.0)
    return gate_of(e, ids_ref, gate_ref) * yrow, dot_nn(place, da), dgate


def middle_kernel(
    tab,
    poscol,
    ids_ref,
    gate_ref,
    g_ref,
    s0,
    s1,
    s2,
    s3,
    t0,
    t1,
    t2,
    t3,
    y1_ref,
    o_ref,
    fill_ref,
    vecs,
    attn_sum,
    out_ref,
    dy1_ref,
    gattn_ref,
    dwo_ref,
    lgrad_ref,
    sums_ref,
    stats_ref,
    moe_ref,
    da2_ref,
):
    shared = (poscol, ids_ref, gate_ref, g_ref)
    dgate = 0.0
    for k, (y, da) in enumerate(((s0, t0), (s1, t1), (s2, t2), (s3, t3))):
        moe, da2, pull = combine(tab[1 + k], *shared, y[...], da[...])
        dgate = dgate + pull
        if k == 0:
            moe_ref[...] = moe
            da2_ref[...] = da2
        else:
            moe_ref[...] += moe
            da2_ref[...] += da2
    rows = y1_ref.shape[0]
    sums = [jnp.zeros((1, D), F32) for _ in range(5)]
    for i in range(rows // 256):
        here = slice(256 * i, 256 * (i + 1))
        y1 = y1_ref[here, :]
        moe = moe_ref[here, :]
        value = y1 + moe
        out_ref[here, :] = value.astype(BF16)
        valid = jnp.where(fill_ref[HALO + 256 * i : HALO + 256 * (i + 1), :] > 0, 1.0, 0.0)
        normed, inverse = norm_parts(y1)
        upstream = da2_ref[here, :]
        dy1 = g_ref[here, :].astype(F32) + norm_back(upstream, normed, inverse, vecs[5:6, :])
        dy1_ref[here, :] = dy1
        low = dy1.astype(BF16)
        gattn_ref[here, :] = low
        parts = (
            upstream * normed,
            upstream,
            low.astype(F32),
            valid * value * value,
            valid * moe * moe,
        )
        sums = [s + jnp.sum(p, axis=0, keepdims=True) for s, p in zip(sums, parts)]
    sums_ref[...] = jnp.zeros_like(sums_ref)
    stats_ref[...] = jnp.zeros_like(stats_ref)
    for i, s in ((4, sums[2]), (5, sums[0]), (6, sums[1])):
        sums_ref[i : i + 1, :] = s
    for i, s in enumerate((sums[3], attn_sum[0:1, :], sums[4])):
        stats_ref[i : i + 1, :] = jnp.broadcast_to(jnp.sum(s, axis=1, keepdims=True), (1, D))
    dwo_ref[...] = dot_tn(o_ref[...], gattn_ref[...]).astype(BF16)
    gate = gate_ref[...]
    lgrad_ref[...] = gate * (dgate - jnp.sum(gate * dgate, axis=1, keepdims=True))


def image_back(j, sc, fill_ref, qkv_ref, gs, wo, masks):
    st = pl.multiple_of(sc[0] + IMG * j, 8)
    row = lax.broadcasted_iota(jnp.int32, (SLOT, 1), 0)
    upstream = jnp.where(row < IMG, gs[pl.ds(st, SLOT), :], 0.0).astype(BF16)
    go = dot_nt(upstream, wo).astype(BF16)
    q8 = qkv_ref[j, :, 0:D] * jnp.asarray(HEAD_DIM**-0.5, BF16)
    k = qkv_ref[j, :, D : 2 * D]
    v = qkv_ref[j, :, 2 * D : 3 * D]
    fill = image_fill(fill_ref, st)
    for hp in range(4):
        cols = slice(hp * 128, hp * 128 + 128)
        gq = gk = gv = None
        for mask in masks:
            km = k[:, cols] * mask
            probs = softmax_t(km, q8[:, cols], fill)
            pull = dot_nt(v[:, cols] * mask, go[:, cols])
            centre = jnp.sum(probs * pull, axis=0, keepdims=True)
            ds = jnp.where(fill > 0, probs * (pull - centre), 0.0).astype(BF16)
            dq = dot_tn(ds, km)
            dk = dot_nn(ds, q8[:, cols] * mask)
            dv = dot_nn(probs.astype(BF16), go[:, cols] * mask)
            gq = dq if gq is None else gq + dq
            gk = dk if gk is None else gk + dk
            gv = dv if gv is None else gv + dv
        yield st, hp * 128, gq * HEAD_DIM**-0.5, gk, gv


def attn_bwd_kernel(sc, fill_ref, qkv_ref, gattn_ref, wvo, grad_ref, gs):
    rows = gattn_ref.shape[0]
    gs[HALO : HALO + rows, :] = gattn_ref[...].astype(F32)
    gs[HALO + rows : HALO + rows + 8, :] = jnp.zeros((8, D), F32)
    masks = lane_halves()
    wo = wvo[:, D : 2 * D]

    def image(j, carry):
        for _, at, *grads in image_back(j + 1, sc, fill_ref, qkv_ref, gs, wo, masks):
            for i, grad in enumerate(grads):
                grad_ref[j, :, i * D + at : i * D + at + 128] = grad.astype(BF16)
        return carry

    lax.fori_loop(0, 4, image, 0)


def attn_end_kernel(
    devices,
    places,
    sc,
    tab,
    x_ref,
    fill_ref,
    qkv_ref,
    before_ref,
    gattn_ref,
    after_ref,
    dy1_ref,
    wqk,
    wvo,
    vecs,
    early_ref,
    dwo_ref,
    sums2_ref,
    stats_ref,
    b0,
    b1,
    b2,
    b3,
    c0,
    c1,
    c2,
    c3,
    dtok_ref,
    keep_ref,
    give_ref,
    gs,
    acc,
    a1s,
    gq_s,
    cols,
    bias,
):
    rows = dy1_ref.shape[0]
    halo_rows(gs, before_ref, gattn_ref, after_ref)
    masks = lane_halves()
    wo = wvo[:, D : 2 * D]

    def image(j, carry):
        for st, at, *grads in image_back(j, sc, fill_ref, qkv_ref, gs, wo, masks):
            for i, grad in enumerate(grads):
                acc[pl.ds(st, SLOT), i * D + at : i * D + at + 128] = grad
        return carry

    image(0, 0)
    for j in range(4):
        st = pl.multiple_of(sc[0] + IMG * (j + 1), 8)
        acc[pl.ds(st, SLOT), :] = early_ref[j].astype(F32)
    lax.fori_loop(5, sc[1], image, 0)
    sums = [jnp.zeros((1, D), F32) for _ in range(4)]
    for i in range(rows // 256):
        own = slice(HALO + 256 * i, HALO + 256 * (i + 1))
        here = slice(256 * i, 256 * (i + 1))
        low = acc[own, :].astype(BF16)
        gq_s[here, :] = low
        normed, inverse = norm_parts(x_ref[here, :].astype(F32))
        a1s[here, :] = (normed * vecs[0:1, :] + vecs[1:2, :]).astype(BF16)
        upstream = dot_nt(low[:, : 2 * D], wqk[:, : 2 * D]) + dot_nt(low[:, 2 * D :], wvo[:, :D])
        dtok_ref[here, :] = dy1_ref[here, :] + norm_back(upstream, normed, inverse, vecs[0:1, :])
        parts = (
            upstream * normed,
            upstream,
            low[:, :D].astype(F32),
            low[:, 2 * D :].astype(F32),
        )
        sums = [s + jnp.sum(p, axis=0, keepdims=True) for s, p in zip(sums, parts)]
    cols[...] = jnp.zeros_like(cols)
    for i, s in enumerate(sums):
        cols[i : i + 1, :] = s
    cols[4:8, :] = sums2_ref[4:8, :]
    cols[8:16, :] = stats_ref[...]
    small = cols[...].T.astype(BF16)
    dbin = b0[...] + b1[...] + b2[...] + b3[...]
    dbout = c0[...] + c1[...] + c2[...] + c3[...]
    bias[...] = jnp.zeros_like(bias)
    width = bias.shape[0] // devices
    lines = max(1, EXPERTS * FF // devices // 128)
    for d in range(devices):
        for i in range(lines):
            at = EXPERTS * FF // devices * d // 128 + i
            bias[width * d + i : width * d + i + 1, :] = dbin[
                at // 4 : at // 4 + 1, at % 4 * 128 : at % 4 * 128 + 128
            ]
        at = EXPERTS * D // devices * d // 128
        bias[width * d + lines : width * d + lines + 1, :] = dbout[
            at // 4 : at // 4 + 1, at % 4 * 128 : at % 4 * 128 + 128
        ]
    a1 = a1s[...]
    dqk = dot_tn(a1, gq_s[:, : 2 * D]).astype(BF16)
    dv = dot_tn(a1, gq_s[:, 2 * D :]).astype(BF16)
    first = jnp.concatenate([dqk, small], axis=1)
    second = jnp.concatenate([dv, dwo_ref[...], bias[...].astype(BF16)], axis=1)
    size = D // 16
    for ref, at, half in ((keep_ref, places, tab[0]), (give_ref, places + 4, 1 - tab[0])):
        for value, own in ((first, 0), (second, 1)):

            @pl.when(half == own)
            def _():
                for b in range(16):
                    ref[b // 4, tab[at + b % 4]] = value[b * size : (b + 1) * size]


def fold_kernel(kinds, *refs):
    step = pl.program_id(0)
    count = len(kinds)
    outs = list(refs[2 * count :])
    for at, kind in enumerate(kinds):
        a, b = refs[2 * at], refs[2 * at + 1]
        total = (a[0].astype(F32) + b[0].astype(F32)).astype(BF16)
        if kind == "sum":
            outs.pop(0)[0] = total
            continue
        low, high = outs.pop(0), outs.pop(0)

        @pl.when(step < 2)
        def _():
            low[0] = total

        @pl.when(step >= 2)
        def _():
            high[0] = total


class Places:
    def __init__(self, n):
        self.n = n
        self.planes = EXPERTS
        self.group = n // EXPERTS
        self.chips = self.group // 2
        self.bits = self.chips.bit_length() - 1
        self.me = lax.axis_index("fsdp")
        self.core = self.me % 2
        self.chip = (self.me // 2) % self.chips
        self.plane = self.me // self.group

    def swap(self):
        return [(i, i ^ 1) for i in range(self.n)]

    def cross(self, step):
        moves = []
        for i in range(self.n):
            bit = step if i % 2 == 0 else self.bits - 1 - step
            moves.append((i, i ^ (2 << bit)))
        return moves

    def turn(self, k):
        return [(i, (i + k * self.group) % self.n) for i in range(self.n)]

    def order(self, core):
        plain = list(range(self.chips))
        back = [int(format(j, "0%db" % self.bits)[::-1], 2) for j in plain]
        rel = jnp.where(core == 0, jnp.array(plain, jnp.int32), jnp.array(back, jnp.int32))
        return jnp.bitwise_xor(self.chip, rel)

    def place(self, core):
        back = [int(format(j, "0%db" % self.bits)[::-1], 2) for j in range(self.chips)]
        rel = jnp.bitwise_xor(self.chip, jnp.arange(self.chips, dtype=jnp.int32))
        return jnp.where(core == 0, rel, jnp.array(back, jnp.int32)[rel])


def send(x, moves):
    return lax.ppermute(x, "fsdp", moves)


def sync(*arrays):
    return lax.optimization_barrier(arrays)


def pair_block(expert_in, expert_out, pos):
    rin, rout = expert_in.shape[0], expert_out.shape[0]
    win = expert_in.reshape(rin, 4, CHUNK)
    halves = [
        jnp.concatenate(
            [expert_out[h * rout // 2 : (h + 1) * rout // 2], win[:, 2 * h], win[:, 2 * h + 1]]
        )
        for h in range(2)
    ]
    first = pos.core == 0
    mine = jnp.where(first, halves[0], halves[1])
    got = send(jnp.where(first, halves[1], halves[0]), pos.swap())
    a = jnp.where(first, mine, got)
    b = jnp.where(first, got, mine)
    cut = rout // 2
    return jnp.concatenate(
        [a[:cut], b[:cut], a[cut : cut + rin], b[cut : cut + rin], a[cut + rin :], b[cut + rin :]]
    )


def fold(*items):
    kinds = tuple(kind for kind, _, _ in items)
    args, in_specs, out_specs, out_shape, finals = [], [], [], [], []
    for kind, a, b in items:
        height = a.size // 4 // CHUNK
        args += [a.reshape(4, height, CHUNK), b.reshape(4, height, CHUNK)]
        in_specs += [pl.BlockSpec((1, height, CHUNK), lambda i: (i, 0, 0))] * 2
        if kind == "sum":
            out_specs.append(pl.BlockSpec((1, height, CHUNK), lambda i: (i, 0, 0)))
            shapes = [(4, height, CHUNK)]
            finals.append(a.shape)
        else:
            out_specs.append(
                pl.BlockSpec((1, height, CHUNK), lambda i: (jnp.minimum(i, 1), 0, 0))
            )
            out_specs.append(
                pl.BlockSpec((1, height, CHUNK), lambda i: (jnp.maximum(i - 2, 0), 0, 0))
            )
            shapes = [(2, height, CHUNK)] * 2
            finals += [(a.shape[0] // 2,) + a.shape[1:]] * 2
        out_shape += [jax.ShapeDtypeStruct(shape, BF16) for shape in shapes]
    outs = pl.pallas_call(
        functools.partial(fold_kernel, kinds),
        name="fold",
        grid=(4,),
        in_specs=in_specs,
        out_specs=tuple(out_specs),
        out_shape=tuple(out_shape),
        compiler_params=pltpu.CompilerParams(vmem_limit_bytes=VMEM_LIMIT),
        cost_estimate=pl.CostEstimate(flops=1000, bytes_accessed=1000, transcendentals=0),
    )(*args)
    return [out.reshape(shape) for out, shape in zip(outs, finals)]


def add_low(a, b):
    return (a.astype(F32) + b.astype(F32)).astype(BF16)


def reduce_step(have, step, pos):
    tail = have.shape[2:]
    have = have.reshape((have.shape[0], 2, -1) + tail)
    return add_low(have[:, 0], send(have[:, 1], pos.cross(step)))


def reduce_chips(have, pos):
    for step in reversed(range(pos.bits)):
        have = reduce_step(have, step, pos)
    return have[:, 0]


def reduce_blocks(keep, give, pos):
    have = reduce_chips(add_low(keep, send(give, pos.swap())), pos)

    def block(k):
        return lax.dynamic_index_in_dim(have, (pos.plane + k) % 4, 0, keepdims=False)

    total = block(0).astype(F32)
    for k in range(1, 4):
        total = total + send(block(k), pos.turn(k)).astype(F32)
    return total


def local(
    tokens,
    out_grad,
    key_valid,
    expert_ids,
    gate_logits,
    attn_norm_gain,
    attn_norm_bias,
    qkv_weight,
    query_bias,
    value_bias,
    attn_out_weight,
    attn_out_bias,
    moe_norm_gain,
    moe_norm_bias,
    expert_in,
    expert_in_bias,
    expert_out,
    expert_out_bias,
):
    n = lax.axis_size("fsdp")
    pos = Places(n)
    rows = tokens.shape[0]
    ext = rows + 2 * HALO
    width = qkv_weight.shape[0]
    total_rows = rows * n
    vmem = pl.BlockSpec(memory_space=pltpu.VMEM)
    smem = pl.BlockSpec(memory_space=pltpu.SMEM)
    params = pltpu.CompilerParams(vmem_limit_bytes=VMEM_LIMIT)

    def sds(shape, kind):
        return jax.ShapeDtypeStruct(shape, kind)

    def cost(flops, moved, trans=0):
        return pl.CostEstimate(flops=int(flops / 1000), bytes_accessed=int(moved / 1000), transcendentals=trans)

    up = [(i, i + 1) for i in range(n - 1)]
    down = [(i + 1, i) for i in range(n - 1)]

    def halo(x):
        return send(x[rows - HALO :], up), send(x[:HALO], down)

    flat = jnp.concatenate(
        [
            attn_norm_gain,
            attn_norm_bias,
            query_bias,
            value_bias,
            attn_out_bias,
            moe_norm_gain,
            moe_norm_bias,
            expert_in_bias,
            expert_out_bias,
            jnp.zeros(((SMALL - 27) * width,), BF16),
        ]
    )
    first = pos.core == 0
    half_0 = jnp.concatenate([qkv_weight[:, : 2 * D], flat.reshape(SMALL, width).T], axis=1)
    pad = jnp.zeros((width, SMALL), BF16)
    half_1 = jnp.concatenate([qkv_weight[:, 2 * D :], attn_out_weight, pad], axis=1)
    mine = jnp.where(first, half_0, half_1)
    got = send(jnp.where(first, half_1, half_0), pos.swap())
    block = jnp.where(first, jnp.stack([mine, got]), jnp.stack([got, mine]))
    block = block.reshape(2 * width, HALF)
    pair = pair_block(expert_in, expert_out, pos)

    turned = [send(block, pos.turn(k)) for k in range(1, 4)]
    *turned, pair = sync(*turned, pair)
    have = jnp.stack([block] + turned)[None]
    crossed = send(have, pos.cross(0))
    poscol, posrow, gate = pl.pallas_call(
        route_kernel,
        name="route",
        out_shape=(
            sds((rows, 8), jnp.int32),
            sds((8, rows), jnp.int32),
            sds((rows, TOP), F32),
        ),
        in_specs=[vmem] * 3,
        out_specs=(vmem,) * 3,
        compiler_params=params,
        cost_estimate=cost(4 * rows * rows * 128, 1 << 20),
    )(expert_ids, expert_ids.T, gate_logits)
    crossed, gate, poscol, posrow = sync(crossed, gate, poscol, posrow)
    have = jnp.concatenate([have, crossed], axis=0)
    piece = send(pair, pos.turn(SEQ[1]))
    for step in range(1, pos.bits):
        have = jnp.concatenate([have, send(have, pos.cross(step))], axis=0)
    before, behind = halo(tokens)
    first_row = pos.me * rows
    offset = first_row % IMG
    key_rows = first_row - HALO + jnp.arange(ext, dtype=jnp.int32)
    usable = lax.dynamic_slice_in_dim(jnp.pad(key_valid, (HALO, HALO)), first_row, ext)
    present = (key_rows >= 0) & (key_rows < total_rows)
    fill = jnp.where(usable == 1, 1.0, jnp.where(present, MASKED_SCORE, FAR_SCORE))
    fill = fill.astype(F32).reshape(ext, 1)
    front = pair[None]
    for step in range(pos.bits - 1):
        got = send(front, pos.cross(step))
        if step < pos.bits - 2:
            front = jnp.concatenate([front, got], axis=0)
    have, piece, before, behind, fill, got = sync(have, piece, before, behind, fill, got)
    other = send(have, pos.swap())
    planes = (pos.plane - jnp.arange(4, dtype=jnp.int32)) % 4
    chips = pos.chips
    if chips == 4:
        spots = [
            (planes[None, :] * 4 + pos.order(c)[:, None]).reshape(-1)
            for c in (pos.core, 1 - pos.core)
        ]
        have = have.reshape(16, 2 * width, HALF)
        other = other.reshape(16, 2 * width, HALF)
    else:
        spots = [jnp.arange(16, dtype=jnp.int32)] * 2
        canonical = []
        for data, c in ((have, pos.core), (other, 1 - pos.core)):
            where = (pos.place(c)[None, :] * 4 + planes[:, None]).reshape(-1)
            data = jnp.take(data.reshape(4 * chips, 2 * width, HALF), where, axis=0)
            canonical.append(data.reshape(16, D // 16, HALF))
        have, other = canonical

    scalars = jnp.concatenate(
        [
            jnp.stack([HALO - offset, (rows + offset + IMG - 1) // IMG, pos.core]),
            jnp.where(first, spots[0], spots[1]),
            jnp.where(first, spots[1], spots[0]),
        ]
    ).astype(jnp.int32)
    def near_chips(piece):
        held = piece[None]
        for step in range(pos.bits - 2):
            held = jnp.concatenate([held, send(held, pos.cross(step))], axis=0)
        return held, send(held, pos.cross(pos.bits - 2))

    held = [jnp.concatenate([front, got])]
    half, got = near_chips(piece)
    flight = [
        send(held[0], pos.cross(pos.bits - 1)),
        send(held[0], pos.swap()),
        got,
        send(pair, pos.turn(SEQ[2])),
    ]
    qkv, o_low, y1, a2, attn_sum, wqk, wvo, vecs = pl.pallas_call(
        attn_fwd_kernel,
        name="attn_fwd",
        out_shape=(
            sds((NIMG, SLOT, 3 * D), BF16),
            sds((rows, D), BF16),
            sds((rows, D), F32),
            sds((rows, D), BF16),
            sds((8, D), F32),
            sds((D, HALF), BF16),
            sds((D, HALF), BF16),
            sds((32, D), F32),
        ),
        in_specs=[smem] + [vmem] * 6,
        out_specs=(vmem,) * 8,
        scratch_shapes=[pltpu.VMEM((ext, D), F32), pltpu.VMEM((ext, D), F32)],
        compiler_params=params,
        cost_estimate=cost(30e9, 12e6),
    )(scalars, before, tokens, behind, fill, have, other)
    full, front, got, piece, a2, vecs = sync(*flight, a2, vecs)

    def by_device(x):
        return x.reshape(-1, n, width).transpose(1, 0, 2).reshape(-1, D)

    bin_all = by_device(vecs[7:23])
    bout_all = by_device(vecs[23:27])
    if chips == 4:
        keep_place = pos.place(pos.core)
        give_place = pos.place(1 - pos.core)
    else:
        keep_place = give_place = jnp.arange(4, dtype=jnp.int32)
    experts = (pos.plane - jnp.array(SEQ, jnp.int32)) % 4
    tab = jnp.concatenate(
        [
            pos.core.reshape(1),
            experts,
            pos.order(pos.core),
            pos.order(1 - pos.core),
            keep_place,
            give_place,
        ]
    ).astype(jnp.int32)
    rin, rout = expert_in.shape[0], expert_out.shape[0]

    def by_chip(x, core):
        if chips == 4:
            return x
        more = chips // 4
        out = x[:, :256].reshape(4, 256, more, 2 * rout).transpose(0, 2, 1, 3)
        win = x[:, 256:].reshape(4, 2, more, 2 * rin, CHUNK).transpose(0, 2, 1, 3, 4)
        both = [out.reshape(chips, rout, CHUNK), win.reshape(chips, 4 * rin, CHUNK)]
        return jnp.take(jnp.concatenate(both, axis=1), pos.order(core), axis=0)

    hbm = pl.BlockSpec(memory_space=pl.ANY)

    def run_expert(k, full, front):
        back = send(full, pos.swap())
        return pl.pallas_call(
            functools.partial(expert_kernel, k, chips),
            name="expert_%d" % k,
            out_shape=(
                sds((CAP, D), BF16),
                sds((CAP, D), BF16),
                sds((16, CHUNK), F32),
                sds((EXPERTS, D), F32),
                sds((4, CHUNK, CHUNK), BF16),
                sds((4, CHUNK, CHUNK), BF16),
            ),
            in_specs=[smem] + [vmem] * 7 + [hbm] * 4,
            out_specs=(vmem,) * 6,
            scratch_shapes=[
                pltpu.VMEM((4, D, CHUNK), BF16),
                pltpu.VMEM((FF, D), BF16),
                pltpu.VMEM((CAP, D), BF16),
                pltpu.VMEM((D, CAP), BF16),
                pltpu.VMEM((CAP, D), BF16),
                pltpu.VMEM((D, CAP), BF16),
                pltpu.VMEM((4, CAP, CHUNK), BF16),
                pltpu.VMEM((4, CAP, CHUNK), BF16),
                pltpu.SemaphoreType.DMA((2,)),
            ],
            compiler_params=params,
            cost_estimate=cost(10e9, 14e6),
        )(
            tab,
            a2,
            out_grad,
            posrow,
            expert_ids,
            gate,
            bin_all,
            bout_all,
            held[k],
            full,
            front,
            back,
        )

    def first_sum(k, got):
        return ("halves", by_chip(results[k][4], pos.core), got)

    def give_of(k):
        return send(by_chip(results[k][5], 1 - pos.core), pos.swap())

    top = pos.bits - 1

    def send_top(x):
        return send(x, pos.cross(top))

    def send_low(keep, x):
        for step in reversed(range(1, top)):
            total = add_low(keep, send(x, pos.cross(step)))
            keep, x = total[: total.shape[0] // 2], total[total.shape[0] // 2 :]
        return keep, send(x, pos.cross(0))

    results = []
    held.append(jnp.concatenate([half, got]))
    half, got = near_chips(piece)
    flight = [
        send(held[1], pos.cross(top)),
        send(held[1], pos.swap()),
        got,
        send(pair, pos.turn(SEQ[3])),
    ]
    done = sync(*run_expert(0, full, front), *flight, a2)
    results.append(done[:6])
    full, front, got, piece, a2 = done[6:]

    held.append(jnp.concatenate([half, got]))
    half, got = near_chips(piece)
    flight = [send(held[2], pos.cross(top)), send(held[2], pos.swap()), got, give_of(0)]
    done = sync(*run_expert(1, full, front), *flight, a2)
    results.append(done[:6])
    full, front, got, swap_0, a2 = done[6:]

    held.append(jnp.concatenate([half, got]))
    keep_0, give_0 = fold(first_sum(0, swap_0))
    flight = [send(held[3], pos.cross(top)), send(held[3], pos.swap()), send_top(give_0), give_of(1)]
    done = sync(*run_expert(2, full, front), *flight, a2)
    results.append(done[:6])
    full, front, top_0, swap_1, a2 = done[6:]

    keep_0, give_0, keep_1, give_1 = fold(("halves", keep_0, top_0), first_sum(1, swap_1))
    keep_0, got = send_low(keep_0, give_0)
    flight = [got, send_top(give_1), give_of(2)]
    done = sync(*run_expert(3, full, front), *flight, a2)
    results.append(done[:6])
    low_0, top_1, swap_2, a2 = done[6:]

    sum_0, keep_1, give_1, keep_2, give_2 = fold(
        ("sum", keep_0, low_0), ("halves", keep_1, top_1), first_sum(2, swap_2)
    )
    keep_1, got = send_low(keep_1, give_1)
    flight = [got, send_top(give_2), give_of(3)]
    routing = (tab, poscol, expert_ids, gate, out_grad)
    middle = pl.pallas_call(
        middle_kernel,
        name="middle",
        out_shape=(
            sds((rows, D), BF16),
            sds((rows, D), F32),
            sds((rows, D), BF16),
            sds((D, D), BF16),
            sds((rows, TOP), F32),
            sds((8, D), F32),
            sds((8, D), F32),
        ),
        in_specs=[smem] + [vmem] * 17,
        out_specs=(vmem,) * 7,
        scratch_shapes=[pltpu.VMEM((rows, D), F32), pltpu.VMEM((rows, D), F32)],
        compiler_params=params,
        cost_estimate=cost(9 * 2 * rows * CAP * D, 16e6),
    )(
        *routing,
        *(r[0] for r in results),
        *(r[1] for r in results),
        y1,
        o_low,
        fill,
        vecs,
        attn_sum,
    )
    done = sync(*middle, *flight)
    block_out, dy1, gattn, dwo, logits_grad, sums2, stats, low_1, top_2, swap_3 = done

    sum_1, keep_2, give_2, keep_3, give_3 = fold(
        ("sum", keep_1, low_1), ("halves", keep_2, top_2), first_sum(3, swap_3)
    )
    keep_2, got = send_low(keep_2, give_2)

    def home(k, x):
        return send(x[0], pos.turn(4 - SEQ[k]))

    flight = [got, send_top(give_3), home(1, sum_1), *halo(gattn)]
    early = pl.pallas_call(
        attn_bwd_kernel,
        name="attn_bwd_early",
        out_shape=sds((4, SLOT, 3 * D), BF16),
        in_specs=[smem] + [vmem] * 4,
        out_specs=vmem,
        scratch_shapes=[pltpu.VMEM((ext, D), F32)],
        compiler_params=params,
        cost_estimate=cost(30e9, 8e6),
    )(scalars, fill, qkv, gattn, wvo)
    early, low_2, top_3, home_1, before, behind = sync(early, *flight)

    sum_2, keep_3, give_3 = fold(("sum", keep_2, low_2), ("halves", keep_3, top_3))
    keep_3, got = send_low(keep_3, give_3)
    flight = [got, home(2, sum_2)]
    tokens_grad, rest_keep, rest_give = pl.pallas_call(
        functools.partial(attn_end_kernel, n, 5 + 2 * chips),
        name="attn_bwd_late",
        out_shape=(
            sds((rows, D), F32),
            sds((EXPERTS, 4, D // 16, HALF), BF16),
            sds((EXPERTS, 4, D // 16, HALF), BF16),
        ),
        in_specs=[smem] * 2 + [vmem] * 22,
        out_specs=(vmem,) * 3,
        scratch_shapes=[
            pltpu.VMEM((ext, D), F32),
            pltpu.VMEM((ext, 3 * D), F32),
            pltpu.VMEM((rows, D), BF16),
            pltpu.VMEM((rows, 3 * D), BF16),
            pltpu.VMEM((128, D), F32),
            pltpu.VMEM((D, SMALL), F32),
        ],
        compiler_params=params,
        cost_estimate=cost(30e9, 16e6),
    )(
        scalars,
        tab,
        tokens,
        fill,
        qkv,
        before,
        gattn,
        behind,
        dy1,
        wqk,
        wvo,
        vecs,
        early,
        dwo,
        sums2,
        stats,
        *(r[2] for r in results),
        *(r[3] for r in results),
    )

    tokens_grad, rest_keep, rest_give, low_3, home_2 = sync(
        tokens_grad, rest_keep, rest_give, *flight
    )

    def by_block(x, core):
        if chips == 4:
            return x
        return jnp.take(x.reshape(EXPERTS, chips, 2 * width, HALF), pos.order(core), axis=1)

    (sum_3,) = fold(("sum", keep_3, low_3))
    total = sum_0[0].astype(F32)
    rest = reduce_blocks(by_block(rest_keep, pos.core), by_block(rest_give, 1 - pos.core), pos)
    home_3, rest = sync(home(3, sum_3), rest)
    for got in (home_1, home_2, home_3):
        total = total + got.astype(F32)

    def own_halves(pair, axis):
        mine = lax.dynamic_index_in_dim(pair, pos.core, 0, keepdims=False)
        got = send(lax.dynamic_index_in_dim(pair, 1 - pos.core, 0, keepdims=False), pos.swap())
        return jnp.where(
            pos.core == 0,
            jnp.concatenate([mine, got], axis=axis),
            jnp.concatenate([got, mine], axis=axis),
        )

    out_sum = total[:rout].reshape(256, 2, rout).transpose(1, 0, 2)
    expert_out_grad = own_halves(out_sum, 0).T
    in_sum = total[rout:].reshape(2, 2, rin, CHUNK).transpose(1, 2, 0, 3)
    expert_in_grad = own_halves(in_sum.reshape(2, rin, 2 * CHUNK), 1)

    rest = own_halves(rest.reshape(2, width, HALF), 1)
    tail = rest[:, 2 * D : HALF]
    bias = rest[:, HALF + 2 * D :].reshape(-1)
    count = jnp.sum((key_valid == 1).astype(F32))
    block_stats = jnp.sqrt(tail[0, 8:11] / (count * D))
    in_size, out_size = expert_in_bias.shape[0], expert_out_bias.shape[0]
    lines = max(1, in_size // 128)

    def bias_part(line, size):
        return lax.dynamic_slice_in_dim(bias, line * 128 + pos.me * size % 128, size)

    return (
        block_out,
        tokens_grad,
        logits_grad,
        tail[:, 0],
        tail[:, 1],
        jnp.concatenate([rest[:, : 2 * D], rest[:, HALF : HALF + D]], axis=1),
        tail[:, 2],
        tail[:, 3],
        rest[:, HALF + D : HALF + 2 * D],
        tail[:, 4],
        tail[:, 5],
        tail[:, 6],
        expert_in_grad,
        bias_part(0, in_size),
        expert_out_grad,
        bias_part(lines, out_size),
        block_stats,
    )


def solution(mesh):
    row = P("fsdp", None)
    vec = P("fsdp")
    return jax.shard_map(
        local,
        mesh=mesh,
        in_specs=(
            row,
            row,
            P(),
            row,
            row,
            vec,
            vec,
            row,
            vec,
            vec,
            row,
            vec,
            vec,
            vec,
            row,
            vec,
            row,
            vec,
        ),
        out_specs=(
            row,
            row,
            row,
            vec,
            vec,
            row,
            vec,
            vec,
            row,
            vec,
            vec,
            vec,
            row,
            vec,
            row,
            vec,
            P(),
        ),
        check_vma=False,
    )
```

```python
import functools

import jax
import jax.numpy as jnp
from jax import lax
from jax.experimental import pallas as pl
from jax.experimental.pallas import tpu as pltpu
from jax.sharding import PartitionSpec as P

D = 512
FF = 2048
HEAD_DIM = 64
EXPERTS = 4
TOP = 2
IMG = 200
CAP = 640
HALO = 200
SLOT = 208
NIMG = 7
CHUNK = 512
SMALL = 128
HALF = 1024 + SMALL

SEQ = (0, 1, 2, 3)

EPS = 1e-06
MASKED_SCORE = -1000000000.0
FAR_SCORE = -1e30
F32 = jnp.float32
BF16 = jnp.bfloat16
VMEM_MIB = {"attn_fwd": 48, "dispatch": 60, "expert": 22, "middle": 18, "early": 8, "late": 23, "fold": 14}


def room(name):
    return pltpu.CompilerParams(vmem_limit_bytes=VMEM_MIB[name] * 1024 * 1024)


def dot_nn(a, b):
    return lax.dot_general(a, b, (((1,), (0,)), ((), ())), preferred_element_type=F32)


def dot_nt(a, b):
    return lax.dot_general(a, b, (((1,), (1,)), ((), ())), preferred_element_type=F32)


def dot_tn(a, b):
    return lax.dot_general(a, b, (((0,), (0,)), ((), ())), preferred_element_type=F32)


def norm_parts(values):
    average = jnp.mean(values, axis=-1, keepdims=True)
    centered = values - average
    inverse = lax.rsqrt(jnp.mean(centered * centered, axis=-1, keepdims=True) + EPS)
    return centered * inverse, inverse


def norm_back(upstream, normed, inverse, gain):
    scaled = upstream * gain
    inner = (
        scaled
        - jnp.mean(scaled, axis=-1, keepdims=True)
        - normed * jnp.mean(scaled * normed, axis=-1, keepdims=True)
    )
    return inverse * inner


def route_kernel(ids_ref, idst_ref, logits_ref, poscol_ref, posrow_ref, gate_ref):
    rows = ids_ref.shape[0]
    lane = lax.broadcasted_iota(jnp.int32, (rows, 128), 1)
    chosen = (ids_ref[:, 0:1] == lane) | (ids_ref[:, 1:2] == lane)
    r0 = lax.broadcasted_iota(jnp.int32, (rows, rows), 0)
    r1 = lax.broadcasted_iota(jnp.int32, (rows, rows), 1)
    lower = jnp.where(r1 < r0, 1.0, 0.0).astype(BF16)
    upper = jnp.where(r0 < r1, 1.0, 0.0).astype(BF16)
    count = dot_nn(lower, jnp.where(chosen, 1.0, 0.0).astype(BF16))
    pos = jnp.where(chosen, count, -1.0)
    poscol_ref[...] = pos[:, :8].astype(jnp.int32)
    sub = lax.broadcasted_iota(jnp.int32, (16, rows), 0)
    chosen_t = (idst_ref[0:1, :] == sub) | (idst_ref[1:2, :] == sub)
    count_t = dot_nn(jnp.where(chosen_t, 1.0, 0.0).astype(BF16), upper)
    posrow_ref[...] = jnp.where(chosen_t, count_t, -1.0)[:8].astype(jnp.int32)
    a = logits_ref[:, 0:1]
    b = logits_ref[:, 1:2]
    top = jnp.maximum(a, b)
    ea = jnp.exp(a - top)
    eb = jnp.exp(b - top)
    total = ea + eb
    which = lax.broadcasted_iota(jnp.int32, (rows, 2), 1)
    gate_ref[...] = jnp.where(which == 0, ea / total, eb / total)


def image_fill(fill_ref, st):
    fill = fill_ref[pl.ds(st, SLOT), :]
    row = lax.broadcasted_iota(jnp.int32, (SLOT, 1), 0)
    return jnp.where(row < IMG, fill, FAR_SCORE)


def lane_halves():
    lane = lax.broadcasted_iota(jnp.int32, (1, 128), 1)
    low = jnp.where(lane < HEAD_DIM, 1.0, 0.0).astype(BF16)
    return low, (1.0 - low.astype(F32)).astype(BF16)


def softmax_t(keys, queries, fill):
    scores = jnp.where(fill > 0, dot_nt(keys, queries), fill)
    raised = jnp.exp(scores - jnp.max(scores, axis=0, keepdims=True))
    return raised * (1.0 / jnp.sum(raised, axis=0, keepdims=True))


def bias_lines(devices):
    lines = max(1, EXPERTS * FF // devices // 128)
    for d in range(devices):
        for i in range(lines):
            yield d, i, 0, EXPERTS * FF // devices * d // 128 + i
        yield d, lines, 1, EXPERTS * D // devices * d // 128


def halo_rows(out, before_ref, x_ref, after_ref):
    rows = x_ref.shape[0]
    out[0:HALO, :] = before_ref[...].astype(F32)
    out[HALO : HALO + rows, :] = x_ref[...].astype(F32)
    out[HALO + rows :, :] = after_ref[...].astype(F32)


def attn_fwd_kernel(
    devices,
    sc,
    before_ref,
    x_ref,
    after_ref,
    fill_ref,
    mine_0,
    mine_1,
    other_0,
    other_1,
    qkv_hbm,
    o_hbm,
    y1_hbm,
    a2_ref,
    stat_ref,
    wqk_hbm,
    wvo_hbm,
    vecs,
    bin_ref,
    bout_ref,
    qkv_ref,
    o_ref,
    y1_ref,
    wqk,
    wvo,
    xs,
    os_,
    sems,
):
    rows = a2_ref.shape[0]
    size = D // 16
    mine, other = (mine_0, mine_1), (other_0, other_1)
    for core, refs in ((0, (mine, other)), (1, (other, mine))):

        @pl.when(sc[2] == core)
        def _():
            for at in range(16):
                for ref, out, base in ((refs[0], wqk, 3), (refs[1], wvo, 19)):
                    row = pl.multiple_of(sc[base + at] * size, size)
                    out[pl.ds(row, size), :] = ref[at // 8][at % 8]

    weights_out = [
        pltpu.make_async_copy(wqk, wqk_hbm, sems.at[NIMG]),
        pltpu.make_async_copy(wvo, wvo_hbm, sems.at[NIMG + 1]),
    ]
    for copy in weights_out:
        copy.start()
    vecs[...] = wqk[:, 2 * D :].astype(F32).T[:8]
    bias = wvo[:, 2 * D :].astype(F32)
    bin_ref[...] = jnp.zeros_like(bin_ref)
    bout_ref[...] = jnp.zeros_like(bout_ref)
    for d, line, out, at in bias_lines(devices):
        out = (bin_ref, bout_ref)[out]
        row = D // devices * d + line
        here = (slice(at // 4, at // 4 + 1), slice(at % 4 * 128, at % 4 * 128 + 128))
        out[here] += bias[row : row + 1, :]
    halo_rows(xs, before_ref, x_ref, after_ref)
    masks = lane_halves()

    def image(j, carry):
        st = pl.multiple_of(sc[0] + IMG * j, 8)
        normed, _ = norm_parts(xs[pl.ds(st, SLOT), :])
        a1 = (normed * vecs[0:1, :] + vecs[1:2, :]).astype(BF16)
        qk = dot_nn(a1, wqk[:, : 2 * D])
        q = (qk[:, :D] + vecs[2:3, :]).astype(BF16)
        k = qk[:, D:].astype(BF16)
        v = (dot_nn(a1, wvo[:, :D]) + vecs[3:4, :]).astype(BF16)
        qkv_ref[j, :, 0:D] = q
        qkv_ref[j, :, D : 2 * D] = k
        qkv_ref[j, :, 2 * D : 3 * D] = v
        fill = image_fill(fill_ref, st)
        q8 = q * jnp.asarray(HEAD_DIM**-0.5, BF16)
        for hp in range(4):
            cols = slice(hp * 128, hp * 128 + 128)
            mixed = None
            for mask in masks:
                probs = softmax_t(k[:, cols] * mask, q8[:, cols], fill).astype(BF16)
                part = dot_tn(probs, v[:, cols] * mask)
                mixed = part if mixed is None else mixed + part
            os_[pl.ds(st, SLOT), cols] = mixed
        pltpu.make_async_copy(qkv_ref.at[j], qkv_hbm.at[j], sems.at[j]).start()
        return carry

    def image_out(j, carry):
        pltpu.make_async_copy(qkv_ref.at[j], qkv_hbm.at[j], sems.at[j]).wait()
        return carry

    lax.fori_loop(0, sc[1], image, 0)
    rows_out = []
    total = jnp.zeros((1, D), F32)
    for i in range(rows // 256):
        own = slice(HALO + 256 * i, HALO + 256 * (i + 1))
        here = slice(256 * i, 256 * (i + 1))
        o_low = os_[own, :].astype(BF16)
        o_ref[here, :] = o_low
        attn = dot_nn(o_low, wvo[:, D : 2 * D]) + vecs[4:5, :]
        valid = jnp.where(fill_ref[own, :] > 0, 1.0, 0.0)
        total = total + jnp.sum(valid * attn * attn, axis=0, keepdims=True)
        y1 = xs[own, :] + attn
        y1_ref[here, :] = y1
        normed, _ = norm_parts(y1)
        a2_ref[here, :] = (normed * vecs[5:6, :] + vecs[6:7, :]).astype(BF16)
        at = NIMG + 2 + 2 * i
        rows_out.append(pltpu.make_async_copy(o_ref.at[here], o_hbm.at[here], sems.at[at]))
        rows_out.append(pltpu.make_async_copy(y1_ref.at[here], y1_hbm.at[here], sems.at[at + 1]))
        rows_out[-2].start()
        rows_out[-1].start()
    stat_ref[...] = jnp.broadcast_to(total, (8, D))
    lax.fori_loop(0, sc[1], image_out, 0)
    for copy in weights_out + rows_out:
        copy.wait()


def gelu_both(x):
    square = x * x
    t = jnp.tanh(0.7978845608028654 * (x + 0.044715 * (x * square)))
    half = 0.5 * (1.0 + t)
    slope = half + 0.5 * x * (1.0 - t * t) * (
        0.7978845608028654 * (1.0 + (3.0 * 0.044715) * square)
    )
    return x * half, slope


def gate_of(e, ids_ref, gate_ref):
    return jnp.sum(jnp.where(ids_ref[...] == e, gate_ref[...], 0.0), axis=1, keepdims=True)


def dispatch_kernel(first, tab, g_ref, posrow, ids_ref, gate_ref, *outs):
    rows = g_ref.shape[0]
    count = (len(outs) - 2) // 2
    sums_ref = outs[count]
    *held, sems = outs[count + 1 :]
    copies = [pltpu.make_async_copy(held[i], outs[i], sems.at[i]) for i in range(count)]
    g = g_ref[...].astype(F32)
    slot = lax.broadcasted_iota(jnp.int32, (CAP, rows), 0)
    sums_ref[...] = jnp.zeros_like(sums_ref)
    for k in range(count // 2):
        e = tab[1 + first + k]
        pick = jnp.where(posrow[pl.ds(e, 1), :] == slot, 1.0, 0.0).astype(BF16)
        gy = (gate_of(e, ids_ref, gate_ref) * g).astype(BF16)
        gslot = dot_nn(pick, gy)
        sums_ref[pl.ds(e, 1), :] = jnp.sum(gslot, axis=0, keepdims=True)
        gslot = gslot.astype(BF16)
        held[2 * k][...] = gslot
        copies[2 * k].start()
        held[2 * k + 1][...] = gslot.T
        copies[2 * k + 1].start()
    for copy in copies:
        copy.wait()


def expert_kernel(
    item,
    chips,
    tab,
    a2_ref,
    gg,
    gt,
    posrow,
    bin_ref,
    bout_ref,
    mine0,
    mine1,
    other0,
    other1,
    y_ref,
    da_ref,
    dbin_ref,
    keep,
    give,
    win,
    wout,
    xg,
    xt,
    hall,
    dall,
):
    core = tab[0]
    e = tab[1 + item]
    half_chips = chips // 2
    rows = a2_ref.shape[0]
    span = D // chips
    part = CHUNK * 4 // chips // 4
    orders = 5
    places = orders + 2 * chips

    def sort_weights():
        for half_at, pieces in ((0, (mine0, mine1)), (1, (other0, other1))):
            half = core if half_at == 0 else 1 - core
            for number, piece in enumerate(pieces):
                for j in range(half_chips):
                    chip = tab[orders + half_at * chips + number * half_chips + j]
                    for c in range(2):
                        at = pl.multiple_of((chip * 4 + 2 * c + half) * part, part)
                        here = c * 2 * part if span % 32 == 0 else c * part
                        wout[pl.ds(at, part), :] = piece[j, here : here + part, :]
                    for i in range(2):
                        out = win.at[2 * half + i]
                        if span % 32 == 0:
                            for c in range(2):
                                at = pl.multiple_of(chip * span + c * span // 2, span // 2)
                                here = c * 2 * part + part + i * span // 2
                                out[pl.ds(at, span // 2), :] = piece[j, here : here + span // 2, :]
                        else:
                            at = pl.multiple_of(chip * span, span)
                            here = 2 * part + i * span
                            out[pl.ds(at, span), :] = piece[j, here : here + span, :]

    slot = lax.broadcasted_iota(jnp.int32, (CAP, rows), 0)
    pick = jnp.where(posrow[pl.ds(e, 1), :] == slot, 1.0, 0.0).astype(BF16)
    x = dot_nn(pick, a2_ref[...]).astype(BF16)
    xg[...] = x
    xt[...] = x.T
    dbin_ref[...] = jnp.zeros_like(dbin_ref)
    sort_weights()

    for c in range(4):
        row = e * 4 + c
        w1 = win[c]
        w2 = wout[CHUNK * c : CHUNK * (c + 1), :]
        total = jnp.zeros((1, CHUNK), F32)
        for r in range(2):
            here = slice(r * (CAP // 2), (r + 1) * (CAP // 2))
            pre = dot_nn(xg[here, :], w1) + bin_ref[pl.ds(row, 1), :]
            hidden, slope = gelu_both(pre)
            hall[c, here, :] = hidden.astype(BF16)
            dpre = (dot_nt(gg[here, :], w2) * slope).astype(BF16)
            dall[c, here, :] = dpre
            total = total + jnp.sum(dpre.astype(F32), axis=0, keepdims=True)
        dbin_ref[pl.ds(row, 1), :] = total

    mine = pl.multiple_of(core * 256, 256)
    theirs = pl.multiple_of((1 - core) * 256, 256)
    for i in range(2):
        for first, where, at in ((1 - core, give, places + 4), (core, keep, places)):
            dwin = dot_nn(xt[...], dall[2 * first + i]).astype(BF16)
            for b in range(4):
                where[tab[at + b], 256 + 128 * i : 384 + 128 * i, :] = dwin[128 * b : 128 * (b + 1)]
    for c in range(4):
        give[tab[places + 4 + c], 0:256, :] = dot_nn(gt[pl.ds(theirs, 256), :], hall[c]).astype(BF16)
        keep[tab[places + c], 0:256, :] = dot_nn(gt[pl.ds(mine, 256), :], hall[c]).astype(BF16)

    hidden = jnp.concatenate([hall[c] for c in range(4)], axis=1)
    y = dot_nn(hidden, wout[...]) + bout_ref[pl.ds(e, 1), :]
    y_ref[...] = y.astype(BF16)
    da = None
    for c in range(4):
        more = dot_nt(dall[c], win[c])
        da = more if da is None else da + more
    da_ref[...] = da.astype(BF16)


def combine(e, poscol, ids_ref, gate_ref, g_ref, y, da):
    rows = poscol.shape[0]
    lane = lax.broadcasted_iota(jnp.int32, (rows, 8), 1)
    pos = jnp.sum(jnp.where(lane == e, poscol[...], 0), axis=1, keepdims=True)
    slot = lax.broadcasted_iota(jnp.int32, (rows, CAP), 1)
    place = jnp.where(pos == slot, 1.0, 0.0).astype(BF16)
    yrow = dot_nn(place, y)
    pull = jnp.sum(g_ref[...].astype(F32) * yrow, axis=1, keepdims=True)
    dgate = jnp.where(ids_ref[...] == e, pull, 0.0)
    return gate_of(e, ids_ref, gate_ref) * yrow, dot_nn(place, da), dgate


def middle_kernel(
    tab,
    poscol,
    ids_ref,
    gate_ref,
    g_ref,
    s0,
    s1,
    s2,
    s3,
    t0,
    t1,
    t2,
    t3,
    y1_ref,
    o_ref,
    fill_ref,
    vecs,
    attn_sum,
    out_ref,
    dy1_ref,
    gattn_ref,
    dwo_ref,
    lgrad_ref,
    sums_ref,
    stats_ref,
    moe_ref,
    da2_ref,
):
    shared = (poscol, ids_ref, gate_ref, g_ref)
    dgate = 0.0
    for k, (y, da) in enumerate(((s0, t0), (s1, t1), (s2, t2), (s3, t3))):
        moe, da2, pull = combine(tab[1 + k], *shared, y[...], da[...])
        dgate = dgate + pull
        if k == 0:
            moe_ref[...] = moe
            da2_ref[...] = da2
        else:
            moe_ref[...] += moe
            da2_ref[...] += da2
    rows = y1_ref.shape[0]
    sums = [jnp.zeros((1, D), F32) for _ in range(5)]
    for i in range(rows // 256):
        here = slice(256 * i, 256 * (i + 1))
        y1 = y1_ref[here, :]
        moe = moe_ref[here, :]
        value = y1 + moe
        out_ref[here, :] = value.astype(BF16)
        valid = jnp.where(fill_ref[HALO + 256 * i : HALO + 256 * (i + 1), :] > 0, 1.0, 0.0)
        normed, inverse = norm_parts(y1)
        upstream = da2_ref[here, :]
        dy1 = g_ref[here, :].astype(F32) + norm_back(upstream, normed, inverse, vecs[5:6, :])
        dy1_ref[here, :] = dy1
        low = dy1.astype(BF16)
        gattn_ref[here, :] = low
        parts = (
            upstream * normed,
            upstream,
            low.astype(F32),
            valid * value * value,
            valid * moe * moe,
        )
        sums = [s + jnp.sum(p, axis=0, keepdims=True) for s, p in zip(sums, parts)]
    sums_ref[...] = jnp.zeros_like(sums_ref)
    stats_ref[...] = jnp.zeros_like(stats_ref)
    for i, s in ((4, sums[2]), (5, sums[0]), (6, sums[1])):
        sums_ref[i : i + 1, :] = s
    for i, s in enumerate((sums[3], attn_sum[0:1, :], sums[4])):
        stats_ref[i : i + 1, :] = jnp.broadcast_to(jnp.sum(s, axis=1, keepdims=True), (1, D))
    dwo_ref[...] = dot_tn(o_ref[...], gattn_ref[...]).astype(BF16)
    gate = gate_ref[...]
    lgrad_ref[...] = gate * (dgate - jnp.sum(gate * dgate, axis=1, keepdims=True))


def image_back(j, sc, fill_ref, qkv_ref, gs, wo, masks):
    st = pl.multiple_of(sc[0] + IMG * j, 8)
    row = lax.broadcasted_iota(jnp.int32, (SLOT, 1), 0)
    upstream = jnp.where(row < IMG, gs[pl.ds(st, SLOT), :], 0.0).astype(BF16)
    go = dot_nt(upstream, wo).astype(BF16)
    q8 = qkv_ref[j, :, 0:D] * jnp.asarray(HEAD_DIM**-0.5, BF16)
    k = qkv_ref[j, :, D : 2 * D]
    v = qkv_ref[j, :, 2 * D : 3 * D]
    fill = image_fill(fill_ref, st)
    for hp in range(4):
        cols = slice(hp * 128, hp * 128 + 128)
        gq = gk = gv = None
        for mask in masks:
            km = k[:, cols] * mask
            probs = softmax_t(km, q8[:, cols], fill)
            pull = dot_nt(v[:, cols] * mask, go[:, cols])
            centre = jnp.sum(probs * pull, axis=0, keepdims=True)
            ds = jnp.where(fill > 0, probs * (pull - centre), 0.0).astype(BF16)
            dq = dot_tn(ds, km)
            dk = dot_nn(ds, q8[:, cols] * mask)
            dv = dot_nn(probs.astype(BF16), go[:, cols] * mask)
            gq = dq if gq is None else gq + dq
            gk = dk if gk is None else gk + dk
            gv = dv if gv is None else gv + dv
        yield st, hp * 128, gq * HEAD_DIM**-0.5, gk, gv


def attn_bwd_kernel(sc, fill_ref, qkv_ref, gattn_ref, wvo, grad_ref, gs):
    rows = gattn_ref.shape[0]
    gs[HALO : HALO + rows, :] = gattn_ref[...].astype(F32)
    gs[HALO + rows : HALO + rows + 8, :] = jnp.zeros((8, D), F32)
    masks = lane_halves()
    wo = wvo[:, D : 2 * D]

    def image(j, carry):
        for _, at, *grads in image_back(j + 1, sc, fill_ref, qkv_ref, gs, wo, masks):
            for i, grad in enumerate(grads):
                grad_ref[j, :, i * D + at : i * D + at + 128] = grad.astype(BF16)
        return carry

    lax.fori_loop(0, 4, image, 0)


def attn_end_kernel(
    devices,
    places,
    sc,
    tab,
    x_ref,
    fill_ref,
    qkv_ref,
    before_ref,
    gattn_ref,
    after_ref,
    dy1_ref,
    wqk,
    wvo,
    vecs,
    early_ref,
    dwo_ref,
    sums2_ref,
    stats_ref,
    b0,
    b1,
    b2,
    b3,
    dbout_ref,
    dbout_2_ref,
    dtok_ref,
    keep_ref,
    give_ref,
    gs,
    acc,
    a1s,
    gq_s,
    cols,
    bias,
):
    rows = dy1_ref.shape[0]
    halo_rows(gs, before_ref, gattn_ref, after_ref)
    masks = lane_halves()
    wo = wvo[:, D : 2 * D]

    def image(j, carry):
        for st, at, *grads in image_back(j, sc, fill_ref, qkv_ref, gs, wo, masks):
            for i, grad in enumerate(grads):
                acc[pl.ds(st, SLOT), i * D + at : i * D + at + 128] = grad
        return carry

    image(0, 0)
    for j in range(4):
        st = pl.multiple_of(sc[0] + IMG * (j + 1), 8)
        acc[pl.ds(st, SLOT), :] = early_ref[j].astype(F32)
    lax.fori_loop(5, sc[1], image, 0)
    sums = [jnp.zeros((1, D), F32) for _ in range(4)]
    for i in range(rows // 256):
        own = slice(HALO + 256 * i, HALO + 256 * (i + 1))
        here = slice(256 * i, 256 * (i + 1))
        low = acc[own, :].astype(BF16)
        gq_s[here, :] = low
        normed, inverse = norm_parts(x_ref[here, :].astype(F32))
        a1s[here, :] = (normed * vecs[0:1, :] + vecs[1:2, :]).astype(BF16)
        upstream = dot_nt(low[:, : 2 * D], wqk[:, : 2 * D]) + dot_nt(low[:, 2 * D :], wvo[:, :D])
        dtok_ref[here, :] = dy1_ref[here, :] + norm_back(upstream, normed, inverse, vecs[0:1, :])
        parts = (
            upstream * normed,
            upstream,
            low[:, :D].astype(F32),
            low[:, 2 * D :].astype(F32),
        )
        sums = [s + jnp.sum(p, axis=0, keepdims=True) for s, p in zip(sums, parts)]
    cols[...] = jnp.zeros_like(cols)
    for i, s in enumerate(sums):
        cols[i : i + 1, :] = s
    cols[4:8, :] = sums2_ref[4:8, :]
    cols[8:16, :] = stats_ref[...]
    small = cols[...].T.astype(BF16)
    dbin = b0[...] + b1[...] + b2[...] + b3[...]
    dbout = dbout_ref[...] + dbout_2_ref[...]
    bias[...] = jnp.zeros_like(bias)
    for d, line, source, at in bias_lines(devices):
        row = D // devices * d + line
        bias[row : row + 1, :] = (dbin, dbout)[source][
            at // 4 : at // 4 + 1, at % 4 * 128 : at % 4 * 128 + 128
        ]
    a1 = a1s[...]
    dqk = dot_tn(a1, gq_s[:, : 2 * D]).astype(BF16)
    dv = dot_tn(a1, gq_s[:, 2 * D :]).astype(BF16)
    first = jnp.concatenate([dqk, small], axis=1)
    second = jnp.concatenate([dv, dwo_ref[...], bias[...].astype(BF16)], axis=1)
    size = D // 16
    for ref, at, half in ((keep_ref, places, tab[0]), (give_ref, places + 4, 1 - tab[0])):
        for value, own in ((first, 0), (second, 1)):

            @pl.when(half == own)
            def _():
                for b in range(16):
                    ref[b // 4, tab[at + b % 4]] = value[b * size : (b + 1) * size]


def fold_kernel(kinds, *refs):
    step = pl.program_id(0)
    count = len(kinds)
    outs = list(refs[2 * count :])
    for at, kind in enumerate(kinds):
        a, b = refs[2 * at], refs[2 * at + 1]
        total = (a[0].astype(F32) + b[0].astype(F32)).astype(BF16)
        if kind == "sum":
            outs.pop(0)[0] = total
            continue
        low, high = outs.pop(0), outs.pop(0)

        @pl.when(step < 2)
        def _():
            low[0] = total

        @pl.when(step >= 2)
        def _():
            high[0] = total


class Places:
    def __init__(self, n):
        self.n = n
        self.planes = EXPERTS
        self.group = n // EXPERTS
        self.chips = self.group // 2
        self.bits = self.chips.bit_length() - 1
        self.me = lax.axis_index("fsdp")
        self.core = self.me % 2
        self.chip = (self.me // 2) % self.chips
        self.plane = self.me // self.group

    def swap(self):
        return [(i, i ^ 1) for i in range(self.n)]

    def cross(self, step):
        moves = []
        for i in range(self.n):
            bit = step if i % 2 == 0 else self.bits - 1 - step
            moves.append((i, i ^ (2 << bit)))
        return moves

    def turn(self, k):
        return [(i, (i + k * self.group) % self.n) for i in range(self.n)]

    def order(self, core):
        plain = list(range(self.chips))
        back = [int(format(j, "0%db" % self.bits)[::-1], 2) for j in plain]
        rel = jnp.where(core == 0, jnp.array(plain, jnp.int32), jnp.array(back, jnp.int32))
        return jnp.bitwise_xor(self.chip, rel)

    def place(self, core):
        back = [int(format(j, "0%db" % self.bits)[::-1], 2) for j in range(self.chips)]
        rel = jnp.bitwise_xor(self.chip, jnp.arange(self.chips, dtype=jnp.int32))
        return jnp.where(core == 0, rel, jnp.array(back, jnp.int32)[rel])


def send(x, moves):
    return lax.ppermute(x, "fsdp", moves)


def sync(*arrays):
    return lax.optimization_barrier(arrays)


def pair_block(expert_in, expert_out, pos):
    rin, rout = expert_in.shape[0], expert_out.shape[0]
    win = expert_in.reshape(rin, 4, CHUNK)
    halves = [
        jnp.concatenate(
            [expert_out[h * rout // 2 : (h + 1) * rout // 2], win[:, 2 * h], win[:, 2 * h + 1]]
        )
        for h in range(2)
    ]
    first = pos.core == 0
    mine = jnp.where(first, halves[0], halves[1])
    got = send(jnp.where(first, halves[1], halves[0]), pos.swap())
    a = jnp.where(first, mine, got)
    b = jnp.where(first, got, mine)
    if rin % 16 == 0:
        return jnp.concatenate([a, b])
    cut = rout // 2
    return jnp.concatenate(
        [a[:cut], b[:cut], a[cut : cut + rin], b[cut : cut + rin], a[cut + rin :], b[cut + rin :]]
    )


def fold(*items):
    kinds = tuple(kind for kind, _, _ in items)
    args, in_specs, out_specs, out_shape, finals = [], [], [], [], []
    for kind, a, b in items:
        height = a.size // 4 // CHUNK
        args += [a.reshape(4, height, CHUNK), b.reshape(4, height, CHUNK)]
        in_specs += [pl.BlockSpec((1, height, CHUNK), lambda i: (i, 0, 0))] * 2
        if kind == "sum":
            out_specs.append(pl.BlockSpec((1, height, CHUNK), lambda i: (i, 0, 0)))
            shapes = [(4, height, CHUNK)]
            finals.append(a.shape)
        else:
            out_specs.append(
                pl.BlockSpec((1, height, CHUNK), lambda i: (jnp.minimum(i, 1), 0, 0))
            )
            out_specs.append(
                pl.BlockSpec((1, height, CHUNK), lambda i: (jnp.maximum(i - 2, 0), 0, 0))
            )
            shapes = [(2, height, CHUNK)] * 2
            finals += [(a.shape[0] // 2,) + a.shape[1:]] * 2
        out_shape += [jax.ShapeDtypeStruct(shape, BF16) for shape in shapes]
    outs = pl.pallas_call(
        functools.partial(fold_kernel, kinds),
        name="fold",
        grid=(4,),
        in_specs=in_specs,
        out_specs=tuple(out_specs),
        out_shape=tuple(out_shape),
        compiler_params=room("fold"),
        cost_estimate=pl.CostEstimate(flops=1000, bytes_accessed=1000, transcendentals=0),
    )(*args)
    return [out.reshape(shape) for out, shape in zip(outs, finals)]


def add_low(a, b):
    return (a.astype(F32) + b.astype(F32)).astype(BF16)


def local(
    tokens,
    out_grad,
    key_valid,
    expert_ids,
    gate_logits,
    attn_norm_gain,
    attn_norm_bias,
    qkv_weight,
    query_bias,
    value_bias,
    attn_out_weight,
    attn_out_bias,
    moe_norm_gain,
    moe_norm_bias,
    expert_in,
    expert_in_bias,
    expert_out,
    expert_out_bias,
):
    n = lax.axis_size("fsdp")
    pos = Places(n)
    rows = tokens.shape[0]
    ext = rows + 2 * HALO
    width = qkv_weight.shape[0]
    total_rows = rows * n
    vmem = pl.BlockSpec(memory_space=pltpu.VMEM)
    smem = pl.BlockSpec(memory_space=pltpu.SMEM)
    far = pl.BlockSpec(memory_space=pl.ANY)

    def sds(shape, kind):
        return jax.ShapeDtypeStruct(shape, kind)

    def cost(flops, moved, trans=0):
        return pl.CostEstimate(flops=int(flops / 1000), bytes_accessed=int(moved / 1000), transcendentals=trans)

    chips = pos.chips
    if chips == 4:
        keep_place = pos.place(pos.core)
        give_place = pos.place(1 - pos.core)
    else:
        keep_place = give_place = jnp.arange(4, dtype=jnp.int32)
    experts = (pos.plane - jnp.array(SEQ, jnp.int32)) % 4
    tab = jnp.concatenate(
        [
            pos.core.reshape(1),
            experts,
            pos.order(pos.core),
            pos.order(1 - pos.core),
            keep_place,
            give_place,
        ]
    ).astype(jnp.int32)
    up = [(i, i + 1) for i in range(n - 1)]
    down = [(i + 1, i) for i in range(n - 1)]

    def halo(x):
        return send(x[rows - HALO :], up), send(x[:HALO], down)

    flat = jnp.concatenate(
        [
            attn_norm_gain,
            attn_norm_bias,
            query_bias,
            value_bias,
            attn_out_bias,
            moe_norm_gain,
            moe_norm_bias,
            jnp.zeros(((SMALL - 7) * width,), BF16),
        ]
    )

    def lines_of(x):
        lines = max(1, x.shape[0] // 128)
        at = pos.me * x.shape[0] % 128
        return lax.dynamic_update_slice_in_dim(jnp.zeros((lines * 128,), BF16), x, at, 0)

    lines = jnp.concatenate([lines_of(expert_in_bias), lines_of(expert_out_bias)])
    lines = jnp.pad(lines, (0, width * SMALL - lines.shape[0])).reshape(width, SMALL)
    first = pos.core == 0
    half_0 = jnp.concatenate([qkv_weight[:, : 2 * D], flat.reshape(SMALL, width).T], axis=1)
    half_1 = jnp.concatenate([qkv_weight[:, 2 * D :], attn_out_weight, lines], axis=1)
    mine = jnp.where(first, half_0, half_1)
    got = send(jnp.where(first, half_1, half_0), pos.swap())
    block = jnp.where(first, jnp.stack([mine, got]), jnp.stack([got, mine]))
    block = block.reshape(2 * width, HALF)
    pair = pair_block(expert_in, expert_out, pos)

    front = pair[None]
    for step in range(pos.bits - 1):
        got = send(front, pos.cross(step))
        if step < pos.bits - 2:
            front = jnp.concatenate([front, got], axis=0)
    turned = [send(block, pos.turn(k)) for k in range(1, 4)]
    *turned, pair, got = sync(*turned, pair, got)
    have = jnp.stack([block] + turned)[None]
    crossed = send(have, pos.cross(0))
    poscol, posrow, gate = pl.pallas_call(
        route_kernel,
        name="route",
        out_shape=(
            sds((rows, 8), jnp.int32),
            sds((8, rows), jnp.int32),
            sds((rows, TOP), F32),
        ),
        in_specs=[vmem] * 3,
        out_specs=(vmem,) * 3,
        compiler_params=room("fold"),
        cost_estimate=cost(4 * rows * rows * 128, 1 << 20),
    )(expert_ids, expert_ids.T, gate_logits)

    def dispatch(first_k, last_k):
        count = 2 * (last_k - first_k)
        *slots, sums = pl.pallas_call(
            functools.partial(dispatch_kernel, first_k),
            name="dispatch",
            out_shape=tuple([sds((CAP, D), BF16), sds((D, CAP), BF16)] * (count // 2))
            + (sds((EXPERTS, D), F32),),
            in_specs=[smem] + [vmem] * 4,
            out_specs=(far,) * count + (vmem,),
            scratch_shapes=[pltpu.VMEM((CAP, D), BF16), pltpu.VMEM((D, CAP), BF16)] * (count // 2)
            + [pltpu.SemaphoreType.DMA((count,))],
            compiler_params=room("dispatch"),
            cost_estimate=cost(count * rows * CAP * D, 4e6),
        )(tab, out_grad, posrow, expert_ids, gate)
        return slots, sums

    before, behind = halo(tokens)
    crossed, gate, poscol, posrow, before, behind = sync(
        crossed, gate, poscol, posrow, before, behind
    )
    piece = send(pair, pos.turn(SEQ[1]))
    slots, dbout = dispatch(0, 2)
    have = jnp.concatenate([have, crossed], axis=0)
    for step in range(1, pos.bits):
        crossed = send(have, pos.cross(step))
        if step < pos.bits - 1:
            have = jnp.concatenate([have, crossed], axis=0)
    slots_2, dbout_2 = dispatch(2, 4)
    first_row = pos.me * rows
    offset = first_row % IMG
    key_rows = first_row - HALO + jnp.arange(ext, dtype=jnp.int32)
    usable = lax.dynamic_slice_in_dim(jnp.pad(key_valid, (HALO, HALO)), first_row, ext)
    present = (key_rows >= 0) & (key_rows < total_rows)
    fill = jnp.where(usable == 1, 1.0, jnp.where(present, MASKED_SCORE, FAR_SCORE))
    fill = fill.astype(F32).reshape(ext, 1)
    have, crossed, piece, fill, dbout, dbout_2, *slots = sync(
        have, crossed, piece, fill, dbout, dbout_2, *slots, *slots_2
    )
    small = [have, crossed, send(have, pos.swap()), send(crossed, pos.swap())]
    planes = (pos.plane - jnp.arange(4, dtype=jnp.int32)) % 4
    if chips == 4:
        spots = [
            (planes[None, :] * 4 + pos.order(c)[:, None]).reshape(-1)
            for c in (pos.core, 1 - pos.core)
        ]
        small = [x.reshape(8, 2 * width, HALF) for x in small]
    else:
        spots = [jnp.arange(16, dtype=jnp.int32)] * 2
        canonical = []
        for data, c in ((small[:2], pos.core), (small[2:], 1 - pos.core)):
            data = jnp.concatenate(data).reshape(4 * chips, 2 * width, HALF)
            where = (pos.place(c)[None, :] * 4 + planes[:, None]).reshape(-1)
            data = jnp.take(data, where, axis=0).reshape(16, D // 16, HALF)
            canonical += [data[:8], data[8:]]
        small = canonical

    scalars = jnp.concatenate(
        [
            jnp.stack([HALO - offset, (rows + offset + IMG - 1) // IMG, pos.core]),
            jnp.where(first, spots[0], spots[1]),
            jnp.where(first, spots[1], spots[0]),
        ]
    ).astype(jnp.int32)
    def near_chips(piece):
        held = piece[None]
        for step in range(pos.bits - 2):
            held = jnp.concatenate([held, send(held, pos.cross(step))], axis=0)
        return held, send(held, pos.cross(pos.bits - 2))

    held = [jnp.concatenate([front, got])]
    half, got = near_chips(piece)
    flight = [
        send(held[0], pos.cross(pos.bits - 1)),
        send(held[0], pos.swap()),
        got,
        send(pair, pos.turn(SEQ[2])),
    ]
    qkv, o_low, y1, a2, attn_sum, wqk, wvo, vecs, bin_all, bout_all = pl.pallas_call(
        functools.partial(attn_fwd_kernel, n),
        name="attn_fwd",
        out_shape=(
            sds((NIMG, SLOT, 3 * D), BF16),
            sds((rows, D), BF16),
            sds((rows, D), F32),
            sds((rows, D), BF16),
            sds((8, D), F32),
            sds((D, HALF), BF16),
            sds((D, HALF), BF16),
            sds((8, D), F32),
            sds((16, CHUNK), F32),
            sds((EXPERTS, D), F32),
        ),
        in_specs=[smem] + [vmem] * 8,
        out_specs=(far, far, far, vmem, vmem, far, far, vmem, vmem, vmem),
        scratch_shapes=[
            pltpu.VMEM((NIMG, SLOT, 3 * D), BF16),
            pltpu.VMEM((rows, D), BF16),
            pltpu.VMEM((rows, D), F32),
            pltpu.VMEM((D, HALF), BF16),
            pltpu.VMEM((D, HALF), BF16),
            pltpu.VMEM((ext, D), F32),
            pltpu.VMEM((ext, D), F32),
            pltpu.SemaphoreType.DMA((NIMG + 2 + 2 * (rows // 256),)),
        ],
        compiler_params=room("attn_fwd"),
        cost_estimate=cost(30e9, 12e6),
    )(scalars, before, tokens, behind, fill, *small)
    full, front, got, piece, a2, vecs = sync(*flight, a2, vecs)

    rin, rout = expert_in.shape[0], expert_out.shape[0]

    def by_chip(x, core):
        if chips == 4:
            return x
        more = chips // 4
        out = x[:, :256].reshape(4, 256, more, 2 * rout).transpose(0, 2, 1, 3)
        win = x[:, 256:].reshape(4, 2, more, 2 * rin, CHUNK).transpose(0, 2, 1, 3, 4)
        both = [out.reshape(chips, rout, CHUNK), win.reshape(chips, 4 * rin, CHUNK)]
        return jnp.take(jnp.concatenate(both, axis=1), pos.order(core), axis=0)

    def run_expert(k, full, front, back):
        return pl.pallas_call(
            functools.partial(expert_kernel, k, chips),
            name="expert_%d" % k,
            out_shape=(
                sds((CAP, D), BF16),
                sds((CAP, D), BF16),
                sds((16, CHUNK), F32),
                sds((4, CHUNK, CHUNK), BF16),
                sds((4, CHUNK, CHUNK), BF16),
            ),
            in_specs=[smem] + [vmem] * 10,
            out_specs=(vmem,) * 5,
            scratch_shapes=[
                pltpu.VMEM((4, D, CHUNK), BF16),
                pltpu.VMEM((FF, D), BF16),
                pltpu.VMEM((CAP, D), BF16),
                pltpu.VMEM((D, CAP), BF16),
                pltpu.VMEM((4, CAP, CHUNK), BF16),
                pltpu.VMEM((4, CAP, CHUNK), BF16),
            ],
            compiler_params=room("expert"),
            cost_estimate=cost(10e9, 14e6),
        )(
            tab,
            a2,
            slots[2 * k],
            slots[2 * k + 1],
            posrow,
            bin_all,
            bout_all,
            held[k],
            full,
            front,
            back,
        )

    def first_sum(k, got):
        return ("halves", by_chip(results[k][3], pos.core), got)

    def give_of(k, *others):
        return send(sync(by_chip(results[k][4], 1 - pos.core), *others)[0], pos.swap())

    top = pos.bits - 1

    def send_top(x):
        return send(x, pos.cross(top))

    def send_low(keep, x):
        for step in reversed(range(1, top)):
            total = add_low(keep, send(x, pos.cross(step)))
            keep, x = total[: total.shape[0] // 2], total[total.shape[0] // 2 :]
        return keep, send(x, pos.cross(0))

    results = []
    back = send(full, pos.swap())
    held.append(jnp.concatenate([half, got]))
    half, got = near_chips(piece)
    flight = [
        send(held[1], pos.cross(top)),
        send(held[1], pos.swap()),
        got,
        send(pair, pos.turn(SEQ[3])),
    ]
    done = sync(*run_expert(0, full, front, back), *flight, a2)
    results.append(done[:5])
    full, front, got, piece, a2 = done[5:]
    back = send(full, pos.swap())

    held.append(jnp.concatenate([half, got]))
    half, got = near_chips(piece)
    flight = [send(held[2], pos.cross(top)), send(held[2], pos.swap()), got, give_of(0, back)]
    done = sync(*run_expert(1, full, front, back), *flight, a2)
    results.append(done[:5])
    full, front, got, swap_0, a2 = done[5:]
    back = send(full, pos.swap())

    held.append(jnp.concatenate([half, got]))
    flight = [send(held[3], pos.cross(top)), send(held[3], pos.swap()), give_of(1, back)]
    done = sync(*run_expert(2, full, front, back), *flight, a2)
    results.append(done[:5])
    full, front, swap_1, a2 = done[5:]
    back = send(full, pos.swap())

    keep_1, give_1 = fold(first_sum(1, swap_1))
    flight = [send_top(give_1), give_of(2, back)]
    done = sync(*run_expert(3, full, front, back), *flight, a2)
    results.append(done[:5])
    top_1, swap_2, a2 = done[5:]

    keep_1, give_1, keep_2, give_2 = fold(("halves", keep_1, top_1), first_sum(2, swap_2))
    keep_1, got = send_low(keep_1, give_1)
    flight = [got, send_top(give_2), give_of(3)]
    routing = (tab, poscol, expert_ids, gate, out_grad)
    middle = pl.pallas_call(
        middle_kernel,
        name="middle",
        out_shape=(
            sds((rows, D), BF16),
            sds((rows, D), F32),
            sds((rows, D), BF16),
            sds((D, D), BF16),
            sds((rows, TOP), F32),
            sds((8, D), F32),
            sds((8, D), F32),
        ),
        in_specs=[smem] + [vmem] * 17,
        out_specs=(vmem,) * 7,
        scratch_shapes=[pltpu.VMEM((rows, D), F32), pltpu.VMEM((rows, D), F32)],
        compiler_params=room("middle"),
        cost_estimate=cost(9 * 2 * rows * CAP * D, 16e6),
    )(
        *routing,
        *(r[0] for r in results),
        *(r[1] for r in results),
        y1,
        o_low,
        fill,
        vecs,
        attn_sum,
    )
    done = sync(*middle, *flight)
    block_out, dy1, gattn, dwo, logits_grad, sums2, stats, low_1, top_2, swap_3 = done

    sum_1, keep_2, give_2, keep_3, give_3 = fold(
        ("sum", keep_1, low_1), ("halves", keep_2, top_2), first_sum(3, swap_3)
    )
    keep_2, got = send_low(keep_2, give_2)

    def home(k, x):
        return send(x, pos.turn(4 - SEQ[k]))

    flight = [got, send_top(give_3), home(1, sum_1[0]), *halo(gattn)]
    early = pl.pallas_call(
        attn_bwd_kernel,
        name="attn_bwd_early",
        out_shape=sds((4, SLOT, 3 * D), BF16),
        in_specs=[smem] + [vmem] * 4,
        out_specs=vmem,
        scratch_shapes=[pltpu.VMEM((ext, D), F32)],
        compiler_params=room("early"),
        cost_estimate=cost(30e9, 8e6),
    )(scalars, fill, qkv, gattn, wvo)
    early, low_2, top_3, home_1, before, behind = sync(early, *flight)

    sum_2, keep_3, give_3, keep_0, give_0 = fold(
        ("sum", keep_2, low_2), ("halves", keep_3, top_3), first_sum(0, swap_0)
    )
    keep_3, got = send_low(keep_3, give_3)
    cut = sum_2.shape[1] // 2
    flight = [got, home(2, sum_2[0, :cut]), send_top(give_0)]
    tokens_grad, rest_keep, rest_give = pl.pallas_call(
        functools.partial(attn_end_kernel, n, 5 + 2 * chips),
        name="attn_bwd_late",
        out_shape=(
            sds((rows, D), F32),
            sds((EXPERTS, 4, D // 16, HALF), BF16),
            sds((EXPERTS, 4, D // 16, HALF), BF16),
        ),
        in_specs=[smem] * 2 + [vmem] * 20,
        out_specs=(vmem,) * 3,
        scratch_shapes=[
            pltpu.VMEM((ext, D), F32),
            pltpu.VMEM((ext, 3 * D), F32),
            pltpu.VMEM((rows, D), BF16),
            pltpu.VMEM((rows, 3 * D), BF16),
            pltpu.VMEM((128, D), F32),
            pltpu.VMEM((D, SMALL), F32),
        ],
        compiler_params=room("late"),
        cost_estimate=cost(30e9, 16e6),
    )(
        scalars,
        tab,
        tokens,
        fill,
        qkv,
        before,
        gattn,
        behind,
        dy1,
        wqk,
        wvo,
        vecs,
        early,
        dwo,
        sums2,
        stats,
        *(r[2] for r in results),
        dbout,
        dbout_2,
    )

    tokens_grad, rest_keep, rest_give, low_3, home_2, top_0 = sync(
        tokens_grad, rest_keep, rest_give, *flight
    )

    def by_block(x, core):
        if chips == 4:
            return x
        return jnp.take(x.reshape(EXPERTS, chips, 2 * width, HALF), pos.order(core), axis=1)

    sum_3, keep_0, give_0 = fold(("sum", keep_3, low_3), ("halves", keep_0, top_0))
    keep_0, got = send_low(keep_0, give_0)
    home_2b = home(2, sum_2[0, cut:])
    home_3 = home(3, sum_3[0])
    rest = add_low(
        by_block(rest_keep, pos.core), send(by_block(rest_give, 1 - pos.core), pos.swap())
    )

    def cross(x, step, *others):
        x = x.reshape((EXPERTS, 2, -1) + x.shape[2:])
        swapped, *others = sync(send(x[:, 1], pos.cross(step)), *others)
        return [add_low(x[:, 0], swapped)] + others

    (rest,) = cross(rest, top)
    for step in reversed(range(1, top)):
        (rest,) = cross(rest, step)
    rest, home_2b, home_3, got = cross(rest, 0, home_2b, home_3, got)
    home_2 = jnp.concatenate([home_2, home_2b])
    total = keep_0[0].astype(F32) + got[0].astype(F32)
    for got in (home_1, home_2, home_3):
        total = total + got.astype(F32)
    rest = rest[:, 0]

    def block_for(k):
        return lax.dynamic_index_in_dim(rest, (pos.plane + k) % 4, 0, keepdims=False)

    others = [send(block_for(k), pos.turn(k)) for k in range(1, 4)]

    def own_halves(pair, axis):
        mine = lax.dynamic_index_in_dim(pair, pos.core, 0, keepdims=False)
        got = send(lax.dynamic_index_in_dim(pair, 1 - pos.core, 0, keepdims=False), pos.swap())
        return jnp.where(
            pos.core == 0,
            jnp.concatenate([mine, got], axis=axis),
            jnp.concatenate([got, mine], axis=axis),
        )

    out_sum = total[:rout].reshape(256, 2, rout).transpose(1, 0, 2)
    expert_out_grad = own_halves(out_sum, 0).T
    in_sum = total[rout:].reshape(2, 2, rin, CHUNK).transpose(1, 2, 0, 3)
    expert_in_grad = own_halves(in_sum.reshape(2, rin, 2 * CHUNK), 1)

    *others, expert_out_grad, expert_in_grad = sync(*others, expert_out_grad, expert_in_grad)
    rest = block_for(0).astype(F32)
    for got in others:
        rest = rest + got.astype(F32)

    rest = own_halves(rest.reshape(2, width, HALF), 1)
    tail = rest[:, 2 * D : HALF]
    bias = rest[:, HALF + 2 * D :].reshape(-1)
    count = jnp.sum((key_valid == 1).astype(F32))
    block_stats = jnp.sqrt(tail[0, 8:11] / (count * D))
    in_size, out_size = expert_in_bias.shape[0], expert_out_bias.shape[0]
    lines = max(1, in_size // 128)

    def bias_part(line, size):
        return lax.dynamic_slice_in_dim(bias, line * 128 + pos.me * size % 128, size)

    return (
        block_out,
        tokens_grad,
        logits_grad,
        tail[:, 0],
        tail[:, 1],
        jnp.concatenate([rest[:, : 2 * D], rest[:, HALF : HALF + D]], axis=1),
        tail[:, 2],
        tail[:, 3],
        rest[:, HALF + D : HALF + 2 * D],
        tail[:, 4],
        tail[:, 5],
        tail[:, 6],
        expert_in_grad,
        bias_part(0, in_size),
        expert_out_grad,
        bias_part(lines, out_size),
        block_stats,
    )


def solution(mesh):
    row = P("fsdp", None)
    vec = P("fsdp")
    return jax.shard_map(
        local,
        mesh=mesh,
        in_specs=(
            row,
            row,
            P(),
            row,
            row,
            vec,
            vec,
            row,
            vec,
            vec,
            row,
            vec,
            vec,
            vec,
            row,
            vec,
            row,
            vec,
        ),
        out_specs=(
            row,
            row,
            row,
            vec,
            vec,
            row,
            vec,
            vec,
            row,
            vec,
            vec,
            vec,
            row,
            vec,
            row,
            vec,
            P(),
        ),
        check_vma=False,
    )
```

```python
import functools

import jax
import jax.numpy as jnp
from jax import lax
from jax.experimental import pallas as pl
from jax.experimental.pallas import tpu as pltpu
from jax.sharding import PartitionSpec as P

D = 512
FF = 2048
HEAD_DIM = 64
EXPERTS = 4
TOP = 2
IMG = 200
CAP = 640
HALO = 200
SLOT = 208
NIMG = 7
CHUNK = 512
SMALL = 128
HALF = 1024 + SMALL

SEQ = (0, 1, 2, 3)

EPS = 1e-06
MASKED_SCORE = -1000000000.0
FAR_SCORE = -1e30
F32 = jnp.float32
BF16 = jnp.bfloat16
VMEM_MIB = {"attn_fwd": 48, "dispatch": 60, "expert": 22, "middle": 18, "early": 8, "late": 23, "fold": 14}


def room(name):
    return pltpu.CompilerParams(vmem_limit_bytes=VMEM_MIB[name] * 1024 * 1024)


def dot_nn(a, b):
    return lax.dot_general(a, b, (((1,), (0,)), ((), ())), preferred_element_type=F32)


def dot_nt(a, b):
    return lax.dot_general(a, b, (((1,), (1,)), ((), ())), preferred_element_type=F32)


def dot_tn(a, b):
    return lax.dot_general(a, b, (((0,), (0,)), ((), ())), preferred_element_type=F32)


def norm_parts(values):
    average = jnp.mean(values, axis=-1, keepdims=True)
    centered = values - average
    inverse = lax.rsqrt(jnp.mean(centered * centered, axis=-1, keepdims=True) + EPS)
    return centered * inverse, inverse


def norm_back(upstream, normed, inverse, gain):
    scaled = upstream * gain
    inner = (
        scaled
        - jnp.mean(scaled, axis=-1, keepdims=True)
        - normed * jnp.mean(scaled * normed, axis=-1, keepdims=True)
    )
    return inverse * inner


def route_kernel(ids_ref, idst_ref, logits_ref, poscol_ref, posrow_ref, gate_ref):
    rows = ids_ref.shape[0]
    lane = lax.broadcasted_iota(jnp.int32, (rows, 128), 1)
    chosen = (ids_ref[:, 0:1] == lane) | (ids_ref[:, 1:2] == lane)
    r0 = lax.broadcasted_iota(jnp.int32, (rows, rows), 0)
    r1 = lax.broadcasted_iota(jnp.int32, (rows, rows), 1)
    lower = jnp.where(r1 < r0, 1.0, 0.0).astype(BF16)
    upper = jnp.where(r0 < r1, 1.0, 0.0).astype(BF16)
    count = dot_nn(lower, jnp.where(chosen, 1.0, 0.0).astype(BF16))
    pos = jnp.where(chosen, count, -1.0)
    poscol_ref[...] = pos[:, :8].astype(jnp.int32)
    sub = lax.broadcasted_iota(jnp.int32, (16, rows), 0)
    chosen_t = (idst_ref[0:1, :] == sub) | (idst_ref[1:2, :] == sub)
    count_t = dot_nn(jnp.where(chosen_t, 1.0, 0.0).astype(BF16), upper)
    posrow_ref[...] = jnp.where(chosen_t, count_t, -1.0)[:8].astype(jnp.int32)
    a = logits_ref[:, 0:1]
    b = logits_ref[:, 1:2]
    top = jnp.maximum(a, b)
    ea = jnp.exp(a - top)
    eb = jnp.exp(b - top)
    total = ea + eb
    which = lax.broadcasted_iota(jnp.int32, (rows, 2), 1)
    gate_ref[...] = jnp.where(which == 0, ea / total, eb / total)


def image_fill(fill_ref, st):
    fill = fill_ref[pl.ds(st, SLOT), :]
    row = lax.broadcasted_iota(jnp.int32, (SLOT, 1), 0)
    return jnp.where(row < IMG, fill, FAR_SCORE)


def lane_halves():
    lane = lax.broadcasted_iota(jnp.int32, (1, 128), 1)
    low = jnp.where(lane < HEAD_DIM, 1.0, 0.0).astype(BF16)
    return low, (1.0 - low.astype(F32)).astype(BF16)


def stack_heads(x, masks):
    return jnp.concatenate([x * mask for mask in masks], axis=0)


def pair_dot(stacked, other):
    both = dot_nt(stacked, other)
    return both[:SLOT], both[SLOT:]


def softmax_t(scores, fill):
    scores = jnp.where(fill > 0, scores, fill)
    raised = jnp.exp(scores - jnp.max(scores, axis=0, keepdims=True))
    return raised * (1.0 / jnp.sum(raised, axis=0, keepdims=True))


def bias_lines(devices):
    lines = max(1, EXPERTS * FF // devices // 128)
    for d in range(devices):
        for i in range(lines):
            yield d, i, 0, EXPERTS * FF // devices * d // 128 + i
        yield d, lines, 1, EXPERTS * D // devices * d // 128


def halo_rows(out, before_ref, x_ref, after_ref):
    rows = x_ref.shape[0]
    out[0:HALO, :] = before_ref[...].astype(F32)
    out[HALO : HALO + rows, :] = x_ref[...].astype(F32)
    out[HALO + rows :, :] = after_ref[...].astype(F32)


def attn_fwd_kernel(
    devices,
    sc,
    before_ref,
    x_ref,
    after_ref,
    fill_ref,
    mine_0,
    mine_1,
    other_0,
    other_1,
    qkv_hbm,
    o_hbm,
    y1_hbm,
    a2_ref,
    stat_ref,
    wqk_hbm,
    wvo_hbm,
    vecs,
    bin_ref,
    bout_ref,
    qkv_ref,
    o_ref,
    y1_ref,
    wqk,
    wvo,
    xs,
    os_,
    sems,
):
    rows = a2_ref.shape[0]
    size = D // 16
    mine, other = (mine_0, mine_1), (other_0, other_1)
    for core, refs in ((0, (mine, other)), (1, (other, mine))):

        @pl.when(sc[2] == core)
        def _():
            for at in range(16):
                for ref, out, base in ((refs[0], wqk, 3), (refs[1], wvo, 19)):
                    row = pl.multiple_of(sc[base + at] * size, size)
                    out[pl.ds(row, size), :] = ref[at // 8][at % 8]

    weights_out = [
        pltpu.make_async_copy(wqk, wqk_hbm, sems.at[NIMG]),
        pltpu.make_async_copy(wvo, wvo_hbm, sems.at[NIMG + 1]),
    ]
    for copy in weights_out:
        copy.start()
    vecs[...] = wqk[:, 2 * D :].astype(F32).T[:8]
    bias = wvo[:, 2 * D :].astype(F32)
    bin_ref[...] = jnp.zeros_like(bin_ref)
    bout_ref[...] = jnp.zeros_like(bout_ref)
    for d, line, out, at in bias_lines(devices):
        out = (bin_ref, bout_ref)[out]
        row = D // devices * d + line
        here = (slice(at // 4, at // 4 + 1), slice(at % 4 * 128, at % 4 * 128 + 128))
        out[here] += bias[row : row + 1, :]
    halo_rows(xs, before_ref, x_ref, after_ref)
    masks = lane_halves()

    def image(j, carry):
        st = pl.multiple_of(sc[0] + IMG * j, 8)
        normed, _ = norm_parts(xs[pl.ds(st, SLOT), :])
        a1 = (normed * vecs[0:1, :] + vecs[1:2, :]).astype(BF16)
        qk = dot_nn(a1, wqk[:, : 2 * D])
        q = (qk[:, :D] + vecs[2:3, :]).astype(BF16)
        k = qk[:, D:].astype(BF16)
        v = (dot_nn(a1, wvo[:, :D]) + vecs[3:4, :]).astype(BF16)
        qkv_ref[j, :, 0:D] = q
        qkv_ref[j, :, D : 2 * D] = k
        qkv_ref[j, :, 2 * D : 3 * D] = v
        fill = image_fill(fill_ref, st)
        q8 = q * jnp.asarray(HEAD_DIM**-0.5, BF16)
        for hp in range(4):
            cols = slice(hp * 128, hp * 128 + 128)
            probs = [
                softmax_t(scores, fill).astype(BF16)
                for scores in pair_dot(stack_heads(k[:, cols], masks), q8[:, cols])
            ]
            probs = jnp.concatenate(probs, axis=0)
            os_[pl.ds(st, SLOT), cols] = dot_tn(probs, stack_heads(v[:, cols], masks))
        pltpu.make_async_copy(qkv_ref.at[j], qkv_hbm.at[j], sems.at[j]).start()
        return carry

    def image_out(j, carry):
        pltpu.make_async_copy(qkv_ref.at[j], qkv_hbm.at[j], sems.at[j]).wait()
        return carry

    lax.fori_loop(0, sc[1], image, 0)
    rows_out = []
    total = jnp.zeros((1, D), F32)
    for i in range(rows // 256):
        own = slice(HALO + 256 * i, HALO + 256 * (i + 1))
        here = slice(256 * i, 256 * (i + 1))
        o_low = os_[own, :].astype(BF16)
        o_ref[here, :] = o_low
        attn = dot_nn(o_low, wvo[:, D : 2 * D]) + vecs[4:5, :]
        valid = jnp.where(fill_ref[own, :] > 0, 1.0, 0.0)
        total = total + jnp.sum(valid * attn * attn, axis=0, keepdims=True)
        y1 = xs[own, :] + attn
        y1_ref[here, :] = y1
        normed, _ = norm_parts(y1)
        a2_ref[here, :] = (normed * vecs[5:6, :] + vecs[6:7, :]).astype(BF16)
        at = NIMG + 2 + 2 * i
        rows_out.append(pltpu.make_async_copy(o_ref.at[here], o_hbm.at[here], sems.at[at]))
        rows_out.append(pltpu.make_async_copy(y1_ref.at[here], y1_hbm.at[here], sems.at[at + 1]))
        rows_out[-2].start()
        rows_out[-1].start()
    stat_ref[...] = jnp.broadcast_to(total, (8, D))
    lax.fori_loop(0, sc[1], image_out, 0)
    for copy in weights_out + rows_out:
        copy.wait()


def gelu_both(x):
    square = x * x
    t = jnp.tanh(0.7978845608028654 * (x + 0.044715 * (x * square)))
    half = 0.5 * (1.0 + t)
    slope = half + 0.5 * x * (1.0 - t * t) * (
        0.7978845608028654 * (1.0 + (3.0 * 0.044715) * square)
    )
    return x * half, slope


def gate_of(e, ids_ref, gate_ref):
    return jnp.sum(jnp.where(ids_ref[...] == e, gate_ref[...], 0.0), axis=1, keepdims=True)


def dispatch_kernel(first, tab, g_ref, posrow, ids_ref, gate_ref, *outs):
    rows = g_ref.shape[0]
    count = (len(outs) - 2) // 2
    sums_ref = outs[count]
    *held, sems = outs[count + 1 :]
    copies = [pltpu.make_async_copy(held[i], outs[i], sems.at[i]) for i in range(count)]
    g = g_ref[...].astype(F32)
    slot = lax.broadcasted_iota(jnp.int32, (CAP, rows), 0)
    sums_ref[...] = jnp.zeros_like(sums_ref)
    for k in range(count // 2):
        e = tab[1 + first + k]
        pick = jnp.where(posrow[pl.ds(e, 1), :] == slot, 1.0, 0.0).astype(BF16)
        gy = (gate_of(e, ids_ref, gate_ref) * g).astype(BF16)
        gslot = dot_nn(pick, gy)
        sums_ref[pl.ds(e, 1), :] = jnp.sum(gslot, axis=0, keepdims=True)
        gslot = gslot.astype(BF16)
        held[2 * k][...] = gslot
        copies[2 * k].start()
        held[2 * k + 1][...] = gslot.T
        copies[2 * k + 1].start()
    for copy in copies:
        copy.wait()


def expert_kernel(
    item,
    chips,
    tab,
    a2_ref,
    gg,
    gt,
    posrow,
    bin_ref,
    bout_ref,
    mine0,
    mine1,
    other0,
    other1,
    y_ref,
    da_ref,
    dbin_ref,
    keep,
    give,
    win,
    wout,
    xg,
    xt,
    hall,
    dall,
):
    core = tab[0]
    e = tab[1 + item]
    half_chips = chips // 2
    rows = a2_ref.shape[0]
    span = D // chips
    part = CHUNK * 4 // chips // 4
    orders = 5
    places = orders + 2 * chips

    def sort_weights():
        for half_at, pieces in ((0, (mine0, mine1)), (1, (other0, other1))):
            half = core if half_at == 0 else 1 - core
            for number, piece in enumerate(pieces):
                for j in range(half_chips):
                    chip = tab[orders + half_at * chips + number * half_chips + j]
                    for c in range(2):
                        at = pl.multiple_of((chip * 4 + 2 * c + half) * part, part)
                        here = c * 2 * part if span % 32 == 0 else c * part
                        wout[pl.ds(at, part), :] = piece[j, here : here + part, :]
                    for i in range(2):
                        out = win.at[2 * half + i]
                        if span % 32 == 0:
                            for c in range(2):
                                at = pl.multiple_of(chip * span + c * span // 2, span // 2)
                                here = c * 2 * part + part + i * span // 2
                                out[pl.ds(at, span // 2), :] = piece[j, here : here + span // 2, :]
                        else:
                            at = pl.multiple_of(chip * span, span)
                            here = 2 * part + i * span
                            out[pl.ds(at, span), :] = piece[j, here : here + span, :]

    slot = lax.broadcasted_iota(jnp.int32, (CAP, rows), 0)
    pick = jnp.where(posrow[pl.ds(e, 1), :] == slot, 1.0, 0.0).astype(BF16)
    x = dot_nn(pick, a2_ref[...]).astype(BF16)
    xg[...] = x
    xt[...] = x.T
    dbin_ref[...] = jnp.zeros_like(dbin_ref)
    sort_weights()

    for c in range(4):
        row = e * 4 + c
        w1 = win[c]
        w2 = wout[CHUNK * c : CHUNK * (c + 1), :]
        total = jnp.zeros((1, CHUNK), F32)
        for r in range(2):
            here = slice(r * (CAP // 2), (r + 1) * (CAP // 2))
            pre = dot_nn(xg[here, :], w1) + bin_ref[pl.ds(row, 1), :]
            hidden, slope = gelu_both(pre)
            hall[c, here, :] = hidden.astype(BF16)
            dpre = (dot_nt(gg[here, :], w2) * slope).astype(BF16)
            dall[c, here, :] = dpre
            total = total + jnp.sum(dpre.astype(F32), axis=0, keepdims=True)
        dbin_ref[pl.ds(row, 1), :] = total

    mine = pl.multiple_of(core * 256, 256)
    theirs = pl.multiple_of((1 - core) * 256, 256)
    for i in range(2):
        for first, where, at in ((1 - core, give, places + 4), (core, keep, places)):
            dwin = dot_nn(xt[...], dall[2 * first + i]).astype(BF16)
            for b in range(4):
                where[tab[at + b], 256 + 128 * i : 384 + 128 * i, :] = dwin[128 * b : 128 * (b + 1)]
    for c in range(4):
        give[tab[places + 4 + c], 0:256, :] = dot_nn(gt[pl.ds(theirs, 256), :], hall[c]).astype(BF16)
        keep[tab[places + c], 0:256, :] = dot_nn(gt[pl.ds(mine, 256), :], hall[c]).astype(BF16)

    hidden = jnp.concatenate([hall[c] for c in range(4)], axis=1)
    y = dot_nn(hidden, wout[...]) + bout_ref[pl.ds(e, 1), :]
    y_ref[...] = y.astype(BF16)
    da = None
    for c in range(4):
        more = dot_nt(dall[c], win[c])
        da = more if da is None else da + more
    da_ref[...] = da.astype(BF16)


def combine(e, poscol, ids_ref, gate_ref, g_ref, y, da):
    rows = poscol.shape[0]
    lane = lax.broadcasted_iota(jnp.int32, (rows, 8), 1)
    pos = jnp.sum(jnp.where(lane == e, poscol[...], 0), axis=1, keepdims=True)
    slot = lax.broadcasted_iota(jnp.int32, (rows, CAP), 1)
    place = jnp.where(pos == slot, 1.0, 0.0).astype(BF16)
    yrow = dot_nn(place, y)
    pull = jnp.sum(g_ref[...].astype(F32) * yrow, axis=1, keepdims=True)
    dgate = jnp.where(ids_ref[...] == e, pull, 0.0)
    return gate_of(e, ids_ref, gate_ref) * yrow, dot_nn(place, da), dgate


def middle_kernel(
    tab,
    poscol,
    ids_ref,
    gate_ref,
    g_ref,
    s0,
    s1,
    s2,
    s3,
    t0,
    t1,
    t2,
    t3,
    y1_ref,
    o_ref,
    fill_ref,
    vecs,
    attn_sum,
    out_ref,
    dy1_ref,
    gattn_ref,
    dwo_ref,
    lgrad_ref,
    sums_ref,
    stats_ref,
    moe_ref,
    da2_ref,
):
    shared = (poscol, ids_ref, gate_ref, g_ref)
    dgate = 0.0
    for k, (y, da) in enumerate(((s0, t0), (s1, t1), (s2, t2), (s3, t3))):
        moe, da2, pull = combine(tab[1 + k], *shared, y[...], da[...])
        dgate = dgate + pull
        if k == 0:
            moe_ref[...] = moe
            da2_ref[...] = da2
        else:
            moe_ref[...] += moe
            da2_ref[...] += da2
    rows = y1_ref.shape[0]
    sums = [jnp.zeros((1, D), F32) for _ in range(5)]
    for i in range(rows // 256):
        here = slice(256 * i, 256 * (i + 1))
        y1 = y1_ref[here, :]
        moe = moe_ref[here, :]
        value = y1 + moe
        out_ref[here, :] = value.astype(BF16)
        valid = jnp.where(fill_ref[HALO + 256 * i : HALO + 256 * (i + 1), :] > 0, 1.0, 0.0)
        normed, inverse = norm_parts(y1)
        upstream = da2_ref[here, :]
        dy1 = g_ref[here, :].astype(F32) + norm_back(upstream, normed, inverse, vecs[5:6, :])
        dy1_ref[here, :] = dy1
        low = dy1.astype(BF16)
        gattn_ref[here, :] = low
        parts = (
            upstream * normed,
            upstream,
            low.astype(F32),
            valid * value * value,
            valid * moe * moe,
        )
        sums = [s + jnp.sum(p, axis=0, keepdims=True) for s, p in zip(sums, parts)]
    sums_ref[...] = jnp.zeros_like(sums_ref)
    stats_ref[...] = jnp.zeros_like(stats_ref)
    for i, s in ((4, sums[2]), (5, sums[0]), (6, sums[1])):
        sums_ref[i : i + 1, :] = s
    for i, s in enumerate((sums[3], attn_sum[0:1, :], sums[4])):
        stats_ref[i : i + 1, :] = jnp.broadcast_to(jnp.sum(s, axis=1, keepdims=True), (1, D))
    dwo_ref[...] = dot_tn(o_ref[...], gattn_ref[...]).astype(BF16)
    gate = gate_ref[...]
    lgrad_ref[...] = gate * (dgate - jnp.sum(gate * dgate, axis=1, keepdims=True))


def image_back(j, sc, fill_ref, qkv_ref, gs, wo, masks):
    st = pl.multiple_of(sc[0] + IMG * j, 8)
    row = lax.broadcasted_iota(jnp.int32, (SLOT, 1), 0)
    upstream = jnp.where(row < IMG, gs[pl.ds(st, SLOT), :], 0.0).astype(BF16)
    go = dot_nt(upstream, wo).astype(BF16)
    q8 = qkv_ref[j, :, 0:D] * jnp.asarray(HEAD_DIM**-0.5, BF16)
    k = qkv_ref[j, :, D : 2 * D]
    v = qkv_ref[j, :, 2 * D : 3 * D]
    fill = image_fill(fill_ref, st)
    for hp in range(4):
        cols = slice(hp * 128, hp * 128 + 128)
        keys = stack_heads(k[:, cols], masks)
        scores = pair_dot(keys, q8[:, cols])
        pulls = pair_dot(stack_heads(v[:, cols], masks), go[:, cols])
        probs = [softmax_t(x, fill) for x in scores]
        ds = []
        for prob, pull in zip(probs, pulls):
            centre = jnp.sum(prob * pull, axis=0, keepdims=True)
            ds.append(jnp.where(fill > 0, prob * (pull - centre), 0.0).astype(BF16))
        gq = dot_tn(jnp.concatenate(ds, axis=0), keys)
        gk = gv = 0.0
        for mask, grad, prob in zip(masks, ds, probs):
            gk = gk + dot_nn(grad, q8[:, cols] * mask)
            gv = gv + dot_nn(prob.astype(BF16), go[:, cols] * mask)
        yield st, hp * 128, gq * HEAD_DIM**-0.5, gk, gv


def attn_bwd_kernel(sc, fill_ref, qkv_ref, gattn_ref, wvo, grad_ref, gs):
    rows = gattn_ref.shape[0]
    gs[HALO : HALO + rows, :] = gattn_ref[...].astype(F32)
    gs[HALO + rows : HALO + rows + 8, :] = jnp.zeros((8, D), F32)
    masks = lane_halves()
    wo = wvo[:, D : 2 * D]

    def image(j, carry):
        for _, at, *grads in image_back(j + 1, sc, fill_ref, qkv_ref, gs, wo, masks):
            for i, grad in enumerate(grads):
                grad_ref[j, :, i * D + at : i * D + at + 128] = grad.astype(BF16)
        return carry

    lax.fori_loop(0, 4, image, 0)


def attn_end_kernel(
    devices,
    places,
    sc,
    tab,
    x_ref,
    fill_ref,
    qkv_ref,
    before_ref,
    gattn_ref,
    after_ref,
    dy1_ref,
    wqk,
    wvo,
    vecs,
    early_ref,
    dwo_ref,
    sums2_ref,
    stats_ref,
    b0,
    b1,
    b2,
    b3,
    dbout_ref,
    dbout_2_ref,
    dtok_ref,
    keep_ref,
    give_ref,
    gs,
    acc,
    a1s,
    gq_s,
    cols,
    bias,
):
    rows = dy1_ref.shape[0]
    halo_rows(gs, before_ref, gattn_ref, after_ref)
    masks = lane_halves()
    wo = wvo[:, D : 2 * D]

    def image(j, carry):
        for st, at, *grads in image_back(j, sc, fill_ref, qkv_ref, gs, wo, masks):
            for i, grad in enumerate(grads):
                acc[pl.ds(st, SLOT), i * D + at : i * D + at + 128] = grad
        return carry

    image(0, 0)
    for j in range(4):
        st = pl.multiple_of(sc[0] + IMG * (j + 1), 8)
        acc[pl.ds(st, SLOT), :] = early_ref[j].astype(F32)
    lax.fori_loop(5, sc[1], image, 0)
    sums = [jnp.zeros((1, D), F32) for _ in range(4)]
    for i in range(rows // 256):
        own = slice(HALO + 256 * i, HALO + 256 * (i + 1))
        here = slice(256 * i, 256 * (i + 1))
        low = acc[own, :].astype(BF16)
        gq_s[here, :] = low
        normed, inverse = norm_parts(x_ref[here, :].astype(F32))
        a1s[here, :] = (normed * vecs[0:1, :] + vecs[1:2, :]).astype(BF16)
        upstream = dot_nt(low[:, : 2 * D], wqk[:, : 2 * D]) + dot_nt(low[:, 2 * D :], wvo[:, :D])
        dtok_ref[here, :] = dy1_ref[here, :] + norm_back(upstream, normed, inverse, vecs[0:1, :])
        parts = (
            upstream * normed,
            upstream,
            low[:, :D].astype(F32),
            low[:, 2 * D :].astype(F32),
        )
        sums = [s + jnp.sum(p, axis=0, keepdims=True) for s, p in zip(sums, parts)]
    cols[...] = jnp.zeros_like(cols)
    for i, s in enumerate(sums):
        cols[i : i + 1, :] = s
    cols[4:8, :] = sums2_ref[4:8, :]
    cols[8:16, :] = stats_ref[...]
    small = cols[...].T.astype(BF16)
    dbin = b0[...] + b1[...] + b2[...] + b3[...]
    dbout = dbout_ref[...] + dbout_2_ref[...]
    bias[...] = jnp.zeros_like(bias)
    for d, line, source, at in bias_lines(devices):
        row = D // devices * d + line
        bias[row : row + 1, :] = (dbin, dbout)[source][
            at // 4 : at // 4 + 1, at % 4 * 128 : at % 4 * 128 + 128
        ]
    a1 = a1s[...]
    dqk = dot_tn(a1, gq_s[:, : 2 * D]).astype(BF16)
    dv = dot_tn(a1, gq_s[:, 2 * D :]).astype(BF16)
    first = jnp.concatenate([dqk, small], axis=1)
    second = jnp.concatenate([dv, dwo_ref[...], bias[...].astype(BF16)], axis=1)
    size = D // 16
    for ref, at, half in ((keep_ref, places, tab[0]), (give_ref, places + 4, 1 - tab[0])):
        for value, own in ((first, 0), (second, 1)):

            @pl.when(half == own)
            def _():
                for b in range(16):
                    ref[b // 4, tab[at + b % 4]] = value[b * size : (b + 1) * size]


def fold_kernel(kinds, *refs):
    step = pl.program_id(0)
    ins = list(refs[: sum(count for _, count in kinds)])
    outs = list(refs[len(ins) :])
    for kind, count in kinds:
        total = ins.pop(0)[0].astype(F32)
        for _ in range(count - 1):
            total = total + ins.pop(0)[0].astype(F32)
        total = total.astype(BF16)
        if kind == "sum":
            outs.pop(0)[0] = total
            continue
        low, high = outs.pop(0), outs.pop(0)

        @pl.when(step < 2)
        def _():
            low[0] = total

        @pl.when(step >= 2)
        def _():
            high[0] = total


class Places:
    def __init__(self, n):
        self.n = n
        self.planes = EXPERTS
        self.group = n // EXPERTS
        self.chips = self.group // 2
        self.bits = self.chips.bit_length() - 1
        self.me = lax.axis_index("fsdp")
        self.core = self.me % 2
        self.chip = (self.me // 2) % self.chips
        self.plane = self.me // self.group

    def swap(self):
        return [(i, i ^ 1) for i in range(self.n)]

    def cross(self, step):
        moves = []
        for i in range(self.n):
            bit = step if i % 2 == 0 else self.bits - 1 - step
            moves.append((i, i ^ (2 << bit)))
        return moves

    def turn(self, k):
        return [(i, (i + k * self.group) % self.n) for i in range(self.n)]

    def order(self, core):
        plain = list(range(self.chips))
        back = [int(format(j, "0%db" % self.bits)[::-1], 2) for j in plain]
        rel = jnp.where(core == 0, jnp.array(plain, jnp.int32), jnp.array(back, jnp.int32))
        return jnp.bitwise_xor(self.chip, rel)

    def place(self, core):
        back = [int(format(j, "0%db" % self.bits)[::-1], 2) for j in range(self.chips)]
        rel = jnp.bitwise_xor(self.chip, jnp.arange(self.chips, dtype=jnp.int32))
        return jnp.where(core == 0, rel, jnp.array(back, jnp.int32)[rel])


def send(x, moves):
    return lax.ppermute(x, "fsdp", moves)


def sync(*arrays):
    return lax.optimization_barrier(arrays)


def pair_block(expert_in, expert_out, pos):
    rin, rout = expert_in.shape[0], expert_out.shape[0]
    win = expert_in.reshape(rin, 4, CHUNK)
    halves = [
        jnp.concatenate(
            [expert_out[h * rout // 2 : (h + 1) * rout // 2], win[:, 2 * h], win[:, 2 * h + 1]]
        )
        for h in range(2)
    ]
    first = pos.core == 0
    mine = jnp.where(first, halves[0], halves[1])
    got = send(jnp.where(first, halves[1], halves[0]), pos.swap())
    a = jnp.where(first, mine, got)
    b = jnp.where(first, got, mine)
    if rin % 16 == 0:
        return jnp.concatenate([a, b])
    cut = rout // 2
    return jnp.concatenate(
        [a[:cut], b[:cut], a[cut : cut + rin], b[cut : cut + rin], a[cut + rin :], b[cut + rin :]]
    )


def fold(*items):
    kinds = tuple((item[0], len(item) - 1) for item in items)
    args, in_specs, out_specs, out_shape, finals = [], [], [], [], []
    for kind, *arrays in items:
        a = arrays[0]
        height = a.size // 4 // CHUNK
        args += [x.reshape(4, height, CHUNK) for x in arrays]
        in_specs += [pl.BlockSpec((1, height, CHUNK), lambda i: (i, 0, 0))] * len(arrays)
        if kind == "sum":
            out_specs.append(pl.BlockSpec((1, height, CHUNK), lambda i: (i, 0, 0)))
            shapes = [(4, height, CHUNK)]
            finals.append(a.shape)
        else:
            out_specs.append(
                pl.BlockSpec((1, height, CHUNK), lambda i: (jnp.minimum(i, 1), 0, 0))
            )
            out_specs.append(
                pl.BlockSpec((1, height, CHUNK), lambda i: (jnp.maximum(i - 2, 0), 0, 0))
            )
            shapes = [(2, height, CHUNK)] * 2
            finals += [(a.shape[0] // 2,) + a.shape[1:]] * 2
        out_shape += [jax.ShapeDtypeStruct(shape, BF16) for shape in shapes]
    outs = pl.pallas_call(
        functools.partial(fold_kernel, kinds),
        name="fold",
        grid=(4,),
        in_specs=in_specs,
        out_specs=tuple(out_specs),
        out_shape=tuple(out_shape),
        compiler_params=room("fold"),
        cost_estimate=pl.CostEstimate(flops=1000, bytes_accessed=1000, transcendentals=0),
    )(*args)
    return [out.reshape(shape) for out, shape in zip(outs, finals)]


def add_low(a, b):
    return (a.astype(F32) + b.astype(F32)).astype(BF16)


def local(
    tokens,
    out_grad,
    key_valid,
    expert_ids,
    gate_logits,
    attn_norm_gain,
    attn_norm_bias,
    qkv_weight,
    query_bias,
    value_bias,
    attn_out_weight,
    attn_out_bias,
    moe_norm_gain,
    moe_norm_bias,
    expert_in,
    expert_in_bias,
    expert_out,
    expert_out_bias,
):
    n = lax.axis_size("fsdp")
    pos = Places(n)
    rows = tokens.shape[0]
    ext = rows + 2 * HALO
    width = qkv_weight.shape[0]
    total_rows = rows * n
    vmem = pl.BlockSpec(memory_space=pltpu.VMEM)
    smem = pl.BlockSpec(memory_space=pltpu.SMEM)
    far = pl.BlockSpec(memory_space=pl.ANY)

    def sds(shape, kind):
        return jax.ShapeDtypeStruct(shape, kind)

    def cost(flops, moved, trans=0):
        return pl.CostEstimate(flops=int(flops / 1000), bytes_accessed=int(moved / 1000), transcendentals=trans)

    chips = pos.chips
    if chips == 4:
        keep_place = pos.place(pos.core)
        give_place = pos.place(1 - pos.core)
    else:
        keep_place = give_place = jnp.arange(4, dtype=jnp.int32)
    experts = (pos.plane - jnp.array(SEQ, jnp.int32)) % 4
    tab = jnp.concatenate(
        [
            pos.core.reshape(1),
            experts,
            pos.order(pos.core),
            pos.order(1 - pos.core),
            keep_place,
            give_place,
        ]
    ).astype(jnp.int32)
    up = [(i, i + 1) for i in range(n - 1)]
    down = [(i + 1, i) for i in range(n - 1)]

    def halo(x):
        return send(x[rows - HALO :], up), send(x[:HALO], down)

    flat = jnp.concatenate(
        [
            attn_norm_gain,
            attn_norm_bias,
            query_bias,
            value_bias,
            attn_out_bias,
            moe_norm_gain,
            moe_norm_bias,
            jnp.zeros(((SMALL - 7) * width,), BF16),
        ]
    )

    def lines_of(x):
        lines = max(1, x.shape[0] // 128)
        at = pos.me * x.shape[0] % 128
        return lax.dynamic_update_slice_in_dim(jnp.zeros((lines * 128,), BF16), x, at, 0)

    lines = jnp.concatenate([lines_of(expert_in_bias), lines_of(expert_out_bias)])
    lines = jnp.pad(lines, (0, width * SMALL - lines.shape[0])).reshape(width, SMALL)
    first = pos.core == 0
    half_0 = jnp.concatenate([qkv_weight[:, : 2 * D], flat.reshape(SMALL, width).T], axis=1)
    half_1 = jnp.concatenate([qkv_weight[:, 2 * D :], attn_out_weight, lines], axis=1)
    mine = jnp.where(first, half_0, half_1)
    got = send(jnp.where(first, half_1, half_0), pos.swap())
    block = jnp.where(first, jnp.stack([mine, got]), jnp.stack([got, mine]))
    block = block.reshape(2 * width, HALF)
    pair = pair_block(expert_in, expert_out, pos)

    front = pair[None]
    for step in range(pos.bits - 1):
        got = send(front, pos.cross(step))
        if step < pos.bits - 2:
            front = jnp.concatenate([front, got], axis=0)
    turned = [send(block, pos.turn(k)) for k in range(1, 4)]
    *turned, pair, got = sync(*turned, pair, got)
    have = jnp.stack([block] + turned)[None]
    crossed = send(have, pos.cross(0))
    poscol, posrow, gate = pl.pallas_call(
        route_kernel,
        name="route",
        out_shape=(
            sds((rows, 8), jnp.int32),
            sds((8, rows), jnp.int32),
            sds((rows, TOP), F32),
        ),
        in_specs=[vmem] * 3,
        out_specs=(vmem,) * 3,
        compiler_params=room("fold"),
        cost_estimate=cost(4 * rows * rows * 128, 1 << 20),
    )(expert_ids, expert_ids.T, gate_logits)

    def dispatch(first_k, last_k):
        count = 2 * (last_k - first_k)
        *slots, sums = pl.pallas_call(
            functools.partial(dispatch_kernel, first_k),
            name="dispatch",
            out_shape=tuple([sds((CAP, D), BF16), sds((D, CAP), BF16)] * (count // 2))
            + (sds((EXPERTS, D), F32),),
            in_specs=[smem] + [vmem] * 4,
            out_specs=(far,) * count + (vmem,),
            scratch_shapes=[pltpu.VMEM((CAP, D), BF16), pltpu.VMEM((D, CAP), BF16)] * (count // 2)
            + [pltpu.SemaphoreType.DMA((count,))],
            compiler_params=room("dispatch"),
            cost_estimate=cost(count * rows * CAP * D, 4e6),
        )(tab, out_grad, posrow, expert_ids, gate)
        return slots, sums

    before, behind = halo(tokens)
    crossed, gate, poscol, posrow, before, behind = sync(
        crossed, gate, poscol, posrow, before, behind
    )
    piece = send(pair, pos.turn(SEQ[1]))
    slots, dbout = dispatch(0, 2)
    have = jnp.concatenate([have, crossed], axis=0)
    for step in range(1, pos.bits):
        crossed = send(have, pos.cross(step))
        if step < pos.bits - 1:
            have = jnp.concatenate([have, crossed], axis=0)
    slots_2, dbout_2 = dispatch(2, 4)
    first_row = pos.me * rows
    offset = first_row % IMG
    key_rows = first_row - HALO + jnp.arange(ext, dtype=jnp.int32)
    usable = lax.dynamic_slice_in_dim(jnp.pad(key_valid, (HALO, HALO)), first_row, ext)
    present = (key_rows >= 0) & (key_rows < total_rows)
    fill = jnp.where(usable == 1, 1.0, jnp.where(present, MASKED_SCORE, FAR_SCORE))
    fill = fill.astype(F32).reshape(ext, 1)
    have, crossed, piece, fill, dbout, dbout_2, *slots = sync(
        have, crossed, piece, fill, dbout, dbout_2, *slots, *slots_2
    )
    small = [have, crossed, send(have, pos.swap()), send(crossed, pos.swap())]
    planes = (pos.plane - jnp.arange(4, dtype=jnp.int32)) % 4
    if chips == 4:
        spots = [
            (planes[None, :] * 4 + pos.order(c)[:, None]).reshape(-1)
            for c in (pos.core, 1 - pos.core)
        ]
        small = [x.reshape(8, 2 * width, HALF) for x in small]
    else:
        spots = [jnp.arange(16, dtype=jnp.int32)] * 2
        canonical = []
        for data, c in ((small[:2], pos.core), (small[2:], 1 - pos.core)):
            data = jnp.concatenate(data).reshape(4 * chips, 2 * width, HALF)
            where = (pos.place(c)[None, :] * 4 + planes[:, None]).reshape(-1)
            data = jnp.take(data, where, axis=0).reshape(16, D // 16, HALF)
            canonical += [data[:8], data[8:]]
        small = canonical

    scalars = jnp.concatenate(
        [
            jnp.stack([HALO - offset, (rows + offset + IMG - 1) // IMG, pos.core]),
            jnp.where(first, spots[0], spots[1]),
            jnp.where(first, spots[1], spots[0]),
        ]
    ).astype(jnp.int32)
    def near_chips(piece):
        held = piece[None]
        for step in range(pos.bits - 2):
            held = jnp.concatenate([held, send(held, pos.cross(step))], axis=0)
        return held, send(held, pos.cross(pos.bits - 2))

    held = [jnp.concatenate([front, got])]
    half, got = near_chips(piece)
    flight = [
        send(held[0], pos.cross(pos.bits - 1)),
        send(held[0], pos.swap()),
        got,
        send(piece, pos.turn(1)),
    ]
    qkv, o_low, y1, a2, attn_sum, wqk, wvo, vecs, bin_all, bout_all = pl.pallas_call(
        functools.partial(attn_fwd_kernel, n),
        name="attn_fwd",
        out_shape=(
            sds((NIMG, SLOT, 3 * D), BF16),
            sds((rows, D), BF16),
            sds((rows, D), F32),
            sds((rows, D), BF16),
            sds((8, D), F32),
            sds((D, HALF), BF16),
            sds((D, HALF), BF16),
            sds((8, D), F32),
            sds((16, CHUNK), F32),
            sds((EXPERTS, D), F32),
        ),
        in_specs=[smem] + [vmem] * 8,
        out_specs=(far, far, far, vmem, vmem, far, far, vmem, vmem, vmem),
        scratch_shapes=[
            pltpu.VMEM((NIMG, SLOT, 3 * D), BF16),
            pltpu.VMEM((rows, D), BF16),
            pltpu.VMEM((rows, D), F32),
            pltpu.VMEM((D, HALF), BF16),
            pltpu.VMEM((D, HALF), BF16),
            pltpu.VMEM((ext, D), F32),
            pltpu.VMEM((ext, D), F32),
            pltpu.SemaphoreType.DMA((NIMG + 2 + 2 * (rows // 256),)),
        ],
        compiler_params=room("attn_fwd"),
        cost_estimate=cost(30e9, 12e6),
    )(scalars, before, tokens, behind, fill, *small)
    full, front, got, piece, a2, vecs = sync(*flight, a2, vecs)

    rin, rout = expert_in.shape[0], expert_out.shape[0]

    def by_chip(x, core):
        if chips == 4:
            return x
        more = chips // 4
        out = x[:, :256].reshape(4, 256, more, 2 * rout).transpose(0, 2, 1, 3)
        win = x[:, 256:].reshape(4, 2, more, 2 * rin, CHUNK).transpose(0, 2, 1, 3, 4)
        both = [out.reshape(chips, rout, CHUNK), win.reshape(chips, 4 * rin, CHUNK)]
        return jnp.take(jnp.concatenate(both, axis=1), pos.order(core), axis=0)

    def run_expert(k, full, front, back):
        return pl.pallas_call(
            functools.partial(expert_kernel, k, chips),
            name="expert_%d" % k,
            out_shape=(
                sds((CAP, D), BF16),
                sds((CAP, D), BF16),
                sds((16, CHUNK), F32),
                sds((4, CHUNK, CHUNK), BF16),
                sds((4, CHUNK, CHUNK), BF16),
            ),
            in_specs=[smem] + [vmem] * 10,
            out_specs=(vmem,) * 5,
            scratch_shapes=[
                pltpu.VMEM((4, D, CHUNK), BF16),
                pltpu.VMEM((FF, D), BF16),
                pltpu.VMEM((CAP, D), BF16),
                pltpu.VMEM((D, CAP), BF16),
                pltpu.VMEM((4, CAP, CHUNK), BF16),
                pltpu.VMEM((4, CAP, CHUNK), BF16),
            ],
            compiler_params=room("expert"),
            cost_estimate=cost(10e9, 14e6),
        )(
            tab,
            a2,
            slots[2 * k],
            slots[2 * k + 1],
            posrow,
            bin_all,
            bout_all,
            held[k],
            full,
            front,
            back,
        )

    def first_sum(k, got):
        return ("halves", by_chip(results[k][3], pos.core), got)

    def give_of(k, *others):
        return send(sync(by_chip(results[k][4], 1 - pos.core), *others)[0], pos.swap())

    top = pos.bits - 1

    def send_top(x):
        return send(x, pos.cross(top))

    def send_low(keep, x):
        for step in reversed(range(1, top)):
            total = add_low(keep, send(x, pos.cross(step)))
            keep, x = total[: total.shape[0] // 2], total[total.shape[0] // 2 :]
        return keep, send(x, pos.cross(0))

    results = []
    back = send(full, pos.swap())
    held.append(jnp.concatenate([half, got]))
    half, got = near_chips(piece)
    flight = [
        send(held[1], pos.cross(top)),
        send(held[1], pos.swap()),
        got,
        send(pair, pos.turn(SEQ[3])),
    ]
    done = sync(*run_expert(0, full, front, back), *flight, a2)
    results.append(done[:5])
    full, front, got, piece, a2 = done[5:]
    back = send(full, pos.swap())

    held.append(jnp.concatenate([half, got]))
    half, got = near_chips(piece)
    flight = [send(held[2], pos.cross(top)), send(held[2], pos.swap()), got, give_of(0, back)]
    done = sync(*run_expert(1, full, front, back), *flight, a2)
    results.append(done[:5])
    full, front, got, swap_0, a2 = done[5:]
    back = send(full, pos.swap())

    held.append(jnp.concatenate([half, got]))
    flight = [send(held[3], pos.cross(top)), send(held[3], pos.swap()), give_of(1, back)]
    done = sync(*run_expert(2, full, front, back), *flight, a2)
    results.append(done[:5])
    full, front, swap_1, a2 = done[5:]
    back = send(full, pos.swap())

    keep_1, give_1 = fold(first_sum(1, swap_1))
    flight = [send_top(give_1), give_of(2, back)]
    done = sync(*run_expert(3, full, front, back), *flight, a2)
    results.append(done[:5])
    top_1, swap_2, a2 = done[5:]

    keep_1, give_1, keep_2, give_2 = fold(("halves", keep_1, top_1), first_sum(2, swap_2))
    keep_1, got = send_low(keep_1, give_1)
    flight = [got, send_top(give_2), give_of(3)]
    routing = (tab, poscol, expert_ids, gate, out_grad)
    middle = pl.pallas_call(
        middle_kernel,
        name="middle",
        out_shape=(
            sds((rows, D), BF16),
            sds((rows, D), F32),
            sds((rows, D), BF16),
            sds((D, D), BF16),
            sds((rows, TOP), F32),
            sds((8, D), F32),
            sds((8, D), F32),
        ),
        in_specs=[smem] + [vmem] * 17,
        out_specs=(vmem,) * 7,
        scratch_shapes=[pltpu.VMEM((rows, D), F32), pltpu.VMEM((rows, D), F32)],
        compiler_params=room("middle"),
        cost_estimate=cost(9 * 2 * rows * CAP * D, 16e6),
    )(
        *routing,
        *(r[0] for r in results),
        *(r[1] for r in results),
        y1,
        o_low,
        fill,
        vecs,
        attn_sum,
    )
    done = sync(*middle, *flight)
    block_out, dy1, gattn, dwo, logits_grad, sums2, stats, low_1, top_2, swap_3 = done

    sum_1, keep_2, give_2, keep_3, give_3 = fold(
        ("sum", keep_1, low_1), ("halves", keep_2, top_2), first_sum(3, swap_3)
    )
    keep_2, got = send_low(keep_2, give_2)

    def home(k, x):
        return send(x, pos.turn(4 - SEQ[k]))

    flight = [got, send_top(give_3), home(1, sum_1[0]), *halo(gattn)]
    early = pl.pallas_call(
        attn_bwd_kernel,
        name="attn_bwd_early",
        out_shape=sds((4, SLOT, 3 * D), BF16),
        in_specs=[smem] + [vmem] * 4,
        out_specs=vmem,
        scratch_shapes=[pltpu.VMEM((ext, D), F32)],
        compiler_params=room("early"),
        cost_estimate=cost(30e9, 8e6),
    )(scalars, fill, qkv, gattn, wvo)
    early, low_2, top_3, home_1, before, behind = sync(early, *flight)

    sum_2, keep_3, give_3, keep_0, give_0 = fold(
        ("sum", keep_2, low_2), ("halves", keep_3, top_3), first_sum(0, swap_0)
    )
    keep_3, got = send_low(keep_3, give_3)
    flight = [got, send(sum_2, pos.turn(1)), send_top(give_0)]
    tokens_grad, rest_keep, rest_give = pl.pallas_call(
        functools.partial(attn_end_kernel, n, 5 + 2 * chips),
        name="attn_bwd_late",
        out_shape=(
            sds((rows, D), F32),
            sds((EXPERTS, 4, D // 16, HALF), BF16),
            sds((EXPERTS, 4, D // 16, HALF), BF16),
        ),
        in_specs=[smem] * 2 + [vmem] * 20,
        out_specs=(vmem,) * 3,
        scratch_shapes=[
            pltpu.VMEM((ext, D), F32),
            pltpu.VMEM((ext, 3 * D), F32),
            pltpu.VMEM((rows, D), BF16),
            pltpu.VMEM((rows, 3 * D), BF16),
            pltpu.VMEM((128, D), F32),
            pltpu.VMEM((D, SMALL), F32),
        ],
        compiler_params=room("late"),
        cost_estimate=cost(30e9, 16e6),
    )(
        scalars,
        tab,
        tokens,
        fill,
        qkv,
        before,
        gattn,
        behind,
        dy1,
        wqk,
        wvo,
        vecs,
        early,
        dwo,
        sums2,
        stats,
        *(r[2] for r in results),
        dbout,
        dbout_2,
    )

    tokens_grad, rest_keep, rest_give, low_3, from_2, top_0 = sync(
        tokens_grad, rest_keep, rest_give, *flight
    )

    def by_block(x, core):
        if chips == 4:
            return x
        return jnp.take(x.reshape(EXPERTS, chips, 2 * width, HALF), pos.order(core), axis=1)

    sum_3, keep_0, give_0 = fold(
        ("sum", keep_3, low_3, from_2), ("halves", keep_0, top_0)
    )
    home_3 = home(3, sum_3[0])
    rest = add_low(
        by_block(rest_keep, pos.core), send(by_block(rest_give, 1 - pos.core), pos.swap())
    )

    def cross(x, step, *others):
        x = x.reshape((EXPERTS, 2, -1) + x.shape[2:])
        swapped, *others = sync(send(x[:, 1], pos.cross(step)), *others)
        return [add_low(x[:, 0], swapped)] + others

    (rest,) = cross(rest, top)
    for step in reversed(range(1, top)):
        (rest,) = cross(rest, step)
    rest, home_3, give_0 = cross(rest, 0, home_3, give_0)
    keep_0, got = send_low(keep_0, give_0)
    rest = rest[:, 0]

    def block_for(k):
        return lax.dynamic_index_in_dim(rest, (pos.plane + k) % 4, 0, keepdims=False)

    others = [send(block_for(k), pos.turn(k)) for k in range(1, 4)]
    *others, got = sync(*others, got)
    total = keep_0[0].astype(F32) + got[0].astype(F32)
    for got in (home_1, home_3):
        total = total + got.astype(F32)

    def own_halves(pair, axis):
        mine = lax.dynamic_index_in_dim(pair, pos.core, 0, keepdims=False)
        got = send(lax.dynamic_index_in_dim(pair, 1 - pos.core, 0, keepdims=False), pos.swap())
        return jnp.where(
            pos.core == 0,
            jnp.concatenate([mine, got], axis=axis),
            jnp.concatenate([got, mine], axis=axis),
        )

    out_sum = total[:rout].reshape(256, 2, rout).transpose(1, 0, 2)
    expert_out_grad = own_halves(out_sum, 0).T
    in_sum = total[rout:].reshape(2, 2, rin, CHUNK).transpose(1, 2, 0, 3)
    expert_in_grad = own_halves(in_sum.reshape(2, rin, 2 * CHUNK), 1)

    *others, expert_out_grad, expert_in_grad = sync(*others, expert_out_grad, expert_in_grad)
    rest = block_for(0).astype(F32)
    for got in others:
        rest = rest + got.astype(F32)

    rest = own_halves(rest.reshape(2, width, HALF), 1)
    tail = rest[:, 2 * D : HALF]
    bias = rest[:, HALF + 2 * D :].reshape(-1)
    count = jnp.sum((key_valid == 1).astype(F32))
    block_stats = jnp.sqrt(tail[0, 8:11] / (count * D))
    in_size, out_size = expert_in_bias.shape[0], expert_out_bias.shape[0]
    lines = max(1, in_size // 128)

    def bias_part(line, size):
        return lax.dynamic_slice_in_dim(bias, line * 128 + pos.me * size % 128, size)

    return (
        block_out,
        tokens_grad,
        logits_grad,
        tail[:, 0],
        tail[:, 1],
        jnp.concatenate([rest[:, : 2 * D], rest[:, HALF : HALF + D]], axis=1),
        tail[:, 2],
        tail[:, 3],
        rest[:, HALF + D : HALF + 2 * D],
        tail[:, 4],
        tail[:, 5],
        tail[:, 6],
        expert_in_grad,
        bias_part(0, in_size),
        expert_out_grad,
        bias_part(lines, out_size),
        block_stats,
    )


def solution(mesh):
    row = P("fsdp", None)
    vec = P("fsdp")
    return jax.shard_map(
        local,
        mesh=mesh,
        in_specs=(
            row,
            row,
            P(),
            row,
            row,
            vec,
            vec,
            row,
            vec,
            vec,
            row,
            vec,
            vec,
            vec,
            row,
            vec,
            row,
            vec,
        ),
        out_specs=(
            row,
            row,
            row,
            vec,
            vec,
            row,
            vec,
            vec,
            row,
            vec,
            vec,
            vec,
            row,
            vec,
            row,
            vec,
            P(),
        ),
        check_vma=False,
    )
```

```python
import functools

import jax
import jax.numpy as jnp
from jax import lax
from jax.experimental import pallas as pl
from jax.experimental.pallas import tpu as pltpu
from jax.sharding import PartitionSpec as P

D = 512
FF = 2048
HEAD_DIM = 64
EXPERTS = 4
TOP = 2
IMG = 200
CAP = 640
HALO = 200
SLOT = 208
NIMG = 7
CHUNK = 512
SMALL = 128
HALF = 1024 + SMALL

SEQ = (0, 1, 2, 3)

EPS = 1e-06
MASKED_SCORE = -1000000000.0
FAR_SCORE = -1e30
F32 = jnp.float32
BF16 = jnp.bfloat16
VMEM_MIB = {"attn_fwd": 40, "dispatch": 40, "expert": 22, "middle": 18, "early": 8, "late": 23, "fold": 14}


def room(name):
    return pltpu.CompilerParams(vmem_limit_bytes=VMEM_MIB[name] * 1024 * 1024)


def dot_nn(a, b):
    return lax.dot_general(a, b, (((1,), (0,)), ((), ())), preferred_element_type=F32)


def dot_nt(a, b):
    return lax.dot_general(a, b, (((1,), (1,)), ((), ())), preferred_element_type=F32)


def dot_tn(a, b):
    return lax.dot_general(a, b, (((0,), (0,)), ((), ())), preferred_element_type=F32)


def norm_parts(values):
    average = jnp.mean(values, axis=-1, keepdims=True)
    centered = values - average
    inverse = lax.rsqrt(jnp.mean(centered * centered, axis=-1, keepdims=True) + EPS)
    return centered * inverse, inverse


def norm_back(upstream, normed, inverse, gain):
    scaled = upstream * gain
    inner = (
        scaled
        - jnp.mean(scaled, axis=-1, keepdims=True)
        - normed * jnp.mean(scaled * normed, axis=-1, keepdims=True)
    )
    return inverse * inner


def route_kernel(ids_ref, idst_ref, logits_ref, poscol_ref, posrow_ref, gate_ref):
    rows = ids_ref.shape[0]
    lane = lax.broadcasted_iota(jnp.int32, (rows, 128), 1)
    chosen = (ids_ref[:, 0:1] == lane) | (ids_ref[:, 1:2] == lane)
    r0 = lax.broadcasted_iota(jnp.int32, (rows, rows), 0)
    r1 = lax.broadcasted_iota(jnp.int32, (rows, rows), 1)
    lower = jnp.where(r1 < r0, 1.0, 0.0).astype(BF16)
    upper = jnp.where(r0 < r1, 1.0, 0.0).astype(BF16)
    count = dot_nn(lower, jnp.where(chosen, 1.0, 0.0).astype(BF16))
    pos = jnp.where(chosen, count, -1.0)
    poscol_ref[...] = pos[:, :8].astype(jnp.int32)
    sub = lax.broadcasted_iota(jnp.int32, (16, rows), 0)
    chosen_t = (idst_ref[0:1, :] == sub) | (idst_ref[1:2, :] == sub)
    count_t = dot_nn(jnp.where(chosen_t, 1.0, 0.0).astype(BF16), upper)
    posrow_ref[...] = jnp.where(chosen_t, count_t, -1.0)[:8].astype(jnp.int32)
    a = logits_ref[:, 0:1]
    b = logits_ref[:, 1:2]
    top = jnp.maximum(a, b)
    ea = jnp.exp(a - top)
    eb = jnp.exp(b - top)
    total = ea + eb
    which = lax.broadcasted_iota(jnp.int32, (rows, 2), 1)
    gate_ref[...] = jnp.where(which == 0, ea / total, eb / total)


def image_fill(fill_ref, st):
    fill = fill_ref[pl.ds(st, SLOT), :]
    row = lax.broadcasted_iota(jnp.int32, (SLOT, 1), 0)
    return jnp.where(row < IMG, fill, FAR_SCORE)


def lane_halves():
    lane = lax.broadcasted_iota(jnp.int32, (1, 128), 1)
    low = jnp.where(lane < HEAD_DIM, 1.0, 0.0).astype(BF16)
    return low, (1.0 - low.astype(F32)).astype(BF16)


def stack_heads(x, masks):
    return jnp.concatenate([x * mask for mask in masks], axis=0)


def pair_dot(stacked, other):
    both = dot_nt(stacked, other)
    return both[:SLOT], both[SLOT:]


def softmax_t(scores, fill):
    scores = jnp.where(fill > 0, scores, fill)
    raised = jnp.exp(scores - jnp.max(scores, axis=0, keepdims=True))
    return raised * (1.0 / jnp.sum(raised, axis=0, keepdims=True))


def bias_lines(devices):
    lines = max(1, EXPERTS * FF // devices // 128)
    for d in range(devices):
        for i in range(lines):
            yield d, i, 0, EXPERTS * FF // devices * d // 128 + i
        yield d, lines, 1, EXPERTS * D // devices * d // 128


def halo_rows(out, before_ref, x_ref, after_ref):
    rows = x_ref.shape[0]
    out[0:HALO, :] = before_ref[...].astype(F32)
    out[HALO : HALO + rows, :] = x_ref[...].astype(F32)
    out[HALO + rows :, :] = after_ref[...].astype(F32)


def attn_fwd_kernel(
    devices,
    sc,
    before_ref,
    x_ref,
    after_ref,
    fill_ref,
    mine_0,
    mine_1,
    other_0,
    other_1,
    qkv_hbm,
    o_hbm,
    y1_hbm,
    a2_ref,
    stat_ref,
    wqk_hbm,
    wvo_hbm,
    vecs,
    bin_ref,
    bout_ref,
    qkv_ref,
    o_ref,
    y1_ref,
    wqk,
    wvo,
    xs,
    os_,
    sems,
):
    rows = a2_ref.shape[0]
    size = D // 16
    mine, other = (mine_0, mine_1), (other_0, other_1)
    for core, refs in ((0, (mine, other)), (1, (other, mine))):

        @pl.when(sc[2] == core)
        def _():
            for at in range(16):
                for ref, out, base in ((refs[0], wqk, 3), (refs[1], wvo, 19)):
                    row = pl.multiple_of(sc[base + at] * size, size)
                    out[pl.ds(row, size), :] = ref[at // 8][at % 8]

    weights_out = [
        pltpu.make_async_copy(wqk, wqk_hbm, sems.at[NIMG]),
        pltpu.make_async_copy(wvo, wvo_hbm, sems.at[NIMG + 1]),
    ]
    for copy in weights_out:
        copy.start()
    vecs[...] = wqk[:, 2 * D :].astype(F32).T[:8]
    bias = wvo[:, 2 * D :].astype(F32)
    bin_ref[...] = jnp.zeros_like(bin_ref)
    bout_ref[...] = jnp.zeros_like(bout_ref)
    for d, line, out, at in bias_lines(devices):
        out = (bin_ref, bout_ref)[out]
        row = D // devices * d + line
        here = (slice(at // 4, at // 4 + 1), slice(at % 4 * 128, at % 4 * 128 + 128))
        out[here] += bias[row : row + 1, :]
    halo_rows(xs, before_ref, x_ref, after_ref)
    masks = lane_halves()

    def image(j, carry):
        st = pl.multiple_of(sc[0] + IMG * j, 8)
        normed, _ = norm_parts(xs[pl.ds(st, SLOT), :])
        a1 = (normed * vecs[0:1, :] + vecs[1:2, :]).astype(BF16)
        qk = dot_nn(a1, wqk[:, : 2 * D])
        q = (qk[:, :D] + vecs[2:3, :]).astype(BF16)
        k = qk[:, D:].astype(BF16)
        v = (dot_nn(a1, wvo[:, :D]) + vecs[3:4, :]).astype(BF16)
        qkv_ref[j, :, 0:D] = q
        qkv_ref[j, :, D : 2 * D] = k
        qkv_ref[j, :, 2 * D : 3 * D] = v
        fill = image_fill(fill_ref, st)
        q8 = q * jnp.asarray(HEAD_DIM**-0.5, BF16)
        for hp in range(4):
            cols = slice(hp * 128, hp * 128 + 128)
            probs = [
                softmax_t(scores, fill).astype(BF16)
                for scores in pair_dot(stack_heads(k[:, cols], masks), q8[:, cols])
            ]
            probs = jnp.concatenate(probs, axis=0)
            os_[pl.ds(st, SLOT), cols] = dot_tn(probs, stack_heads(v[:, cols], masks))
        pltpu.make_async_copy(qkv_ref.at[j], qkv_hbm.at[j], sems.at[j]).start()
        return carry

    def image_out(j, carry):
        pltpu.make_async_copy(qkv_ref.at[j], qkv_hbm.at[j], sems.at[j]).wait()
        return carry

    lax.fori_loop(0, sc[1], image, 0)
    rows_out = []
    total = jnp.zeros((1, D), F32)
    for i in range(rows // 256):
        own = slice(HALO + 256 * i, HALO + 256 * (i + 1))
        here = slice(256 * i, 256 * (i + 1))
        o_low = os_[own, :].astype(BF16)
        o_ref[here, :] = o_low
        attn = dot_nn(o_low, wvo[:, D : 2 * D]) + vecs[4:5, :]
        valid = jnp.where(fill_ref[own, :] > 0, 1.0, 0.0)
        total = total + jnp.sum(valid * attn * attn, axis=0, keepdims=True)
        y1 = xs[own, :] + attn
        y1_ref[here, :] = y1
        normed, _ = norm_parts(y1)
        a2_ref[here, :] = (normed * vecs[5:6, :] + vecs[6:7, :]).astype(BF16)
        at = NIMG + 2 + 2 * i
        rows_out.append(pltpu.make_async_copy(o_ref.at[here], o_hbm.at[here], sems.at[at]))
        rows_out.append(pltpu.make_async_copy(y1_ref.at[here], y1_hbm.at[here], sems.at[at + 1]))
        rows_out[-2].start()
        rows_out[-1].start()
    stat_ref[...] = jnp.broadcast_to(total, (8, D))
    lax.fori_loop(0, sc[1], image_out, 0)
    for copy in weights_out + rows_out:
        copy.wait()


def gelu_both(x):
    square = x * x
    t = jnp.tanh(0.7978845608028654 * (x + 0.044715 * (x * square)))
    half = 0.5 * (1.0 + t)
    slope = half + 0.5 * x * (1.0 - t * t) * (
        0.7978845608028654 * (1.0 + (3.0 * 0.044715) * square)
    )
    return x * half, slope


def gate_of(e, ids_ref, gate_ref):
    return jnp.sum(jnp.where(ids_ref[...] == e, gate_ref[...], 0.0), axis=1, keepdims=True)


def dispatch_kernel(first, tab, g_ref, posrow, ids_ref, gate_ref, *outs):
    rows = g_ref.shape[0]
    count = (len(outs) - 2) // 2
    sums_ref = outs[count]
    *held, sems = outs[count + 1 :]
    copies = [pltpu.make_async_copy(held[i], outs[i], sems.at[i]) for i in range(count)]
    g = g_ref[...].astype(F32)
    slot = lax.broadcasted_iota(jnp.int32, (CAP, rows), 0)
    sums_ref[...] = jnp.zeros_like(sums_ref)
    for k in range(count // 2):
        e = tab[1 + first + k]
        pick = jnp.where(posrow[pl.ds(e, 1), :] == slot, 1.0, 0.0).astype(BF16)
        gy = (gate_of(e, ids_ref, gate_ref) * g).astype(BF16)
        gslot = dot_nn(pick, gy)
        sums_ref[pl.ds(e, 1), :] = jnp.sum(gslot, axis=0, keepdims=True)
        gslot = gslot.astype(BF16)
        held[2 * k][...] = gslot
        copies[2 * k].start()
        held[2 * k + 1][...] = gslot.T
        copies[2 * k + 1].start()
    for copy in copies:
        copy.wait()


def expert_kernel(
    item,
    chips,
    tab,
    a2_ref,
    gg,
    gt,
    posrow,
    bin_ref,
    bout_ref,
    mine0,
    mine1,
    other0,
    other1,
    y_ref,
    da_ref,
    dbin_ref,
    keep,
    give,
    win,
    wout,
    xg,
    xt,
    hall,
    dall,
):
    core = tab[0]
    e = tab[1 + item]
    half_chips = chips // 2
    rows = a2_ref.shape[0]
    span = D // chips
    part = CHUNK * 4 // chips // 4
    orders = 5
    places = orders + 2 * chips

    def sort_weights():
        for half_at, pieces in ((0, (mine0, mine1)), (1, (other0, other1))):
            half = core if half_at == 0 else 1 - core
            for number, piece in enumerate(pieces):
                for j in range(half_chips):
                    chip = tab[orders + half_at * chips + number * half_chips + j]
                    for c in range(2):
                        at = pl.multiple_of((chip * 4 + 2 * c + half) * part, part)
                        here = c * 2 * part if span % 32 == 0 else c * part
                        wout[pl.ds(at, part), :] = piece[j, here : here + part, :]
                    for i in range(2):
                        out = win.at[2 * half + i]
                        if span % 32 == 0:
                            for c in range(2):
                                at = pl.multiple_of(chip * span + c * span // 2, span // 2)
                                here = c * 2 * part + part + i * span // 2
                                out[pl.ds(at, span // 2), :] = piece[j, here : here + span // 2, :]
                        else:
                            at = pl.multiple_of(chip * span, span)
                            here = 2 * part + i * span
                            out[pl.ds(at, span), :] = piece[j, here : here + span, :]

    slot = lax.broadcasted_iota(jnp.int32, (CAP, rows), 0)
    pick = jnp.where(posrow[pl.ds(e, 1), :] == slot, 1.0, 0.0).astype(BF16)
    x = dot_nn(pick, a2_ref[...]).astype(BF16)
    xg[...] = x
    xt[...] = x.T
    dbin_ref[...] = jnp.zeros_like(dbin_ref)
    sort_weights()

    for c in range(4):
        row = e * 4 + c
        w1 = win[c]
        w2 = wout[CHUNK * c : CHUNK * (c + 1), :]
        total = jnp.zeros((1, CHUNK), F32)
        for r in range(2):
            here = slice(r * (CAP // 2), (r + 1) * (CAP // 2))
            pre = dot_nn(xg[here, :], w1) + bin_ref[pl.ds(row, 1), :]
            hidden, slope = gelu_both(pre)
            hall[c, here, :] = hidden.astype(BF16)
            dpre = (dot_nt(gg[here, :], w2) * slope).astype(BF16)
            dall[c, here, :] = dpre
            total = total + jnp.sum(dpre.astype(F32), axis=0, keepdims=True)
        dbin_ref[pl.ds(row, 1), :] = total

    mine = pl.multiple_of(core * 256, 256)
    theirs = pl.multiple_of((1 - core) * 256, 256)
    for i in range(2):
        for first, where, at in ((1 - core, give, places + 4), (core, keep, places)):
            dwin = dot_nn(xt[...], dall[2 * first + i]).astype(BF16)
            for b in range(4):
                where[tab[at + b], 256 + 128 * i : 384 + 128 * i, :] = dwin[128 * b : 128 * (b + 1)]
    for c in range(4):
        give[tab[places + 4 + c], 0:256, :] = dot_nn(gt[pl.ds(theirs, 256), :], hall[c]).astype(BF16)
        keep[tab[places + c], 0:256, :] = dot_nn(gt[pl.ds(mine, 256), :], hall[c]).astype(BF16)

    hidden = jnp.concatenate([hall[c] for c in range(4)], axis=1)
    y = dot_nn(hidden, wout[...]) + bout_ref[pl.ds(e, 1), :]
    y_ref[...] = y.astype(BF16)
    da = None
    for c in range(4):
        more = dot_nt(dall[c], win[c])
        da = more if da is None else da + more
    da_ref[...] = da.astype(BF16)


def combine(e, poscol, ids_ref, gate_ref, g_ref, y, da):
    rows = poscol.shape[0]
    lane = lax.broadcasted_iota(jnp.int32, (rows, 8), 1)
    pos = jnp.sum(jnp.where(lane == e, poscol[...], 0), axis=1, keepdims=True)
    slot = lax.broadcasted_iota(jnp.int32, (rows, CAP), 1)
    place = jnp.where(pos == slot, 1.0, 0.0).astype(BF16)
    yrow = dot_nn(place, y)
    pull = jnp.sum(g_ref[...].astype(F32) * yrow, axis=1, keepdims=True)
    dgate = jnp.where(ids_ref[...] == e, pull, 0.0)
    return gate_of(e, ids_ref, gate_ref) * yrow, dot_nn(place, da), dgate


def middle_kernel(
    tab,
    poscol,
    ids_ref,
    gate_ref,
    g_ref,
    s0,
    s1,
    s2,
    s3,
    t0,
    t1,
    t2,
    t3,
    y1_ref,
    o_ref,
    fill_ref,
    vecs,
    attn_sum,
    out_ref,
    dy1_ref,
    gattn_ref,
    dwo_ref,
    lgrad_ref,
    sums_ref,
    stats_ref,
    moe_ref,
    da2_ref,
):
    shared = (poscol, ids_ref, gate_ref, g_ref)
    dgate = 0.0
    for k, (y, da) in enumerate(((s0, t0), (s1, t1), (s2, t2), (s3, t3))):
        moe, da2, pull = combine(tab[1 + k], *shared, y[...], da[...])
        dgate = dgate + pull
        if k == 0:
            moe_ref[...] = moe
            da2_ref[...] = da2
        else:
            moe_ref[...] += moe
            da2_ref[...] += da2
    rows = y1_ref.shape[0]
    sums = [jnp.zeros((1, D), F32) for _ in range(5)]
    for i in range(rows // 256):
        here = slice(256 * i, 256 * (i + 1))
        y1 = y1_ref[here, :]
        moe = moe_ref[here, :]
        value = y1 + moe
        out_ref[here, :] = value.astype(BF16)
        valid = jnp.where(fill_ref[HALO + 256 * i : HALO + 256 * (i + 1), :] > 0, 1.0, 0.0)
        normed, inverse = norm_parts(y1)
        upstream = da2_ref[here, :]
        dy1 = g_ref[here, :].astype(F32) + norm_back(upstream, normed, inverse, vecs[5:6, :])
        dy1_ref[here, :] = dy1
        low = dy1.astype(BF16)
        gattn_ref[here, :] = low
        parts = (
            upstream * normed,
            upstream,
            low.astype(F32),
            valid * value * value,
            valid * moe * moe,
        )
        sums = [s + jnp.sum(p, axis=0, keepdims=True) for s, p in zip(sums, parts)]
    sums_ref[...] = jnp.zeros_like(sums_ref)
    stats_ref[...] = jnp.zeros_like(stats_ref)
    for i, s in ((4, sums[2]), (5, sums[0]), (6, sums[1])):
        sums_ref[i : i + 1, :] = s
    for i, s in enumerate((sums[3], attn_sum[0:1, :], sums[4])):
        stats_ref[i : i + 1, :] = jnp.broadcast_to(jnp.sum(s, axis=1, keepdims=True), (1, D))
    dwo_ref[...] = dot_tn(o_ref[...], gattn_ref[...]).astype(BF16)
    gate = gate_ref[...]
    lgrad_ref[...] = gate * (dgate - jnp.sum(gate * dgate, axis=1, keepdims=True))


def image_back(j, sc, fill_ref, qkv_ref, gs, wo, masks):
    st = pl.multiple_of(sc[0] + IMG * j, 8)
    row = lax.broadcasted_iota(jnp.int32, (SLOT, 1), 0)
    upstream = jnp.where(row < IMG, gs[pl.ds(st, SLOT), :], 0.0).astype(BF16)
    go = dot_nt(upstream, wo).astype(BF16)
    q8 = qkv_ref[j, :, 0:D] * jnp.asarray(HEAD_DIM**-0.5, BF16)
    k = qkv_ref[j, :, D : 2 * D]
    v = qkv_ref[j, :, 2 * D : 3 * D]
    fill = image_fill(fill_ref, st)
    for hp in range(4):
        cols = slice(hp * 128, hp * 128 + 128)
        keys = stack_heads(k[:, cols], masks)
        scores = pair_dot(keys, q8[:, cols])
        pulls = pair_dot(stack_heads(v[:, cols], masks), go[:, cols])
        probs = [softmax_t(x, fill) for x in scores]
        ds = []
        for prob, pull in zip(probs, pulls):
            centre = jnp.sum(prob * pull, axis=0, keepdims=True)
            ds.append(jnp.where(fill > 0, prob * (pull - centre), 0.0).astype(BF16))
        gq = dot_tn(jnp.concatenate(ds, axis=0), keys)
        gk = gv = 0.0
        for mask, grad, prob in zip(masks, ds, probs):
            gk = gk + dot_nn(grad, q8[:, cols] * mask)
            gv = gv + dot_nn(prob.astype(BF16), go[:, cols] * mask)
        yield st, hp * 128, gq * HEAD_DIM**-0.5, gk, gv


def attn_bwd_kernel(sc, fill_ref, qkv_ref, gattn_ref, wvo, grad_ref, gs):
    rows = gattn_ref.shape[0]
    gs[HALO : HALO + rows, :] = gattn_ref[...].astype(F32)
    gs[HALO + rows : HALO + rows + 8, :] = jnp.zeros((8, D), F32)
    masks = lane_halves()
    wo = wvo[:, D : 2 * D]

    def image(j, carry):
        for _, at, *grads in image_back(j + 1, sc, fill_ref, qkv_ref, gs, wo, masks):
            for i, grad in enumerate(grads):
                grad_ref[j, :, i * D + at : i * D + at + 128] = grad.astype(BF16)
        return carry

    lax.fori_loop(0, 4, image, 0)


def attn_end_kernel(
    devices,
    places,
    sc,
    tab,
    x_ref,
    fill_ref,
    qkv_ref,
    before_ref,
    gattn_ref,
    after_ref,
    dy1_ref,
    wqk,
    wvo,
    vecs,
    early_ref,
    dwo_ref,
    sums2_ref,
    stats_ref,
    b0,
    b1,
    b2,
    b3,
    dbout_ref,
    dbout_2_ref,
    dtok_ref,
    keep_ref,
    give_ref,
    gs,
    acc,
    a1s,
    gq_s,
    cols,
    bias,
):
    rows = dy1_ref.shape[0]
    halo_rows(gs, before_ref, gattn_ref, after_ref)
    masks = lane_halves()
    wo = wvo[:, D : 2 * D]

    def image(j, carry):
        for st, at, *grads in image_back(j, sc, fill_ref, qkv_ref, gs, wo, masks):
            for i, grad in enumerate(grads):
                acc[pl.ds(st, SLOT), i * D + at : i * D + at + 128] = grad
        return carry

    image(0, 0)
    for j in range(4):
        st = pl.multiple_of(sc[0] + IMG * (j + 1), 8)
        acc[pl.ds(st, SLOT), :] = early_ref[j].astype(F32)
    lax.fori_loop(5, sc[1], image, 0)
    sums = [jnp.zeros((1, D), F32) for _ in range(4)]
    for i in range(rows // 256):
        own = slice(HALO + 256 * i, HALO + 256 * (i + 1))
        here = slice(256 * i, 256 * (i + 1))
        low = acc[own, :].astype(BF16)
        gq_s[here, :] = low
        normed, inverse = norm_parts(x_ref[here, :].astype(F32))
        a1s[here, :] = (normed * vecs[0:1, :] + vecs[1:2, :]).astype(BF16)
        upstream = dot_nt(low[:, : 2 * D], wqk[:, : 2 * D]) + dot_nt(low[:, 2 * D :], wvo[:, :D])
        dtok_ref[here, :] = dy1_ref[here, :] + norm_back(upstream, normed, inverse, vecs[0:1, :])
        parts = (
            upstream * normed,
            upstream,
            low[:, :D].astype(F32),
            low[:, 2 * D :].astype(F32),
        )
        sums = [s + jnp.sum(p, axis=0, keepdims=True) for s, p in zip(sums, parts)]
    cols[...] = jnp.zeros_like(cols)
    for i, s in enumerate(sums):
        cols[i : i + 1, :] = s
    cols[4:8, :] = sums2_ref[4:8, :]
    cols[8:16, :] = stats_ref[...]
    small = cols[...].T.astype(BF16)
    dbin = b0[...] + b1[...] + b2[...] + b3[...]
    dbout = dbout_ref[...] + dbout_2_ref[...]
    bias[...] = jnp.zeros_like(bias)
    for d, line, source, at in bias_lines(devices):
        row = D // devices * d + line
        bias[row : row + 1, :] = (dbin, dbout)[source][
            at // 4 : at // 4 + 1, at % 4 * 128 : at % 4 * 128 + 128
        ]
    a1 = a1s[...]
    dqk = dot_tn(a1, gq_s[:, : 2 * D]).astype(BF16)
    dv = dot_tn(a1, gq_s[:, 2 * D :]).astype(BF16)
    first = jnp.concatenate([dqk, small], axis=1)
    second = jnp.concatenate([dv, dwo_ref[...], bias[...].astype(BF16)], axis=1)
    size = D // 16
    for ref, at, half in ((keep_ref, places, tab[0]), (give_ref, places + 4, 1 - tab[0])):
        for value, own in ((first, 0), (second, 1)):

            @pl.when(half == own)
            def _():
                for b in range(16):
                    ref[b // 4, tab[at + b % 4]] = value[b * size : (b + 1) * size]


def fold_kernel(kinds, *refs):
    step = pl.program_id(0)
    ins = list(refs[: sum(count for _, count in kinds)])
    outs = list(refs[len(ins) :])
    for kind, count in kinds:
        total = ins.pop(0)[0].astype(F32)
        for _ in range(count - 1):
            total = total + ins.pop(0)[0].astype(F32)
        total = total.astype(BF16)
        if kind == "sum":
            outs.pop(0)[0] = total
            continue
        low, high = outs.pop(0), outs.pop(0)

        @pl.when(step < 2)
        def _():
            low[0] = total

        @pl.when(step >= 2)
        def _():
            high[0] = total


class Places:
    def __init__(self, n):
        self.n = n
        self.planes = EXPERTS
        self.group = n // EXPERTS
        self.chips = self.group // 2
        self.bits = self.chips.bit_length() - 1
        self.me = lax.axis_index("fsdp")
        self.core = self.me % 2
        self.chip = (self.me // 2) % self.chips
        self.plane = self.me // self.group

    def swap(self):
        return [(i, i ^ 1) for i in range(self.n)]

    def cross(self, step):
        moves = []
        for i in range(self.n):
            bit = step if i % 2 == 0 else self.bits - 1 - step
            moves.append((i, i ^ (2 << bit)))
        return moves

    def turn(self, k):
        return [(i, (i + k * self.group) % self.n) for i in range(self.n)]

    def order(self, core):
        plain = list(range(self.chips))
        back = [int(format(j, "0%db" % self.bits)[::-1], 2) for j in plain]
        rel = jnp.where(core == 0, jnp.array(plain, jnp.int32), jnp.array(back, jnp.int32))
        return jnp.bitwise_xor(self.chip, rel)

    def place(self, core):
        back = [int(format(j, "0%db" % self.bits)[::-1], 2) for j in range(self.chips)]
        rel = jnp.bitwise_xor(self.chip, jnp.arange(self.chips, dtype=jnp.int32))
        return jnp.where(core == 0, rel, jnp.array(back, jnp.int32)[rel])


def send(x, moves):
    return lax.ppermute(x, "fsdp", moves)


def sync(*arrays):
    return lax.optimization_barrier(arrays)


def pair_block(expert_in, expert_out, pos):
    rin, rout = expert_in.shape[0], expert_out.shape[0]
    win = expert_in.reshape(rin, 4, CHUNK)
    halves = [
        jnp.concatenate(
            [expert_out[h * rout // 2 : (h + 1) * rout // 2], win[:, 2 * h], win[:, 2 * h + 1]]
        )
        for h in range(2)
    ]
    first = pos.core == 0
    mine = jnp.where(first, halves[0], halves[1])
    got = send(jnp.where(first, halves[1], halves[0]), pos.swap())
    a = jnp.where(first, mine, got)
    b = jnp.where(first, got, mine)
    if rin % 16 == 0:
        return jnp.concatenate([a, b])
    cut = rout // 2
    return jnp.concatenate(
        [a[:cut], b[:cut], a[cut : cut + rin], b[cut : cut + rin], a[cut + rin :], b[cut + rin :]]
    )


def fold(*items):
    kinds = tuple((item[0], len(item) - 1) for item in items)
    args, in_specs, out_specs, out_shape, finals = [], [], [], [], []
    for kind, *arrays in items:
        a = arrays[0]
        height = a.size // 4 // CHUNK
        args += [x.reshape(4, height, CHUNK) for x in arrays]
        in_specs += [pl.BlockSpec((1, height, CHUNK), lambda i: (i, 0, 0))] * len(arrays)
        if kind == "sum":
            out_specs.append(pl.BlockSpec((1, height, CHUNK), lambda i: (i, 0, 0)))
            shapes = [(4, height, CHUNK)]
            finals.append(a.shape)
        else:
            out_specs.append(
                pl.BlockSpec((1, height, CHUNK), lambda i: (jnp.minimum(i, 1), 0, 0))
            )
            out_specs.append(
                pl.BlockSpec((1, height, CHUNK), lambda i: (jnp.maximum(i - 2, 0), 0, 0))
            )
            shapes = [(2, height, CHUNK)] * 2
            finals += [(a.shape[0] // 2,) + a.shape[1:]] * 2
        out_shape += [jax.ShapeDtypeStruct(shape, BF16) for shape in shapes]
    outs = pl.pallas_call(
        functools.partial(fold_kernel, kinds),
        name="fold",
        grid=(4,),
        in_specs=in_specs,
        out_specs=tuple(out_specs),
        out_shape=tuple(out_shape),
        compiler_params=room("fold"),
        cost_estimate=pl.CostEstimate(flops=1000, bytes_accessed=1000, transcendentals=0),
    )(*args)
    return [out.reshape(shape) for out, shape in zip(outs, finals)]


def add_low(a, b):
    return (a.astype(F32) + b.astype(F32)).astype(BF16)


def local(
    tokens,
    out_grad,
    key_valid,
    expert_ids,
    gate_logits,
    attn_norm_gain,
    attn_norm_bias,
    qkv_weight,
    query_bias,
    value_bias,
    attn_out_weight,
    attn_out_bias,
    moe_norm_gain,
    moe_norm_bias,
    expert_in,
    expert_in_bias,
    expert_out,
    expert_out_bias,
):
    n = lax.axis_size("fsdp")
    pos = Places(n)
    rows = tokens.shape[0]
    ext = rows + 2 * HALO
    width = qkv_weight.shape[0]
    total_rows = rows * n
    vmem = pl.BlockSpec(memory_space=pltpu.VMEM)
    smem = pl.BlockSpec(memory_space=pltpu.SMEM)
    far = pl.BlockSpec(memory_space=pl.ANY)

    def sds(shape, kind):
        return jax.ShapeDtypeStruct(shape, kind)

    def cost(flops, moved, trans=0):
        return pl.CostEstimate(flops=int(flops / 1000), bytes_accessed=int(moved / 1000), transcendentals=trans)

    chips = pos.chips
    if chips == 4:
        keep_place = pos.place(pos.core)
        give_place = pos.place(1 - pos.core)
    else:
        keep_place = give_place = jnp.arange(4, dtype=jnp.int32)
    experts = (pos.plane - jnp.array(SEQ, jnp.int32)) % 4
    tab = jnp.concatenate(
        [
            pos.core.reshape(1),
            experts,
            pos.order(pos.core),
            pos.order(1 - pos.core),
            keep_place,
            give_place,
        ]
    ).astype(jnp.int32)
    up = [(i, i + 1) for i in range(n - 1)]
    down = [(i + 1, i) for i in range(n - 1)]

    def halo(x):
        return send(x[rows - HALO :], up), send(x[:HALO], down)

    flat = jnp.concatenate(
        [
            attn_norm_gain,
            attn_norm_bias,
            query_bias,
            value_bias,
            attn_out_bias,
            moe_norm_gain,
            moe_norm_bias,
            jnp.zeros(((SMALL - 7) * width,), BF16),
        ]
    )

    def lines_of(x):
        lines = max(1, x.shape[0] // 128)
        at = pos.me * x.shape[0] % 128
        return lax.dynamic_update_slice_in_dim(jnp.zeros((lines * 128,), BF16), x, at, 0)

    lines = jnp.concatenate([lines_of(expert_in_bias), lines_of(expert_out_bias)])
    lines = jnp.pad(lines, (0, width * SMALL - lines.shape[0])).reshape(width, SMALL)
    first = pos.core == 0
    half_0 = jnp.concatenate([qkv_weight[:, : 2 * D], flat.reshape(SMALL, width).T], axis=1)
    half_1 = jnp.concatenate([qkv_weight[:, 2 * D :], attn_out_weight, lines], axis=1)
    mine = jnp.where(first, half_0, half_1)
    got = send(jnp.where(first, half_1, half_0), pos.swap())
    block = jnp.where(first, jnp.stack([mine, got]), jnp.stack([got, mine]))
    block = block.reshape(2 * width, HALF)
    pair = pair_block(expert_in, expert_out, pos)

    front = pair[None]
    for step in range(pos.bits - 1):
        got = send(front, pos.cross(step))
        if step < pos.bits - 2:
            front = jnp.concatenate([front, got], axis=0)
    turned = [send(block, pos.turn(k)) for k in range(1, 4)]
    *turned, pair, got = sync(*turned, pair, got)
    have = jnp.stack([block] + turned)[None]
    crossed = send(have, pos.cross(0))
    poscol, posrow, gate = pl.pallas_call(
        route_kernel,
        name="route",
        out_shape=(
            sds((rows, 8), jnp.int32),
            sds((8, rows), jnp.int32),
            sds((rows, TOP), F32),
        ),
        in_specs=[vmem] * 3,
        out_specs=(vmem,) * 3,
        compiler_params=room("fold"),
        cost_estimate=cost(4 * rows * rows * 128, 1 << 20),
    )(expert_ids, expert_ids.T, gate_logits)

    def dispatch(first_k, last_k):
        count = 2 * (last_k - first_k)
        *slots, sums = pl.pallas_call(
            functools.partial(dispatch_kernel, first_k),
            name="dispatch",
            out_shape=tuple([sds((CAP, D), BF16), sds((D, CAP), BF16)] * (count // 2))
            + (sds((EXPERTS, D), F32),),
            in_specs=[smem] + [vmem] * 4,
            out_specs=(far,) * count + (vmem,),
            scratch_shapes=[pltpu.VMEM((CAP, D), BF16), pltpu.VMEM((D, CAP), BF16)] * (count // 2)
            + [pltpu.SemaphoreType.DMA((count,))],
            compiler_params=room("dispatch"),
            cost_estimate=cost(count * rows * CAP * D, 4e6),
        )(tab, out_grad, posrow, expert_ids, gate)
        return slots, sums

    before, behind = halo(tokens)
    crossed, gate, poscol, posrow, before, behind = sync(
        crossed, gate, poscol, posrow, before, behind
    )
    piece = send(pair, pos.turn(SEQ[1]))
    slots, dbout = dispatch(0, 2)
    have = jnp.concatenate([have, crossed], axis=0)
    for step in range(1, pos.bits):
        crossed = send(have, pos.cross(step))
        if step < pos.bits - 1:
            have = jnp.concatenate([have, crossed], axis=0)
    slots_2, dbout_2 = dispatch(2, 4)
    first_row = pos.me * rows
    offset = first_row % IMG
    key_rows = first_row - HALO + jnp.arange(ext, dtype=jnp.int32)
    usable = lax.dynamic_slice_in_dim(jnp.pad(key_valid, (HALO, HALO)), first_row, ext)
    present = (key_rows >= 0) & (key_rows < total_rows)
    fill = jnp.where(usable == 1, 1.0, jnp.where(present, MASKED_SCORE, FAR_SCORE))
    fill = fill.astype(F32).reshape(ext, 1)
    have, crossed, piece, fill, dbout, dbout_2, *slots = sync(
        have, crossed, piece, fill, dbout, dbout_2, *slots, *slots_2
    )
    small = [have, crossed, send(have, pos.swap()), send(crossed, pos.swap())]
    planes = (pos.plane - jnp.arange(4, dtype=jnp.int32)) % 4
    if chips == 4:
        spots = [
            (planes[None, :] * 4 + pos.order(c)[:, None]).reshape(-1)
            for c in (pos.core, 1 - pos.core)
        ]
        small = [x.reshape(8, 2 * width, HALF) for x in small]
    else:
        spots = [jnp.arange(16, dtype=jnp.int32)] * 2
        canonical = []
        for data, c in ((small[:2], pos.core), (small[2:], 1 - pos.core)):
            data = jnp.concatenate(data).reshape(4 * chips, 2 * width, HALF)
            where = (pos.place(c)[None, :] * 4 + planes[:, None]).reshape(-1)
            data = jnp.take(data, where, axis=0).reshape(16, D // 16, HALF)
            canonical += [data[:8], data[8:]]
        small = canonical

    scalars = jnp.concatenate(
        [
            jnp.stack([HALO - offset, (rows + offset + IMG - 1) // IMG, pos.core]),
            jnp.where(first, spots[0], spots[1]),
            jnp.where(first, spots[1], spots[0]),
        ]
    ).astype(jnp.int32)
    def near_chips(piece):
        held = piece[None]
        for step in range(pos.bits - 2):
            held = jnp.concatenate([held, send(held, pos.cross(step))], axis=0)
        return held, send(held, pos.cross(pos.bits - 2))

    held = [jnp.concatenate([front, got])]
    half, got = near_chips(piece)
    flight = [
        send(held[0], pos.cross(pos.bits - 1)),
        send(held[0], pos.swap()),
        got,
        send(piece, pos.turn(1)),
    ]
    qkv, o_low, y1, a2, attn_sum, wqk, wvo, vecs, bin_all, bout_all = pl.pallas_call(
        functools.partial(attn_fwd_kernel, n),
        name="attn_fwd",
        out_shape=(
            sds((NIMG, SLOT, 3 * D), BF16),
            sds((rows, D), BF16),
            sds((rows, D), F32),
            sds((rows, D), BF16),
            sds((8, D), F32),
            sds((D, HALF), BF16),
            sds((D, HALF), BF16),
            sds((8, D), F32),
            sds((16, CHUNK), F32),
            sds((EXPERTS, D), F32),
        ),
        in_specs=[smem] + [vmem] * 8,
        out_specs=(far, far, far, vmem, vmem, far, far, vmem, vmem, vmem),
        scratch_shapes=[
            pltpu.VMEM((NIMG, SLOT, 3 * D), BF16),
            pltpu.VMEM((rows, D), BF16),
            pltpu.VMEM((rows, D), F32),
            pltpu.VMEM((D, HALF), BF16),
            pltpu.VMEM((D, HALF), BF16),
            pltpu.VMEM((ext, D), F32),
            pltpu.VMEM((ext, D), F32),
            pltpu.SemaphoreType.DMA((NIMG + 2 + 2 * (rows // 256),)),
        ],
        compiler_params=room("attn_fwd"),
        cost_estimate=cost(30e9, 12e6),
    )(scalars, before, tokens, behind, fill, *small)
    full, front, got, piece, a2, vecs = sync(*flight, a2, vecs)

    rin, rout = expert_in.shape[0], expert_out.shape[0]

    def by_chip(x, core):
        if chips == 4:
            return x
        more = chips // 4
        out = x[:, :256].reshape(4, 256, more, 2 * rout).transpose(0, 2, 1, 3)
        win = x[:, 256:].reshape(4, 2, more, 2 * rin, CHUNK).transpose(0, 2, 1, 3, 4)
        both = [out.reshape(chips, rout, CHUNK), win.reshape(chips, 4 * rin, CHUNK)]
        return jnp.take(jnp.concatenate(both, axis=1), pos.order(core), axis=0)

    def run_expert(k, full, front, back):
        return pl.pallas_call(
            functools.partial(expert_kernel, k, chips),
            name="expert_%d" % k,
            out_shape=(
                sds((CAP, D), BF16),
                sds((CAP, D), BF16),
                sds((16, CHUNK), F32),
                sds((4, CHUNK, CHUNK), BF16),
                sds((4, CHUNK, CHUNK), BF16),
            ),
            in_specs=[smem] + [vmem] * 10,
            out_specs=(vmem,) * 5,
            scratch_shapes=[
                pltpu.VMEM((4, D, CHUNK), BF16),
                pltpu.VMEM((FF, D), BF16),
                pltpu.VMEM((CAP, D), BF16),
                pltpu.VMEM((D, CAP), BF16),
                pltpu.VMEM((4, CAP, CHUNK), BF16),
                pltpu.VMEM((4, CAP, CHUNK), BF16),
            ],
            compiler_params=room("expert"),
            cost_estimate=cost(10e9, 14e6),
        )(
            tab,
            a2,
            slots[2 * k],
            slots[2 * k + 1],
            posrow,
            bin_all,
            bout_all,
            held[k],
            full,
            front,
            back,
        )

    def first_sum(k, got):
        return ("halves", by_chip(results[k][3], pos.core), got)

    def give_of(k, *others):
        return send(sync(by_chip(results[k][4], 1 - pos.core), *others)[0], pos.swap())

    top = pos.bits - 1

    def send_top(x):
        return send(x, pos.cross(top))

    def send_low(keep, x):
        for step in reversed(range(1, top)):
            total = add_low(keep, send(x, pos.cross(step)))
            keep, x = total[: total.shape[0] // 2], total[total.shape[0] // 2 :]
        return keep, send(x, pos.cross(0))

    results = []
    back = send(full, pos.swap())
    held.append(jnp.concatenate([half, got]))
    half, got = near_chips(piece)
    flight = [
        send(held[1], pos.cross(top)),
        send(held[1], pos.swap()),
        got,
        send(pair, pos.turn(SEQ[3])),
    ]
    done = sync(*run_expert(0, full, front, back), *flight, a2)
    results.append(done[:5])
    full, front, got, piece, a2 = done[5:]
    back = send(full, pos.swap())

    held.append(jnp.concatenate([half, got]))
    half, got = near_chips(piece)
    flight = [send(held[2], pos.cross(top)), send(held[2], pos.swap()), got, give_of(0, back)]
    done = sync(*run_expert(1, full, front, back), *flight, a2)
    results.append(done[:5])
    full, front, got, swap_0, a2 = done[5:]
    back = send(full, pos.swap())

    held.append(jnp.concatenate([half, got]))
    flight = [send(held[3], pos.cross(top)), send(held[3], pos.swap()), give_of(1, back)]
    done = sync(*run_expert(2, full, front, back), *flight, a2)
    results.append(done[:5])
    full, front, swap_1, a2 = done[5:]
    back = send(full, pos.swap())

    keep_1, give_1 = fold(first_sum(1, swap_1))
    flight = [send_top(give_1), give_of(2, back)]
    done = sync(*run_expert(3, full, front, back), *flight, a2)
    results.append(done[:5])
    top_1, swap_2, a2 = done[5:]

    keep_1, give_1, keep_2, give_2 = fold(("halves", keep_1, top_1), first_sum(2, swap_2))
    keep_1, got = send_low(keep_1, give_1)
    flight = [got, send_top(give_2), give_of(3)]
    routing = (tab, poscol, expert_ids, gate, out_grad)
    middle = pl.pallas_call(
        middle_kernel,
        name="middle",
        out_shape=(
            sds((rows, D), BF16),
            sds((rows, D), F32),
            sds((rows, D), BF16),
            sds((D, D), BF16),
            sds((rows, TOP), F32),
            sds((8, D), F32),
            sds((8, D), F32),
        ),
        in_specs=[smem] + [vmem] * 17,
        out_specs=(vmem,) * 7,
        scratch_shapes=[pltpu.VMEM((rows, D), F32), pltpu.VMEM((rows, D), F32)],
        compiler_params=room("middle"),
        cost_estimate=cost(9 * 2 * rows * CAP * D, 16e6),
    )(
        *routing,
        *(r[0] for r in results),
        *(r[1] for r in results),
        y1,
        o_low,
        fill,
        vecs,
        attn_sum,
    )
    done = sync(*middle, *flight)
    block_out, dy1, gattn, dwo, logits_grad, sums2, stats, low_1, top_2, swap_3 = done

    sum_1, keep_2, give_2, keep_3, give_3 = fold(
        ("sum", keep_1, low_1), ("halves", keep_2, top_2), first_sum(3, swap_3)
    )
    keep_2, got = send_low(keep_2, give_2)

    def home(k, x):
        return send(x, pos.turn(4 - SEQ[k]))

    flight = [got, send_top(give_3), home(1, sum_1[0]), *halo(gattn)]
    early = pl.pallas_call(
        attn_bwd_kernel,
        name="attn_bwd_early",
        out_shape=sds((4, SLOT, 3 * D), BF16),
        in_specs=[smem] + [vmem] * 4,
        out_specs=vmem,
        scratch_shapes=[pltpu.VMEM((ext, D), F32)],
        compiler_params=room("early"),
        cost_estimate=cost(30e9, 8e6),
    )(scalars, fill, qkv, gattn, wvo)
    early, low_2, top_3, home_1, before, behind = sync(early, *flight)

    sum_2, keep_3, give_3, keep_0, give_0 = fold(
        ("sum", keep_2, low_2), ("halves", keep_3, top_3), first_sum(0, swap_0)
    )
    keep_3, got = send_low(keep_3, give_3)
    flight = [got, send(sum_2, pos.turn(1)), send_top(give_0)]
    tokens_grad, rest_keep, rest_give = pl.pallas_call(
        functools.partial(attn_end_kernel, n, 5 + 2 * chips),
        name="attn_bwd_late",
        out_shape=(
            sds((rows, D), F32),
            sds((EXPERTS, 4, D // 16, HALF), BF16),
            sds((EXPERTS, 4, D // 16, HALF), BF16),
        ),
        in_specs=[smem] * 2 + [vmem] * 20,
        out_specs=(vmem,) * 3,
        scratch_shapes=[
            pltpu.VMEM((ext, D), F32),
            pltpu.VMEM((ext, 3 * D), F32),
            pltpu.VMEM((rows, D), BF16),
            pltpu.VMEM((rows, 3 * D), BF16),
            pltpu.VMEM((128, D), F32),
            pltpu.VMEM((D, SMALL), F32),
        ],
        compiler_params=room("late"),
        cost_estimate=cost(30e9, 16e6),
    )(
        scalars,
        tab,
        tokens,
        fill,
        qkv,
        before,
        gattn,
        behind,
        dy1,
        wqk,
        wvo,
        vecs,
        early,
        dwo,
        sums2,
        stats,
        *(r[2] for r in results),
        dbout,
        dbout_2,
    )

    tokens_grad, rest_keep, rest_give, low_3, from_2, top_0 = sync(
        tokens_grad, rest_keep, rest_give, *flight
    )

    def by_block(x, core):
        if chips == 4:
            return x
        return jnp.take(x.reshape(EXPERTS, chips, 2 * width, HALF), pos.order(core), axis=1)

    sum_3, keep_0, give_0 = fold(
        ("sum", keep_3, low_3, from_2), ("halves", keep_0, top_0)
    )
    home_3 = home(3, sum_3[0])
    rest = add_low(
        by_block(rest_keep, pos.core), send(by_block(rest_give, 1 - pos.core), pos.swap())
    )

    def cross(x, step, *others):
        x = x.reshape((EXPERTS, 2, -1) + x.shape[2:])
        swapped, *others = sync(send(x[:, 1], pos.cross(step)), *others)
        return [add_low(x[:, 0], swapped)] + others

    (rest,) = cross(rest, top)
    for step in reversed(range(1, top)):
        (rest,) = cross(rest, step)
    rest, home_3, give_0 = cross(rest, 0, home_3, give_0)
    keep_0, got = send_low(keep_0, give_0)
    rest = rest[:, 0]

    def block_for(k):
        return lax.dynamic_index_in_dim(rest, (pos.plane + k) % 4, 0, keepdims=False)

    others = [send(block_for(k), pos.turn(k)) for k in range(1, 4)]
    *others, got = sync(*others, got)
    total = keep_0[0].astype(F32) + got[0].astype(F32)
    for got in (home_1, home_3):
        total = total + got.astype(F32)

    def own_halves(pair, axis):
        mine = lax.dynamic_index_in_dim(pair, pos.core, 0, keepdims=False)
        got = send(lax.dynamic_index_in_dim(pair, 1 - pos.core, 0, keepdims=False), pos.swap())
        return jnp.where(
            pos.core == 0,
            jnp.concatenate([mine, got], axis=axis),
            jnp.concatenate([got, mine], axis=axis),
        )

    out_sum = total[:rout].reshape(256, 2, rout).transpose(1, 0, 2)
    expert_out_grad = own_halves(out_sum, 0).T
    in_sum = total[rout:].reshape(2, 2, rin, CHUNK).transpose(1, 2, 0, 3)
    expert_in_grad = own_halves(in_sum.reshape(2, rin, 2 * CHUNK), 1)

    *others, expert_out_grad, expert_in_grad = sync(*others, expert_out_grad, expert_in_grad)
    rest = block_for(0).astype(F32)
    for got in others:
        rest = rest + got.astype(F32)

    rest = own_halves(rest.reshape(2, width, HALF), 1)
    tail = rest[:, 2 * D : HALF]
    bias = rest[:, HALF + 2 * D :].reshape(-1)
    count = jnp.sum((key_valid == 1).astype(F32))
    block_stats = jnp.sqrt(tail[0, 8:11] / (count * D))
    in_size, out_size = expert_in_bias.shape[0], expert_out_bias.shape[0]
    lines = max(1, in_size // 128)

    def bias_part(line, size):
        return lax.dynamic_slice_in_dim(bias, line * 128 + pos.me * size % 128, size)

    return (
        block_out,
        tokens_grad,
        logits_grad,
        tail[:, 0],
        tail[:, 1],
        jnp.concatenate([rest[:, : 2 * D], rest[:, HALF : HALF + D]], axis=1),
        tail[:, 2],
        tail[:, 3],
        rest[:, HALF + D : HALF + 2 * D],
        tail[:, 4],
        tail[:, 5],
        tail[:, 6],
        expert_in_grad,
        bias_part(0, in_size),
        expert_out_grad,
        bias_part(lines, out_size),
        block_stats,
    )


def solution(mesh):
    row = P("fsdp", None)
    vec = P("fsdp")
    return jax.shard_map(
        local,
        mesh=mesh,
        in_specs=(
            row,
            row,
            P(),
            row,
            row,
            vec,
            vec,
            row,
            vec,
            vec,
            row,
            vec,
            vec,
            vec,
            row,
            vec,
            row,
            vec,
        ),
        out_specs=(
            row,
            row,
            row,
            vec,
            vec,
            row,
            vec,
            vec,
            row,
            vec,
            vec,
            vec,
            row,
            vec,
            row,
            vec,
            P(),
        ),
        check_vma=False,
    )
```
